32 devices in a mesh: batch: 2 (over x), head: 4 (over y, core), wide: 4 (over z).
Axes of the slice: x: 2, y: 2, z: 4, core: 2. Of those that a mesh axis runs over, the one named last changes fastest.
Arguments:
- tokens: bfloat16 [4, 1024, 768], P('batch', 'wide'), may hold values from -6 to 6
- patches: int32 [4, 4], P('batch'), may hold values from 0 to 1024, as said below
- w_qkv: bfloat16 [2, 3, 768, 768], P(None, None, 'head'), may hold values from -0.21875 to 0.21875
- w_att: bfloat16 [2, 768, 768], P(None, 'head'), may hold values from -0.875 to 0.875
- w_in: bfloat16 [2, 3072, 768], P(None, 'wide'), may hold values from -0.21875 to 0.21875
- w_mlp: bfloat16 [2, 3072, 768], P(None, 'wide'), may hold values from -0.21875 to 0.21875
- gains: float32 [2, 768], replicated, may hold values from 0.1 to 1.9
- cotangent: bfloat16 [4, 1024, 768], P('batch', 'wide'), may hold values from -6 to 6
Outputs:
- out: float32 [4, 1024, 768], P('batch', 'wide')
- d_tokens: float32 [4, 1024, 768], P('batch', 'wide')
- d_qkv: float32 [2, 3, 768, 768], P(None, None, 'head')
- d_att: float32 [2, 768, 768], P(None, 'head')
- d_in: float32 [2, 3072, 768], P(None, 'wide')
- d_mlp: float32 [2, 3072, 768], P(None, 'wide')
- d_gains: float32 [2, 768], replicated
The draws below stay inside these ranges and needn't reach their ends.
Inputs may be any that keep to these rules, and one draw needn't show every extreme that they name: Each row packs images of 1024, 576 or 196 patches from its first slot on, entries of absent images are 0 and stand last, and the counts of a row sum to at most 1024; among the rows of each index of batch one holds a single image of 1024 patches.
All inputs are finite; a program needn't handle non-finite values.
Results may differ from the reference program's by a relative error of at most 0.023.
Values may be sent and summed in bfloat16 or wider, within the bound.
No kernel may reach another device: no remote copies, remote signals or barrier semaphores. Data moves between devices by JAX's collectives and lax.ppermute only.
A program may use at most 256 MiB of HBM per device.

```python
import jax
import jax.numpy as jnp
from jax import lax

D = 768
HEAD_DIM = 64
FF = 3072
LAYERS = 2
ROW = 1024
ROWS_HALF = 2
ROWS = 4


def draw_patches(key, part):
    key = jax.random.fold_in(key, 11)
    full_image = ROW
    mid_image = ROW * 9 // 16
    small_image = ROW * 49 // 256
    patterns = jnp.array([[full_image, 0, 0, 0], [mid_image, small_image, small_image, 0], [mid_image, small_image, 0, 0], [small_image, small_image, small_image, small_image], [mid_image, 0, 0, 0]], dtype=jnp.int32)
    choose_key, force_key = jax.random.split(key)
    halves = ROWS // ROWS_HALF
    picks = jax.random.randint(choose_key, (ROWS,), 0, 5)
    forced = jax.random.randint(force_key, (halves,), 0, ROWS_HALF) + jnp.arange(halves, dtype=jnp.int32) * ROWS_HALF
    picks = picks.at[forced].set(0)
    return patterns[picks]


def steps_of(key, shape, cuts, least, top_value):
    level, own = 1.0, jax.random.fold_in(key, 6)
    for position, shards_of in cuts:
        draws = jnp.exp(jax.random.uniform(jax.random.fold_in(own, position), (shards_of,), jnp.float32, least / len(cuts), top_value / len(cuts)))
        level = level * jnp.repeat(draws, shape[position] // shards_of).reshape([-1 if axis == position else 1 for axis in range(len(shape))])
    return level


def noise(own_key, extent, width, reach, cuts=(), kind=jnp.bfloat16):
    level = steps_of(own_key, extent, cuts, -0.22, 0.18) if cuts else 1.0
    values = jax.random.normal(own_key, extent, jnp.float32) * width * level
    return jnp.minimum(jnp.maximum(values, -reach), reach).astype(kind)


def setup_inputs(seed: int = 0) -> dict:
    key_of = jax.random.split(jax.random.key(seed), 9)
    return {
        "tokens": noise(key_of[0], (ROWS, ROW, D), 1.0, 6.0, ((0, 2), (1, 4))),
        "patches": draw_patches(jax.random.fold_in(key_of[8], 71), 0),
        "w_qkv": noise(key_of[2], (LAYERS, 3, D, D), D ** -0.5, 0.21875, ((2, 4),)),
        "w_att": noise(key_of[3], (LAYERS, D, D), (D // 16) ** -0.5, 0.875, ((1, 4),)),
        "w_in": noise(key_of[4], (LAYERS, FF, D), D ** -0.5, 0.21875, ((1, 4),)),
        "w_mlp": noise(key_of[5], (LAYERS, FF, D), (FF // 4) ** -0.5, 0.21875, ((1, 4),)),
        "gains": jnp.clip(1.0 + 0.18 * jax.random.normal(key_of[6], (LAYERS, D), jnp.float32), 0.1, 1.9),
        "cotangent": noise(key_of[7], (ROWS, ROW, D), 1.0, 6.0, ((0, 2), (1, 4))),
    }


@jax.custom_vjp
def low(v):
    return lax.optimization_barrier(v.astype(jnp.bfloat16)).astype(jnp.float32)

@jax.custom_vjp
def low_back(v):
    return v

def low_keep(v):
    return (low(v), None)

def low_pass(kept, grad):
    return (grad,)

def back_keep(v):
    return (v, None)

def back_low(kept, grad):
    return (low(grad),)
low.defvjp(low_keep, low_pass)
low_back.defvjp(back_keep, back_low)
HIGH = lax.Precision.HIGHEST
EPS = 1e-06
NEGATIVE = -1e+30

def layer_norm(stream, gain_row):
    centre = lax.optimization_barrier(jnp.mean(stream, axis=-1, keepdims=True))
    centred = stream - centre
    spread = lax.optimization_barrier(jnp.mean(centred * centred, axis=-1, keepdims=True))
    return centred * lax.rsqrt(spread + EPS) * gain_row

def image_slots(patches, row_length):
    image_ends = jnp.cumsum(patches, axis=1).astype(jnp.int32)
    slot_index = jnp.arange(row_length, dtype=jnp.int32)
    image_of = lax.optimization_barrier(jnp.sum((slot_index[None, :, None] >= image_ends[:, None, :]).astype(jnp.int32), axis=2))
    live_slot = slot_index[None, :] < image_ends[:, -1:]
    return (image_of, live_slot)

def attend_row(inputs):
    queries, key_heads, values, image_of, live_slot = inputs
    scores = low_back(jnp.einsum('qhd,khd->hqk', queries, key_heads, precision=HIGH) * HEAD_DIM ** (-0.5))
    allowed = (image_of[:, None] == image_of[None, :]) & live_slot[:, None] & live_slot[None, :]
    row_top = lax.optimization_barrier(jnp.max(jnp.where(allowed, scores, NEGATIVE), axis=-1, keepdims=True))
    exp_terms = jnp.where(allowed, jnp.exp(jnp.where(allowed, scores - row_top, 0.0)), 0.0)
    row_total = jnp.maximum(lax.optimization_barrier(jnp.sum(exp_terms, axis=-1, keepdims=True)), 1.0)
    probs = low(exp_terms / row_total)
    return jnp.einsum('hqk,khd->qhd', probs, values, precision=HIGH)

def layer(stream, gain_row, qkv_weight, att_weight, in_weight, mlp_weight, image_of, live_slot):
    row_count, row_length, model_width = stream.shape
    act = low(layer_norm(stream, gain_row))
    proj = low(low_back(jnp.einsum('rsd,tcd->rstc', act, qkv_weight, precision=HIGH)))
    head_count = qkv_weight.shape[1] // HEAD_DIM
    split = proj.reshape(row_count, row_length, 3, head_count, HEAD_DIM)
    attended = lax.map(jax.checkpoint(attend_row), (split[:, :, 0], split[:, :, 1], split[:, :, 2], image_of, live_slot))
    attended = low(low_back(attended.reshape(row_count, row_length, model_width)))
    branch = jnp.einsum('rsc,cd->rsd', attended, att_weight, precision=HIGH)
    pre_act = low_back(jnp.einsum('rsd,fd->rsf', act, in_weight, precision=HIGH))
    hidden = low(jax.nn.gelu(pre_act))
    branch = branch + jnp.einsum('rsf,fd->rsd', hidden, mlp_weight, precision=HIGH)
    return stream + low_back(branch)

def reference(tokens, patches, w_qkv, w_att, w_in, w_mlp, gains, cotangent):
    image_of, live_slot = image_slots(patches, tokens.shape[1])

    def forward(stream, qkv_all, att_all, in_all, mlp_all, gain_all):
        for depth_level in range(qkv_all.shape[0]):
            stream = layer(stream, gain_all[depth_level], qkv_all[depth_level], att_all[depth_level], in_all[depth_level], mlp_all[depth_level], image_of, live_slot)
        return stream
    primals = (tokens.astype(jnp.float32), w_qkv.astype(jnp.float32), w_att.astype(jnp.float32), w_in.astype(jnp.float32), w_mlp.astype(jnp.float32), gains.astype(jnp.float32))
    result, pull_back = jax.vjp(forward, *primals)
    grads = pull_back(cotangent.astype(jnp.float32))
    return (result, grads[0], grads[1], grads[2], grads[3], grads[4], grads[5])
```

```python
import jax
import jax.numpy as jnp
from jax import lax
from jax.sharding import PartitionSpec as P

HEAD_DIM = 64
EPS = 1e-06
NEGATIVE = -1e30
BF = jnp.bfloat16
F32 = jnp.float32
DIRECT = 8


def norm_parts(stream):
    centre = jnp.mean(stream, axis=-1, keepdims=True)
    centred = stream - centre
    spread = jnp.mean(centred * centred, axis=-1, keepdims=True)
    rstd = lax.rsqrt(spread + EPS)
    return centred * rstd, rstd


def norm_back(d_act, xhat, rstd, gain_row):
    dxh = d_act * gain_row
    m1 = jnp.mean(dxh, axis=-1, keepdims=True)
    m2 = jnp.mean(dxh * xhat, axis=-1, keepdims=True)
    return (dxh - m1 - xhat * m2) * rstd


def trans_dot(left, right):
    return lax.dot_general(left, right, (((0,), (0,)), ((), ())), preferred_element_type=F32)


def right_dot(left, right):
    return lax.dot_general(left, right, (((1,), (1,)), ((), ())), preferred_element_type=F32)


def plain_dot(left, right):
    return jnp.dot(left, right, preferred_element_type=F32)


def swap(x, bit):
    size = lax.axis_size("head")
    return lax.ppermute(x, "head", [(i, i ^ bit) for i in range(size)])


def shift(x, step):
    size = lax.axis_size("wide")
    return lax.ppermute(x, "wide", [(i, (i + step) % size) for i in range(size)])


def gather_wide(x):
    size = lax.axis_size("wide")
    if size <= DIRECT:
        return jnp.concatenate([x] + [shift(x, s) for s in range(1, size)], axis=0)
    whole = lax.all_gather(x, "wide", axis=0, tiled=False)
    order = (lax.axis_index("wide") - jnp.arange(size)) % size
    return whole[order].reshape(size * x.shape[0], *x.shape[1:])


def scatter_wide(parts):
    size = lax.axis_size("wide")
    rows = parts.shape[0] // size
    if size <= DIRECT:
        total = parts[:rows]
        low = [shift(parts[s * rows : (s + 1) * rows].astype(BF), -s) for s in range(1, size)]
        for piece in low:
            total = total + piece.astype(F32)
        return total
    order = (lax.axis_index("wide") - jnp.arange(size)) % size
    blocks = parts.astype(BF).reshape(size, rows, -1)[order]
    return lax.psum_scatter(blocks, "wide", scatter_dimension=0, tiled=False).astype(F32)


def gather_head(x):
    place = lax.axis_index("head")
    a = x
    b = swap(x, 2)
    c = swap(a, 1)
    d = swap(b, 1)
    low_bit = (place & 1) == 1
    high_bit = (place & 2) == 2
    a, c = jnp.where(low_bit, c, a), jnp.where(low_bit, a, c)
    b, d = jnp.where(low_bit, d, b), jnp.where(low_bit, b, d)
    a, b = jnp.where(high_bit, b, a), jnp.where(high_bit, a, b)
    c, d = jnp.where(high_bit, d, c), jnp.where(high_bit, c, d)
    return jnp.stack([a, c, b, d])


def local(tokens, patches, w_qkv, w_att, w_in, w_mlp, gains, cotangent):
    rows_all, slots, width = tokens.shape
    wide = lax.axis_size("wide")
    place = lax.axis_index("head")
    wide_place = lax.axis_index("wide")
    levels = w_qkv.shape[0]
    group = w_att.shape[1]
    heads = 2 * group // HEAD_DIM
    n = rows_all * slots // 4
    rows = rows_all // 2
    scale = HEAD_DIM ** (-0.5)

    def assemble(own, other, count):
        if rows == 1:
            return jnp.concatenate([own, other], axis=0)[None]
        half = rows // 2
        def turn(v):
            v = v.reshape(count, half, slots, *v.shape[1:])
            return jnp.moveaxis(v, 1, 0).reshape(half, count * slots, *v.shape[3:])
        return jnp.concatenate([turn(own), turn(other)], axis=0)

    def take_apart(v, count):
        if rows == 1:
            return v[0, : count * n], v[0, count * n :]
        half = rows // 2
        def turn(u):
            u = u.reshape(half, count, slots, *u.shape[2:])
            return jnp.moveaxis(u, 1, 0).reshape(count * n, *u.shape[3:])
        return turn(v[:half]), turn(v[half:])

    ends = jnp.cumsum(patches, axis=1)
    slot_index = jnp.arange(slots * wide, dtype=jnp.int32)
    image = jnp.sum((slot_index[None, :, None] >= ends[:, None, :]).astype(jnp.int32), axis=2)
    image = jnp.where(slot_index[None, :] < ends[:, -1:], image, -1)
    image = image.reshape(rows_all, wide, slots).transpose(1, 0, 2).reshape(wide, 4, n)
    order = (wide_place - jnp.arange(wide)) % wide
    image = image[order]
    own_image = lax.dynamic_index_in_dim(image, place, 1, keepdims=False)
    other_image = lax.dynamic_index_in_dim(image, place ^ 1, 1, keepdims=False)
    key_image = assemble(own_image.reshape(-1), other_image.reshape(-1), wide)
    query_image = assemble(own_image[0], other_image[0], 1)
    allowed = (query_image[:, :, None] == key_image[:, None, :]) & (key_image >= 0)[:, None, :]
    allowed = allowed[:, None]

    def split(v):
        return v.reshape(*v.shape[:-1], -1, HEAD_DIM)

    own = lax.dynamic_index_in_dim(tokens.reshape(4, n, width), place, 0, keepdims=False)
    cot = lax.dynamic_index_in_dim(cotangent.reshape(4, n, width), place, 0, keepdims=False)
    stream = own.astype(F32)
    saved = []
    for l in range(levels):
        gain_row = gains[l]
        xhat, rstd = norm_parts(stream)
        act = (xhat * gain_row).astype(BF)
        ff_act = gather_wide(act)
        other_act = swap(ff_act, 1)
        qkv_w = jnp.concatenate([w_qkv[l], swap(w_qkv[l], 2)], axis=1)
        att_w = jnp.concatenate([w_att[l], swap(w_att[l], 2)], axis=0)
        pre = right_dot(ff_act, w_in[l])
        hidden = jax.nn.gelu(pre).astype(BF)
        branch = scatter_wide(plain_dot(hidden, w_mlp[l]))
        key_act = assemble(ff_act, other_act, wide)
        query_act = assemble(act, other_act[:n], 1)
        q = jnp.einsum("rse,ce->rsc", query_act, qkv_w[0], preferred_element_type=F32).astype(BF)
        kv = jnp.einsum(
            "rse,ce->rsc", key_act, qkv_w[1:].reshape(4 * group, width), preferred_element_type=F32
        ).astype(BF)
        q, k, v = split(q), split(kv[..., : 2 * group]), split(kv[..., 2 * group :])
        scores = jnp.einsum("rqhd,rkhd->rhqk", q, k, preferred_element_type=F32) * scale
        top = jnp.max(jnp.where(allowed, scores, NEGATIVE), axis=-1, keepdims=True)
        expo = jnp.where(allowed, jnp.exp(jnp.where(allowed, scores - top, 0.0)), 0.0)
        probs = expo / jnp.maximum(jnp.sum(expo, axis=-1, keepdims=True), 1.0)
        probs_low = probs.astype(BF)
        attended = jnp.einsum("rhqk,rkhd->rqhd", probs_low, v, preferred_element_type=F32)
        attended = attended.reshape(rows, -1, 2 * group).astype(BF)
        att_own, att_other = take_apart(
            jnp.einsum("rqc,ce->rqe", attended, att_w, preferred_element_type=F32), 1
        )
        branch = branch + att_own + swap(att_other.astype(BF), 1).astype(F32)
        saved.append(
            (xhat, rstd, ff_act, key_act, query_act, qkv_w, att_w, pre, hidden, q, k, v, probs, attended)
        )
        stream = stream + branch
    delta = gather_head((stream - own.astype(F32)).astype(BF))
    out = tokens.astype(F32) + delta.reshape(tokens.shape).astype(F32)

    grad = cot.astype(F32)
    qkv_grads, att_grads, in_grads, mlp_grads, gain_grads = [], [], [], [], []
    for l in reversed(range(levels)):
        xhat, rstd, ff_act, key_act, query_act, qkv_w, att_w, pre, hidden, q, k, v, probs, attended = saved[l]
        gain_row = gains[l]
        low = grad.astype(BF)
        ff_grad = gather_wide(low)
        query_grad = assemble(low, swap(low, 1), 1)
        d_att = jnp.einsum("rqc,rqe->ce", attended, query_grad, preferred_element_type=F32)
        d_attended = split(
            jnp.einsum("rqe,ce->rqc", query_grad, att_w, preferred_element_type=F32).astype(BF)
        )
        probs_low = probs.astype(BF)
        d_probs = jnp.einsum("rqhd,rkhd->rhqk", d_attended, v, preferred_element_type=F32)
        d_scores = (probs * (d_probs - jnp.sum(probs * d_probs, axis=-1, keepdims=True))).astype(BF)
        dq = jnp.einsum("rhqk,rkhd->rqhd", d_scores, k, preferred_element_type=F32) * scale
        dk = jnp.einsum("rhqk,rqhd->rkhd", d_scores, q, preferred_element_type=F32) * scale
        dv = jnp.einsum("rhqk,rqhd->rkhd", probs_low, d_attended, preferred_element_type=F32)
        dq = dq.astype(BF).reshape(rows, -1, 2 * group)
        dkv = jnp.concatenate([dk, dv], axis=2).astype(BF).reshape(rows, -1, 4 * group)
        d_q_w = jnp.einsum("rqc,rqe->ce", dq, query_act, preferred_element_type=F32)
        d_kv_w = jnp.einsum("rqc,rqe->ce", dkv, key_act, preferred_element_type=F32)
        d_qkv = jnp.concatenate([d_q_w, d_kv_w]).reshape(3, 2, group, width)
        d_att = d_att.reshape(1, 2, group, width)
        d_attn = jnp.concatenate([d_qkv, d_att], axis=0)
        d_attn = d_attn[:, 0] + swap(d_attn[:, 1].astype(BF), 2).astype(F32)
        d_act_kv = jnp.einsum(
            "rkc,ce->rke", dkv, qkv_w[1:].reshape(4 * group, width), preferred_element_type=F32
        )
        d_act_q = jnp.einsum("rqc,ce->rqe", dq, qkv_w[0], preferred_element_type=F32)
        kv_own, kv_other = take_apart(d_act_kv, wide)
        q_own, q_other = take_apart(d_act_q, 1)
        kv_other = kv_other.at[:n].add(q_other)
        from_other = swap(kv_other.astype(BF), 1).astype(F32)
        d_hidden = right_dot(ff_grad, w_mlp[l])
        unused, pull = jax.vjp(jax.nn.gelu, pre)
        d_pre = pull(d_hidden)[0].astype(BF)
        d_mlp = trans_dot(hidden, ff_grad)
        d_in = trans_dot(d_pre, ff_act)
        parts = plain_dot(d_pre, w_in[l]) + kv_own + from_other
        parts = parts.at[:n].add(q_own)
        d_act = scatter_wide(parts)
        gain_grads.insert(0, jnp.sum(d_act * xhat, axis=0))
        grad = grad + norm_back(d_act, xhat, rstd, gain_row)
        d_attn = lax.psum(d_attn.astype(BF), ("batch", "wide")).astype(F32)
        d_in, d_mlp = lax.psum((d_in.astype(BF), d_mlp.astype(BF)), ("batch", "head"))
        qkv_grads.insert(0, d_attn[:3])
        att_grads.insert(0, d_attn[3])
        in_grads.insert(0, d_in.astype(F32))
        mlp_grads.insert(0, d_mlp.astype(F32))
    d_gains = lax.psum(jnp.stack(gain_grads), ("batch", "head", "wide"))
    delta = gather_head((grad - cot.astype(F32)).astype(BF))
    d_tokens = cotangent.astype(F32) + delta.reshape(tokens.shape).astype(F32)
    return (
        out,
        d_tokens,
        jnp.stack(qkv_grads),
        jnp.stack(att_grads),
        jnp.stack(in_grads),
        jnp.stack(mlp_grads),
        d_gains,
    )


def solution(mesh):
    return jax.shard_map(
        local,
        mesh=mesh,
        in_specs=(
            P("batch", "wide", None),
            P("batch", None),
            P(None, None, "head", None),
            P(None, "head", None),
            P(None, "wide", None),
            P(None, "wide", None),
            P(),
            P("batch", "wide", None),
        ),
        out_specs=(
            P("batch", "wide", None),
            P("batch", "wide", None),
            P(None, None, "head", None),
            P(None, "head", None),
            P(None, "wide", None),
            P(None, "wide", None),
            P(),
        ),
        check_vma=False,
    )
```

```python
import functools

import jax
import jax.numpy as jnp
from jax import lax
from jax.experimental import pallas as pl
from jax.experimental.pallas import tpu as pltpu
from jax.sharding import PartitionSpec as P

HEAD_DIM = 64
EPS = 1e-06
NEGATIVE = -1e30
BF = jnp.bfloat16
F32 = jnp.float32
DIRECT = 8


def norm_parts(stream):
    centre = jnp.mean(stream, axis=-1, keepdims=True)
    centred = stream - centre
    spread = jnp.mean(centred * centred, axis=-1, keepdims=True)
    rstd = lax.rsqrt(spread + EPS)
    return centred * rstd, rstd


def norm_back(d_act, xhat, rstd, gain_row):
    dxh = d_act * gain_row
    m1 = jnp.mean(dxh, axis=-1, keepdims=True)
    m2 = jnp.mean(dxh * xhat, axis=-1, keepdims=True)
    return (dxh - m1 - xhat * m2) * rstd


def trans_dot(left, right):
    return lax.dot_general(left, right, (((0,), (0,)), ((), ())), preferred_element_type=F32)


def right_dot(left, right):
    return lax.dot_general(left, right, (((1,), (1,)), ((), ())), preferred_element_type=F32)


def plain_dot(left, right):
    return jnp.dot(left, right, preferred_element_type=F32)


def swap(x, bit):
    size = lax.axis_size("head")
    return lax.ppermute(x, "head", [(i, i ^ bit) for i in range(size)])


def shift(x, step):
    size = lax.axis_size("wide")
    return lax.ppermute(x, "wide", [(i, (i + step) % size) for i in range(size)])


def gather_wide(x):
    size = lax.axis_size("wide")
    if size <= DIRECT:
        return jnp.concatenate([x] + [shift(x, s) for s in range(1, size)], axis=0)
    whole = lax.all_gather(x, "wide", axis=0, tiled=False)
    order = (lax.axis_index("wide") - jnp.arange(size)) % size
    return whole[order].reshape(size * x.shape[0], *x.shape[1:])


def scatter_wide(parts):
    size = lax.axis_size("wide")
    rows = parts.shape[0] // size
    if size <= DIRECT:
        total = parts[:rows]
        low = [shift(parts[s * rows : (s + 1) * rows].astype(BF), -s) for s in range(1, size)]
        for piece in low:
            total = total + piece.astype(F32)
        return total
    order = (lax.axis_index("wide") - jnp.arange(size)) % size
    blocks = parts.astype(BF).reshape(size, rows, -1)[order]
    return lax.psum_scatter(blocks, "wide", scatter_dimension=0, tiled=False).astype(F32)


def gather_head(x):
    place = lax.axis_index("head")
    a = x
    b = swap(x, 2)
    c = swap(a, 1)
    d = swap(b, 1)
    low_bit = (place & 1) == 1
    high_bit = (place & 2) == 2
    a, c = jnp.where(low_bit, c, a), jnp.where(low_bit, a, c)
    b, d = jnp.where(low_bit, d, b), jnp.where(low_bit, b, d)
    a, b = jnp.where(high_bit, b, a), jnp.where(high_bit, a, b)
    c, d = jnp.where(high_bit, d, c), jnp.where(high_bit, c, d)
    return jnp.stack([a, c, b, d])


PAIR = 2 * HEAD_DIM
FLOOR = -1e29


def head_softmax(q, k, allowed):
    s = jnp.where(allowed, right_dot(q, k), NEGATIVE)
    top = jnp.maximum(jnp.max(s, axis=-1, keepdims=True), FLOOR)
    expo = jnp.exp(s - top)
    inverse = 1.0 / jnp.maximum(jnp.sum(expo, axis=-1, keepdims=True), 1.0)
    return expo * inverse, top, inverse


def attend_kernel(q_ref, k_ref, v_ref, qid_ref, kid_ref, o_ref, stat_ref):
    allowed = qid_ref[0] == kid_ref[0]
    q = q_ref[0] * jnp.asarray(HEAD_DIM ** (-0.5), BF)
    k, v = k_ref[0], v_ref[0]
    lane = lax.broadcasted_iota(jnp.int32, (q.shape[0], PAIR), 1)
    stats = jnp.zeros((q.shape[0], PAIR), F32)
    outs = []
    for j in range(2):
        cut = slice(j * HEAD_DIM, (j + 1) * HEAD_DIM)
        probs, top, inverse = head_softmax(q[:, cut], k[:, cut], allowed)
        outs.append(plain_dot(probs.astype(BF), v[:, cut]))
        stats = jnp.where(lane == 2 * j, top, jnp.where(lane == 2 * j + 1, inverse, stats))
    o_ref[0] = jnp.concatenate(outs, axis=1).astype(BF)
    stat_ref[0, 0] = stats


def attend_back_kernel(saved, q_ref, k_ref, v_ref, g_ref, qid_ref, kid_ref, *refs):
    if saved:
        stat_ref, dq_ref, dk_ref, dv_ref = refs
    else:
        o_ref, dq_ref, dk_ref, dv_ref = refs
    allowed = qid_ref[0] == kid_ref[0]
    scale = HEAD_DIM ** (-0.5)
    q = q_ref[0] * jnp.asarray(scale, BF)
    k, v, g = k_ref[0], v_ref[0], g_ref[0]
    outs, dqs, dks, dvs = [], [], [], []
    for j in range(2):
        cut = slice(j * HEAD_DIM, (j + 1) * HEAD_DIM)
        qj, kj, vj, gj = q[:, cut], k[:, cut], v[:, cut], g[:, cut]
        if saved:
            top = stat_ref[0, 0, :, 2 * j : 2 * j + 1]
            inverse = stat_ref[0, 0, :, 2 * j + 1 : 2 * j + 2]
            probs = jnp.exp(jnp.where(allowed, right_dot(qj, kj), NEGATIVE) - top) * inverse
        else:
            probs, top, inverse = head_softmax(qj, kj, allowed)
        low = probs.astype(BF)
        if not saved:
            outs.append(plain_dot(low, vj))
        dp = right_dot(gj, vj)
        ds = (probs * (dp - jnp.sum(probs * dp, axis=-1, keepdims=True))).astype(BF)
        dqs.append(plain_dot(ds, kj) * scale)
        dks.append(trans_dot(ds, qj))
        dvs.append(trans_dot(low, gj))
    if not saved:
        o_ref[0] = jnp.concatenate(outs, axis=1).astype(BF)
    dq_ref[0] = jnp.concatenate(dqs, axis=1).astype(BF)
    dk_ref[0] = jnp.concatenate(dks, axis=1).astype(BF)
    dv_ref[0] = jnp.concatenate(dvs, axis=1).astype(BF)


def attend_specs(q, k):
    rows, tq, width = q.shape
    tk = k.shape[1]
    q_spec = pl.BlockSpec((1, tq, PAIR), lambda r, j: (r, 0, j))
    k_spec = pl.BlockSpec((1, tk, PAIR), lambda r, j: (r, 0, j))
    qid_spec = pl.BlockSpec((1, tq, 1), lambda r, j: (r, 0, 0))
    kid_spec = pl.BlockSpec((1, 1, tk), lambda r, j: (r, 0, 0))
    stat_spec = pl.BlockSpec((1, 1, tq, PAIR), lambda r, j: (r, j, 0, 0))
    work = rows * tq * tk * width
    return (rows, width // PAIR), q_spec, k_spec, qid_spec, kid_spec, stat_spec, work


def attend(q, k, v, qid, kid):
    grid, q_spec, k_spec, qid_spec, kid_spec, stat_spec, work = attend_specs(q, k)
    return pl.pallas_call(
        attend_kernel,
        grid=grid,
        in_specs=[q_spec, k_spec, k_spec, qid_spec, kid_spec],
        out_specs=[q_spec, stat_spec],
        out_shape=[
            jax.ShapeDtypeStruct(q.shape, BF),
            jax.ShapeDtypeStruct((*grid, q.shape[1], PAIR), F32),
        ],
        cost_estimate=pl.CostEstimate(flops=16 * work, bytes_accessed=4 * k.size * 2, transcendentals=work // HEAD_DIM),
        compiler_params=pltpu.CompilerParams(vmem_limit_bytes=40 * 2**20),
    )(q, k, v, qid, kid)


def attend_back(q, k, v, g, qid, kid, stats=None):
    grid, q_spec, k_spec, qid_spec, kid_spec, stat_spec, work = attend_specs(q, k)
    saved = stats is not None
    low = lambda v: jax.ShapeDtypeStruct(v.shape, BF)
    return pl.pallas_call(
        functools.partial(attend_back_kernel, saved),
        grid=grid,
        in_specs=[q_spec, k_spec, k_spec, q_spec, qid_spec, kid_spec] + ([stat_spec] if saved else []),
        out_specs=([] if saved else [q_spec]) + [q_spec, k_spec, k_spec],
        out_shape=([] if saved else [low(q)]) + [low(q), low(k), low(v)],
        cost_estimate=pl.CostEstimate(flops=48 * work, bytes_accessed=6 * k.size * 2, transcendentals=work // HEAD_DIM),
        compiler_params=pltpu.CompilerParams(vmem_limit_bytes=40 * 2**20),
    )(q, k, v, g, qid, kid, *([stats] if saved else []))


def tie(x, *deps):
    return lax.optimization_barrier((x, *deps))


def turn_batch(x):
    size = lax.axis_size("batch")
    return lax.ppermute(x, "batch", [(i, size - 1 - i) for i in range(size)])


def turn_low(x):
    return swap(x, 1)


def turn_high(x):
    return swap(x, 2)


def halve(x, turn, bit):
    halves = x.reshape(2, x.shape[0] // 2, x.shape[1])
    send = lax.dynamic_index_in_dim(halves, 1 - bit, 0, keepdims=False).astype(BF)
    keep = lax.dynamic_index_in_dim(halves, bit, 0, keepdims=False)
    return keep.astype(F32) + turn(send).astype(F32)


def join(x, turn, bit):
    x = x.astype(BF)
    other = turn(x)
    return jnp.concatenate([jnp.where(bit == 0, x, other), jnp.where(bit == 0, other, x)], axis=0)


def reduce_ff(d_in, d_mlp):
    place = lax.axis_index("head")
    x_bit, y_bit = lax.axis_index("batch"), place >> 1
    core = (place & 1) == 1
    d_in, d_mlp = d_in.astype(BF), d_mlp.astype(BF)
    mine = jnp.where(core, d_mlp, d_in).astype(F32) + turn_low(jnp.where(core, d_in, d_mlp)).astype(F32)
    cut = mine.shape[0] // 2
    a, b = mine[:cut], mine[cut:]
    a, b = halve(a, turn_batch, x_bit), halve(b, turn_high, y_bit)
    a, b = halve(a, turn_high, y_bit), halve(b, turn_batch, x_bit)
    a, b = join(a, turn_high, y_bit), join(b, turn_batch, x_bit)
    a, b = join(a, turn_batch, x_bit), join(b, turn_high, y_bit)
    full = jnp.concatenate([a, b], axis=0)
    other = turn_low(full)
    return jnp.where(core, other, full).astype(F32), jnp.where(core, full, other).astype(F32)


def reduce_attn(own, partner):
    batch = lax.axis_index("batch")
    wide = lax.axis_index("wide")
    size = lax.axis_size("wide")
    own = own + turn_high(partner.astype(BF)).astype(F32)
    rows, width = own.shape
    mine = halve(own, turn_batch, batch)
    blocks = mine.reshape(size, -1, width)
    if size <= DIRECT:
        pick = lambda s: lax.dynamic_index_in_dim(blocks, (wide - s) % size, 0, keepdims=False)
        arrived = [shift(pick(s).astype(BF), -s) for s in range(1, size)]
        total = pick(0)
        for piece in arrived:
            total = total + piece.astype(F32)
        total = total.astype(BF)
        full = jnp.zeros(blocks.shape, BF)
        for s in range(size):
            piece = shift(total, s) if s else total
            full = lax.dynamic_update_index_in_dim(full, piece, (wide - s) % size, 0)
    else:
        total = lax.psum_scatter(blocks.astype(BF), "wide", scatter_dimension=0, tiled=False)
        full = lax.all_gather(total, "wide", axis=0, tiled=False)
    return join(full.reshape(rows // 2, width), turn_batch, batch).astype(F32)


def sum_all(x):
    x = x + turn_low(x)
    x = x + turn_high(x)
    x = x + turn_batch(x)
    size = lax.axis_size("wide")
    if size > DIRECT:
        return lax.psum(x, "wide")
    total = x
    for s in range(1, size):
        total = total + shift(x, s)
    return total


def general(tokens, patches, w_qkv, w_att, w_in, w_mlp, gains, cotangent):
    rows_all, slots, width = tokens.shape
    wide = lax.axis_size("wide")
    place = lax.axis_index("head")
    wide_place = lax.axis_index("wide")
    levels = w_qkv.shape[0]
    group = w_att.shape[1]
    n = rows_all * slots // 4
    rows = rows_all // 2

    def assemble(own, other, count):
        if rows == 1:
            return jnp.concatenate([own, other], axis=0)[None]
        half = rows // 2
        def turn(v):
            v = v.reshape(count, half, slots, *v.shape[1:])
            return jnp.moveaxis(v, 1, 0).reshape(half, count * slots, *v.shape[3:])
        return jnp.concatenate([turn(own), turn(other)], axis=0)

    def take_apart(v, count):
        if rows == 1:
            return v[0, : count * n], v[0, count * n :]
        half = rows // 2
        def turn(u):
            u = u.reshape(half, count, slots, *u.shape[2:])
            return jnp.moveaxis(u, 1, 0).reshape(count * n, *u.shape[3:])
        return turn(v[:half]), turn(v[half:])

    ends = jnp.cumsum(patches, axis=1)
    slot_index = jnp.arange(slots * wide, dtype=jnp.int32)
    image = jnp.sum((slot_index[None, :, None] >= ends[:, None, :]).astype(jnp.int32), axis=2)
    image = jnp.where(slot_index[None, :] < ends[:, -1:], image, -1)
    image = image.reshape(rows_all, wide, slots).transpose(1, 0, 2).reshape(wide, 4, n)
    order = (wide_place - jnp.arange(wide)) % wide
    image = image[order]
    own_image = lax.dynamic_index_in_dim(image, place, 1, keepdims=False)
    other_image = lax.dynamic_index_in_dim(image, place ^ 1, 1, keepdims=False)
    key_image = assemble(own_image.reshape(-1), other_image.reshape(-1), wide)
    query_image = assemble(own_image[0], other_image[0], 1)
    key_id = key_image[:, None, :]
    query_id = jnp.where(query_image >= 0, query_image, -2)[:, :, None]

    own = lax.dynamic_index_in_dim(tokens.reshape(4, n, width), place, 0, keepdims=False)
    cot = lax.dynamic_index_in_dim(cotangent.reshape(4, n, width), place, 0, keepdims=False)
    cot_other = lax.dynamic_index_in_dim(cotangent.reshape(4, n, width), place ^ 1, 0, keepdims=False)

    project = lambda act, w: jnp.einsum("rse,ce->rsc", act, w, preferred_element_type=F32).astype(BF)
    pull_back = lambda d, w: jnp.einsum("rkc,ce->rke", d, w, preferred_element_type=F32)
    weigh = lambda d, act: jnp.einsum("rqc,rqe->ce", d, act, preferred_element_type=F32)

    qkv_ws = [swap(w_qkv[l], 2) for l in range(levels)]
    att_ws = [swap(w_att[l], 2) for l in range(levels)]

    def weights(l, qkv_part, att_part):
        return jnp.concatenate([w_qkv[l], qkv_part], axis=1), jnp.concatenate([w_att[l], att_part], axis=0)

    def branch_of(attended, att_w):
        att_own, att_other = take_apart(
            jnp.einsum("rqc,ce->rqe", attended, att_w, preferred_element_type=F32), 1
        )
        return att_own + turn_low(att_other.astype(BF)).astype(F32)

    def act_terms(dq, dk, dv, qkv_w):
        d_act_kv = pull_back(dk, qkv_w[1]) + pull_back(dv, qkv_w[2])
        kv_own, kv_other = take_apart(d_act_kv, wide)
        q_own, q_other = take_apart(pull_back(dq, qkv_w[0]), 1)
        kv_other = kv_other.at[:n].add(q_other).astype(BF)
        return kv_own.at[:n].add(q_own) + turn_low(kv_other).astype(F32)

    def ff_back(pre, ff_grad, l):
        d_hidden = right_dot(ff_grad, w_mlp[l])
        unused, pull = jax.vjp(jax.nn.gelu, pre)
        return pull(d_hidden)[0].astype(BF)

    stream = own.astype(F32)
    saved = []
    for l in range(levels - 1):
        xhat, rstd = norm_parts(stream)
        act = (xhat * gains[l]).astype(BF)
        ff_act = gather_wide(act)
        other_act = turn_low(ff_act)
        pre = right_dot(ff_act, w_in[l])
        hidden = jax.nn.gelu(pre).astype(BF)
        parts = plain_dot(hidden, w_mlp[l])
        parts, ff_act, other_act = tie(parts, ff_act, other_act)
        branch = scatter_wide(parts)
        qkv_w, att_w = weights(l, qkv_ws[l], att_ws[l])
        key_act = assemble(ff_act, other_act, wide)
        query_act = assemble(act, other_act[:n], 1)
        q, k, v = project(query_act, qkv_w[0]), project(key_act, qkv_w[1]), project(key_act, qkv_w[2])
        attended, stats = attend(q, k, v, query_id, key_id)
        branch = branch + branch_of(attended, att_w)
        branch, qkv_ws[l + 1], att_ws[l + 1] = tie(branch, qkv_ws[l + 1], att_ws[l + 1])
        saved.append((xhat, rstd, ff_act, key_act, query_act, qkv_w, att_w, pre, hidden, q, k, v, attended, stats))
        stream = stream + branch

    l = levels - 1
    xhat, rstd = norm_parts(stream)
    act = (xhat * gains[l]).astype(BF)
    qkv_w, att_w = weights(l, qkv_ws[l], att_ws[l])
    query_grad = assemble(cot, cot_other, 1)
    d_attended = project(query_grad, att_w)
    ff_act = gather_wide(act)
    ff_act, cot, d_attended = tie(ff_act, cot, d_attended)
    ff_grad = gather_wide(cot)
    other_act = turn_low(ff_act)
    pre = right_dot(ff_act, w_in[l])
    hidden = jax.nn.gelu(pre).astype(BF)
    key_act = assemble(ff_act, other_act, wide)
    query_act = assemble(act, other_act[:n], 1)
    q, k, v = project(query_act, qkv_w[0]), project(key_act, qkv_w[1]), project(key_act, qkv_w[2])
    attended, dq, dk, dv = attend_back(q, k, v, d_attended, query_id, key_id)
    terms = act_terms(dq, dk, dv, qkv_w)
    d_pre = ff_back(pre, ff_grad, l)
    parts = terms + plain_dot(d_pre, w_in[l])
    parts, hidden, d_pre, dq, dk, dv, attended = tie(parts, hidden, d_pre, dq, dk, dv, attended)
    d_act = scatter_wide(parts)
    pieces = [weigh(dq, query_act), weigh(dk, key_act), weigh(dv, key_act), weigh(attended, query_grad)]
    last_attn = jnp.concatenate([t[:group] for t in pieces]) + turn_high(
        jnp.concatenate([t[group:] for t in pieces]).astype(BF)
    ).astype(F32)
    last_ff = jnp.concatenate([trans_dot(d_pre, ff_act), trans_dot(hidden, ff_grad)]).astype(BF)
    last_branch = branch_of(attended, att_w)
    last_parts = plain_dot(hidden, w_mlp[l])
    d_act, last_parts, last_attn, last_ff = tie(d_act, last_parts, last_attn, last_ff)
    gain_last = jnp.sum(d_act * xhat, axis=0)
    grad = cot.astype(F32) + norm_back(d_act, xhat, rstd, gains[l])
    last_attn = lax.psum(last_attn.astype(BF), ("batch", "wide"))
    last_ff = lax.psum(last_ff, ("batch", "head"))

    assert levels == 2
    l = 0
    xhat, rstd, ff_act, key_act, query_act, qkv_w, att_w, pre, hidden, q, k, v, attended, stats = saved[0]
    low = grad.astype(BF)
    other_low = turn_low(low)
    ff_grad = gather_wide(low)
    query_grad = assemble(low, other_low, 1)
    d_attended = project(query_grad, att_w)
    dq, dk, dv = attend_back(q, k, v, d_attended, query_id, key_id, stats)
    terms = act_terms(dq, dk, dv, qkv_w)
    piece_o, piece_v = weigh(attended, query_grad), weigh(dv, key_act)
    piece_q, piece_k = weigh(dq, query_act), weigh(dk, key_act)
    first_ov = reduce_attn(
        jnp.concatenate([piece_o[:group], piece_v[:group]]), jnp.concatenate([piece_o[group:], piece_v[group:]])
    )
    first_qk = reduce_attn(
        jnp.concatenate([piece_q[:group], piece_k[:group]]), jnp.concatenate([piece_q[group:], piece_k[group:]])
    )
    d_pre = ff_back(pre, ff_grad, l)
    parts = terms + plain_dot(d_pre, w_in[l])
    parts, hidden, d_pre = tie(parts, hidden, d_pre)
    d_act = scatter_wide(parts)
    first_in, first_mlp = reduce_ff(trans_dot(d_pre, ff_act), trans_dot(hidden, ff_grad))
    d_act, last_parts = tie(d_act, last_parts)
    gain_first = jnp.sum(d_act * xhat, axis=0)
    grad = grad + norm_back(d_act, xhat, rstd, gains[l])
    delta = gather_head((grad - cot.astype(F32)).astype(BF))
    d_tokens = cotangent.astype(F32) + delta.reshape(tokens.shape).astype(F32)
    d_gains = sum_all(jnp.stack([gain_first, gain_last]))
    stream = stream + last_branch + scatter_wide(last_parts)
    delta = gather_head((stream - own.astype(F32)).astype(BF))
    out = tokens.astype(F32) + delta.reshape(tokens.shape).astype(F32)
    last_attn = last_attn.astype(F32).reshape(4, group, width)
    last_in, last_mlp = last_ff[: last_ff.shape[0] // 2].astype(F32), last_ff[last_ff.shape[0] // 2 :].astype(F32)
    d_qkv = jnp.stack([jnp.stack([first_qk[:group], first_qk[group:], first_ov[group:]]), last_attn[:3]])
    return (
        out,
        d_tokens,
        d_qkv,
        jnp.stack([first_ov[:group], last_attn[3]]),
        jnp.stack([first_in, last_in]),
        jnp.stack([first_mlp, last_mlp]),
        d_gains,
    )


COST = 2 * 10**10


def full_spec(x):
    return pl.BlockSpec(x.shape, lambda i, *_, nd=x.ndim: (0,) * nd)


def layer_spec(x, l):
    return pl.BlockSpec((1, *x.shape[1:]), lambda i, *_, nd=x.ndim: (l,) + (0,) * (nd - 1))


def call(kernel, grid, ins, outs, scratch=(), prefetch=(), limit=16, cost=COST):
    return pl.pallas_call(
        kernel,
        grid_spec=pltpu.PrefetchScalarGridSpec(
            num_scalar_prefetch=len(prefetch),
            grid=(grid,),
            in_specs=[spec for _, spec in ins],
            out_specs=[spec for _, _, spec in outs],
            scratch_shapes=list(scratch),
        ),
        out_shape=[jax.ShapeDtypeStruct(shape, kind) for shape, kind, _ in outs],
        cost_estimate=pl.CostEstimate(flops=cost, bytes_accessed=0, transcendentals=0),
        compiler_params=pltpu.CompilerParams(vmem_limit_bytes=limit * 2**20),
    )(*prefetch, *[x for x, _ in ins])


def whole_out(shape, kind):
    return (shape, kind, pl.BlockSpec(shape, lambda i, *_, nd=len(shape): (0,) * nd))


def total_of(refs):
    total = refs[0][...].astype(F32)
    for ref in refs[1:]:
        total = total + ref[...].astype(F32)
    return total


def start_norm_kernel(place_ref, tok_ref, gain_ref, act_ref):
    xhat, unused = norm_parts(tok_ref[0].astype(F32))
    act_ref[...] = (xhat * gain_ref[0]).astype(BF)


def start_norm(place, tokens, gains):
    n, width = tokens.shape[1:]
    return call(
        start_norm_kernel,
        1,
        [(tokens, pl.BlockSpec((1, n, width), lambda i, p: (p[0], 0, 0))), (gains, layer_spec(gains, 0))],
        [whole_out((n, width), BF)],
        prefetch=(place,),
    )[0]


def norm_kernel(place_ref, tok_ref, gain_ref, *refs):
    stream_ref, act_ref = refs[-2:]
    stream = tok_ref[0].astype(F32) + total_of(refs[:-2])
    xhat, unused = norm_parts(stream)
    stream_ref[...] = stream
    act_ref[...] = (xhat * gain_ref[0]).astype(BF)


def norm(place, tokens, gains, l, terms):
    n, width = tokens.shape[1:]
    return call(
        norm_kernel,
        1,
        [(tokens, pl.BlockSpec((1, n, width), lambda i, p: (p[0], 0, 0))), (gains, layer_spec(gains, l))]
        + [(t, full_spec(t)) for t in terms],
        [whole_out((n, width), F32), whole_out((n, width), BF)],
        prefetch=(place,),
    )


def norm_back_kernel(first, place_ref, cot_ref, gain_ref, stream_ref, *refs):
    *refs, delta_ref, low_ref, gain_out = refs
    if not first:
        earlier, *refs = refs
    d_act = total_of(refs)
    stream = stream_ref[0] if stream_ref.ndim == 3 else stream_ref[...]
    xhat, rstd = norm_parts(stream.astype(F32))
    gain_out[...] = jnp.sum(d_act * xhat, axis=0, keepdims=True)
    delta = norm_back(d_act, xhat, rstd, gain_ref[0])
    if not first:
        delta = delta + earlier[...]
        low_ref[...] = delta.astype(BF)
    else:
        low_ref[...] = (cot_ref[0].astype(F32) + delta).astype(BF)
    delta_ref[...] = delta


def norm_back_call(place, cotangent, gains, l, stream, terms, earlier=None):
    n, width = cotangent.shape[1:]
    own = pl.BlockSpec((1, n, width), lambda i, p: (p[0], 0, 0))
    first = earlier is None
    return call(
        functools.partial(norm_back_kernel, first),
        1,
        [(cotangent, own), (gains, layer_spec(gains, l))]
        + [(stream, own if stream.ndim == 3 else full_spec(stream))]
        + ([] if first else [(earlier, full_spec(earlier))])
        + [(t, full_spec(t)) for t in terms],
        [whole_out((n, width), F32), whole_out((n, width), BF), whole_out((1, width), F32)],
        prefetch=(place,),
    )


GELU_A = 0.7978845608028654
GELU_B = 0.044715


def gelu_both(x):
    square = x * x
    t = jnp.tanh(GELU_A * (x + GELU_B * (square * x)))
    value = 0.5 * x * (1.0 + t)
    slope = 0.5 * (1.0 + t) + 0.5 * x * (1.0 - t * t) * (GELU_A * (1.0 + 3.0 * GELU_B * square))
    return value, slope


def chunks_of(total):
    step = 256 if total % 256 == 0 else total
    return [slice(i, i + step) for i in range(0, total, step)]


def write_parts(total, n, part_refs):
    for s, ref in enumerate(part_refs):
        ref[...] = total[s * n : (s + 1) * n].astype(ref.dtype)


def ff_kernel(count, *refs):
    x_refs, (in_ref, mlp_ref, slope_ref, hidden_ref, all_ref), part_refs = refs[:count], refs[count : count + 5], refs[count + 5 :]
    n = x_refs[0].shape[0]
    x = jnp.concatenate([r[...] for r in x_refs], axis=0)
    all_ref[...] = x
    total = None
    for cut in chunks_of(in_ref.shape[1]):
        value, slope = gelu_both(right_dot(x, in_ref[0, cut, :]))
        low = value.astype(BF)
        slope_ref[:, cut] = slope
        hidden_ref[:, cut] = low
        term = plain_dot(low, mlp_ref[0, cut, :])
        total = term if total is None else total + term
    write_parts(total, n, part_refs)


def part_outs(count, n, width):
    return [whole_out((n, width), F32 if s == 0 else BF) for s in range(count)]


def ff(xs, w_in, w_mlp, l):
    count, (n, width) = len(xs), xs[0].shape
    hidden = w_in.shape[1]
    slope, low, x_all, *parts = call(
        functools.partial(ff_kernel, count),
        1,
        [(x, full_spec(x)) for x in xs] + [(w_in, layer_spec(w_in, l)), (w_mlp, layer_spec(w_mlp, l))],
        [whole_out((count * n, hidden), F32), whole_out((count * n, hidden), BF), whole_out((count * n, width), BF)]
        + part_outs(count, n, width),
    )
    return slope, low, x_all, parts


def ff_slope_kernel(count, *refs):
    g_refs, (mlp_ref, slope_ref, d_pre_ref, all_ref) = refs[:count], refs[count:]
    g = jnp.concatenate([r[...] for r in g_refs], axis=0)
    all_ref[...] = g
    for cut in chunks_of(mlp_ref.shape[1]):
        d_pre_ref[:, cut] = (slope_ref[:, cut] * right_dot(g, mlp_ref[0, cut, :])).astype(BF)


def ff_slope(gs, w_mlp, l, slope):
    count, (n, width) = len(gs), gs[0].shape
    return call(
        functools.partial(ff_slope_kernel, count),
        1,
        [(g, full_spec(g)) for g in gs] + [(w_mlp, layer_spec(w_mlp, l)), (slope, full_spec(slope))],
        [whole_out(slope.shape, BF), whole_out((count * n, width), BF)],
    )


def ff_back_kernel(n, d_pre_ref, in_ref, own_ref, got_ref, *part_refs):
    total = own_ref[...] + got_ref[...].astype(F32) + plain_dot(d_pre_ref[...], in_ref[0])
    write_parts(total, n, part_refs)


def ff_back(count, d_pre, w_in, l, own, got):
    n, width = d_pre.shape[0] // count, w_in.shape[2]
    return call(
        functools.partial(ff_back_kernel, n),
        1,
        [(d_pre, full_spec(d_pre)), (w_in, layer_spec(w_in, l)), (own, full_spec(own)), (got, full_spec(got))],
        part_outs(count, n, width),
    )


def ff_weights_kernel(place_ref, x_ref, g_ref, d_pre_ref, hidden_ref, keep_ref, send_ref):
    core = (place_ref[0] & 1) == 1
    d_in = trans_dot(d_pre_ref[...], x_ref[...])
    d_mlp = trans_dot(hidden_ref[...], g_ref[...])
    keep_ref[...] = jnp.where(core, d_mlp, d_in)
    send_ref[...] = jnp.where(core, d_in, d_mlp).astype(BF)


def ff_weights(place, xs, gs, d_pre, hidden):
    width = xs.shape[1]
    tokens, size = d_pre.shape
    step = 256 if size % 256 == 0 else size
    cut = pl.BlockSpec((tokens, step), lambda i, p: (0, i))
    out = pl.BlockSpec((step, width), lambda i, p: (i, 0))
    return call(
        ff_weights_kernel,
        size // step,
        [(x, full_spec(x)) for x in (xs, gs)] + [(d_pre, cut), (hidden, cut)],
        [((size, width), F32, out), ((size, width), BF, out)],
        prefetch=(place,),
    )


def attn_kernel(mode, count, *refs):
    refs = list(refs)
    take = lambda k: [refs.pop(0) for _ in range(k)]
    if mode != "back":
        act_refs = take(2)
    if mode != "fwd":
        g_refs = take(2)
    w_own, w_part, a_own, a_part, qid_ref, kid_ref = take(6)
    if mode == "back":
        q_ref, k_ref, v_ref, stat_ref = take(4)
    step = pl.program_id(0)
    scale = HEAD_DIM ** (-0.5)
    n = qid_ref.shape[0] // 2
    half = count * n
    if mode == "fwd":
        q_out, k_out, v_out, o_out, stat_out, b_own, b_other, act_all, branch = refs
    elif mode == "both":
        q_out, k_out, v_out, o_out, t_own, t_other, b_own, b_other, act_all, branch, terms = refs
    else:
        q_out, k_out, v_out, t_own, t_other, terms = refs
    if mode != "back":

        @pl.when(step == 0)
        def _():
            act_all[:half, :] = act_refs[0][...]
            act_all[half:, :] = act_refs[1][...]

    w_kv = jnp.concatenate([w_own[0, 1], w_part[1], w_own[0, 2], w_part[2]], axis=0)
    w_q = jnp.concatenate([w_own[0, 0], w_part[0]], axis=0)
    w_o = jnp.concatenate([a_own[0], a_part[...]], axis=0)
    if mode != "back":
        kv = right_dot(act_all[...], w_kv).astype(BF)
        k, v = kv[:, :PAIR], kv[:, PAIR:]
        q_in = jnp.concatenate([act_refs[0][:n, :], act_refs[1][:n, :]], axis=0)
        q = right_dot(q_in, w_q).astype(BF)
    else:
        q, k, v = q_ref[...], k_ref[...], v_ref[...]
    if mode == "fwd":
        q_out[...], k_out[...], v_out[...] = q, k, v
    q = q * jnp.asarray(scale, BF)
    allowed = qid_ref[...] == kid_ref[...]
    if mode != "fwd":
        g = right_dot(jnp.concatenate([r[...] for r in g_refs], axis=0), w_o).astype(BF)
    lane = lax.broadcasted_iota(jnp.int32, (2 * n, PAIR), 1)
    stats = jnp.zeros((2 * n, PAIR), F32)
    outs, dqs, dks, dvs = [], [], [], []
    for j in range(2):
        cut = slice(j * HEAD_DIM, (j + 1) * HEAD_DIM)
        qj, kj, vj = q[:, cut], k[:, cut], v[:, cut]
        if mode == "back":
            top, inverse = stat_ref[0, :, 2 * j : 2 * j + 1], stat_ref[0, :, 2 * j + 1 : 2 * j + 2]
            probs = jnp.exp(jnp.where(allowed, right_dot(qj, kj), NEGATIVE) - top) * inverse
        else:
            probs, top, inverse = head_softmax(qj, kj, allowed)
            stats = jnp.where(lane == 2 * j, top, jnp.where(lane == 2 * j + 1, inverse, stats))
        low = probs.astype(BF)
        if mode != "back":
            outs.append(plain_dot(low, vj))
        if mode != "fwd":
            gj = g[:, cut]
            dp = right_dot(gj, vj)
            ds = (probs * (dp - jnp.sum(probs * dp, axis=-1, keepdims=True))).astype(BF)
            dqs.append(plain_dot(ds, kj) * scale)
            dks.append(trans_dot(ds, qj))
            dvs.append(trans_dot(low, gj))
    last = step == pl.num_programs(0) - 1
    if mode != "back":
        attended = jnp.concatenate(outs, axis=1).astype(BF)
        o_out[...] = attended
        term = plain_dot(attended, w_o)

        @pl.when(step == 0)
        def _():
            branch[...] = term

        @pl.when(step > 0)
        def _():
            branch[...] += term

        @pl.when(last)
        def _():
            b_own[...] = branch[:n, :]
            b_other[...] = branch[n:, :].astype(BF)

    if mode == "fwd":
        stat_out[0] = stats
    else:
        dq = jnp.concatenate(dqs, axis=1).astype(BF)
        dkv = jnp.concatenate(dks + dvs, axis=1).astype(BF)
        q_out[...], k_out[...], v_out[...] = dq, dkv[:, :PAIR], dkv[:, PAIR:]
        term_kv = plain_dot(dkv, w_kv)
        term_q = plain_dot(dq, w_q)

        @pl.when(step == 0)
        def _():
            terms[...] = term_kv

        @pl.when(step > 0)
        def _():
            terms[...] += term_kv

        terms[:n, :] += term_q[:n]
        terms[half : half + n, :] += term_q[n:]

        @pl.when(last)
        def _():
            t_own[...] = terms[:half, :]
            t_other[...] = terms[half:, :].astype(BF)


def attn(mode, count, l, w_qkv, w_att, qkv_part, att_part, qid, kid, acts=(), grads=(), kept=()):
    group, width = att_part.shape
    n = qid.shape[0] // 2
    tq, tk = 2 * n, 2 * count * n
    steps = group // HEAD_DIM
    pair_q = pl.BlockSpec((tq, PAIR), lambda i: (0, i))
    pair_k = pl.BlockSpec((tk, PAIR), lambda i: (0, i))
    stat = pl.BlockSpec((1, tq, PAIR), lambda i: (i, 0, 0))
    ins = [(x, full_spec(x)) for x in (*acts, *grads)] + [
        (w_qkv, pl.BlockSpec((1, 3, HEAD_DIM, width), lambda i: (l, 0, i, 0))),
        (qkv_part, pl.BlockSpec((3, HEAD_DIM, width), lambda i: (0, i, 0))),
        (w_att, pl.BlockSpec((1, HEAD_DIM, width), lambda i: (l, i, 0))),
        (att_part, pl.BlockSpec((HEAD_DIM, width), lambda i: (i, 0))),
        (qid, full_spec(qid)),
        (kid, full_spec(kid)),
    ]
    if mode == "back":
        q, k, v, stats = kept
        ins += [(q, pair_q), (k, pair_k), (v, pair_k), (stats, stat)]
    q_shape, k_shape = (tq, 2 * group), (tk, 2 * group)
    outs = [(q_shape, BF, pair_q), (k_shape, BF, pair_k), (k_shape, BF, pair_k)]
    scratch = []
    if mode != "back":
        outs += [(q_shape, BF, pair_q)]
        scratch += [pltpu.VMEM((tk, width), BF), pltpu.VMEM((tq, width), F32)]
    if mode == "fwd":
        outs += [((steps, tq, PAIR), F32, stat)]
    else:
        outs += [whole_out((tk // 2, width), F32), whole_out((tk // 2, width), BF)]
        scratch += [pltpu.VMEM((tk, width), F32)]
    if mode != "back":
        outs += [whole_out((n, width), F32), whole_out((n, width), BF)]
    return call(functools.partial(attn_kernel, mode, count), steps, ins, outs, scratch, limit=28)


def attn_weights_kernel(own_act, other_act, g_own, g_other, dq_ref, dk_ref, dv_ref, o_ref, own_ref, part_ref, act_all):
    half = act_all.shape[0] // 2
    n = g_own.shape[0]

    @pl.when(pl.program_id(0) == 0)
    def _():
        act_all[:half, :] = own_act[...]
        act_all[half:, :] = other_act[...]

    q_in = jnp.concatenate([own_act[:n, :], other_act[:n, :]], axis=0)
    g_in = jnp.concatenate([g_own[...], g_other[...]], axis=0)
    kv = trans_dot(jnp.concatenate([dk_ref[...], dv_ref[...]], axis=1), act_all[...])
    for t, pair in enumerate((trans_dot(dq_ref[...], q_in), kv[:PAIR], kv[PAIR:], trans_dot(o_ref[...], g_in))):
        own_ref[t] = pair[:HEAD_DIM]
        part_ref[t] = pair[HEAD_DIM:].astype(BF)


def attn_weights(acts, grads, dq, dk, dv, attended):
    n, width = grads[0].shape
    tq, tk, group = 2 * n, 2 * acts[0].shape[0], dq.shape[1] // 2
    pair_q = pl.BlockSpec((tq, PAIR), lambda i: (0, i))
    pair_k = pl.BlockSpec((tk, PAIR), lambda i: (0, i))
    out = pl.BlockSpec((4, HEAD_DIM, width), lambda i: (0, i, 0))
    return call(
        attn_weights_kernel,
        group // HEAD_DIM,
        [(x, full_spec(x)) for x in (*acts, *grads)] + [(dq, pair_q), (dk, pair_k), (dv, pair_k), (attended, pair_q)],
        [((4, group, width), F32, out), ((4, group, width), BF, out)],
        [pltpu.VMEM((tk, width), BF)],
    )


def spread_kernel(place_ref, base_ref, *refs):
    *refs, out_ref = refs
    for j, ref in enumerate(refs):

        @pl.when(pl.program_id(0) == j)
        def _():
            out_ref[0] = base_ref[0].astype(F32) + ref[...].astype(F32)


def spread(place, base, blocks, col):
    n, width = base.shape[1:]
    block = pl.BlockSpec((1, n, width), lambda i, p: (i ^ p[0], 0, 0))
    return call(
        spread_kernel,
        4,
        [(base, block)] + [(x, pl.BlockSpec((n, width), lambda i, p: (0, col))) for x in blocks],
        [(base.shape, F32, block)],
        prefetch=(place,),
    )[0]


def gather_list(x):
    return [x] + [shift(x, s) for s in range(1, lax.axis_size("wide"))]


def return_list(parts):
    return [parts[0]] + [shift(p, -s) for s, p in enumerate(parts) if s]


def reduce_ff_rest(keep, got):
    x_bit, y_bit = lax.axis_index("batch"), lax.axis_index("head") >> 1
    core = (lax.axis_index("head") & 1) == 1
    mine = keep + got.astype(F32)
    cut = mine.shape[0] // 2
    a, b = mine[:cut], mine[cut:]
    a, b = halve(a, turn_batch, x_bit), halve(b, turn_high, y_bit)
    a, b = halve(a, turn_high, y_bit), halve(b, turn_batch, x_bit)
    a, b = join(a, turn_high, y_bit), join(b, turn_batch, x_bit)
    a, b = join(a, turn_batch, x_bit), join(b, turn_high, y_bit)
    full = jnp.concatenate([a, b], axis=0)
    other = turn_low(full)
    return jnp.where(core, other, full), jnp.where(core, full, other)


def together(*pairs):
    sent = tie(*[x for x, _ in pairs])
    return tie(*[f(x) for x, (_, f) in zip(sent, pairs)])


def half_of(x, bit):
    halves = x.reshape(2, x.shape[0] // 2, x.shape[1])
    return (
        lax.dynamic_index_in_dim(halves, bit, 0, keepdims=False),
        lax.dynamic_index_in_dim(halves, 1 - bit, 0, keepdims=False).astype(BF),
    )


def shifts(sign):
    return [functools.partial(shift, step=sign * s) for s in range(1, lax.axis_size("wide"))]


def blocks_of(x):
    wide, size = lax.axis_index("wide"), lax.axis_size("wide")
    blocks = x.reshape(size, -1, x.shape[1])
    own, *others = [lax.dynamic_index_in_dim(blocks, (wide - s) % size, 0, keepdims=False) for s in range(size)]
    return own, [o.astype(BF) for o in others]


def laid(pieces):
    wide, size = lax.axis_index("wide"), lax.axis_size("wide")
    full = jnp.zeros((size, *pieces[0].shape), pieces[0].dtype)
    for s, piece in enumerate(pieces):
        full = lax.dynamic_update_index_in_dim(full, piece, (wide - s) % size, 0)
    return full.reshape(-1, pieces[0].shape[1])


def ordered(mine, other, bit):
    return jnp.where(bit == 0, mine, other), jnp.where(bit == 0, other, mine)


def sum_of(first, pieces):
    total = first.astype(F32)
    for piece in pieces:
        total = total + piece.astype(F32)
    return total


def fast(tokens, patches, w_qkv, w_att, w_in, w_mlp, gains, cotangent):
    rows_all, slots, width = tokens.shape
    shape = tokens.shape
    wide = lax.axis_size("wide")
    head_place, wide_place = lax.axis_index("head"), lax.axis_index("wide")
    place = head_place.reshape(1)
    group = w_att.shape[1]
    n = rows_all * slots // 4
    tokens, cotangent = tokens.reshape(4, n, width), cotangent.reshape(4, n, width)
    gains = gains[:, None, :]

    own_ws = [jnp.concatenate([w_qkv[l], w_att[l][None]]) for l in range(2)]
    act = start_norm(place, tokens, gains)
    xs = gather_list(act)
    part0 = turn_high(own_ws[0])

    ends = jnp.cumsum(patches, axis=1)
    slot_index = jnp.arange(slots * wide, dtype=jnp.int32)
    image = jnp.sum((slot_index[None, :, None] >= ends[:, None, :]).astype(jnp.int32), axis=2)
    image = jnp.where(slot_index[None, :] < ends[:, -1:], image, -1)
    image = image.reshape(rows_all, wide, slots).transpose(1, 0, 2).reshape(wide, 4, n)
    order = (wide_place - jnp.arange(wide)) % wide
    image = image[order]
    own_image = lax.dynamic_index_in_dim(image, head_place, 1, keepdims=False)
    other_image = lax.dynamic_index_in_dim(image, head_place ^ 1, 1, keepdims=False)
    kid = jnp.concatenate([own_image.reshape(-1), other_image.reshape(-1)])[None, :]
    qid = jnp.concatenate([own_image[0], other_image[0]])
    qid = jnp.where(qid >= 0, qid, -2)[:, None]
    cot = lax.dynamic_index_in_dim(cotangent, head_place, 0, keepdims=False)
    cot_other = lax.dynamic_index_in_dim(cotangent, head_place ^ 1, 0, keepdims=False)

    slope0, hidden0, own0, parts = ff(xs, w_in, w_mlp, 0)
    terms = return_list(parts)
    acts0 = (own0, turn_low(own0))
    part0, next_w = tie(part0, own_ws[1])
    part1 = turn_high(next_w)
    q, k, v, attended0, stats, b_own, b_other = attn(
        "fwd", wide, 0, w_qkv, w_att, part0[:3], part0[3], qid, kid, acts=acts0
    )
    b_got = turn_low(b_other)
    stream1, act = norm(place, tokens, gains, 1, [*terms, b_own, b_got])

    xs1 = gather_list(act)
    slope1, hidden1, own1, out_parts = ff(xs1, w_in, w_mlp, 1)
    other1 = turn_low(own1)
    cot_tied, unused = tie(cot, own1)
    gs1 = gather_list(cot_tied)
    dq1, dk1, dv1, attended1, t_own, t_other, b_own1, b_other1 = attn(
        "both", wide, 1, w_qkv, w_att, part1[:3], part1[3], qid, kid, acts=(own1, other1), grads=(cot, cot_other)
    )
    t_got = turn_low(t_other)
    d_pre1, g_all1 = ff_slope(gs1, w_mlp, 1, slope1)
    parts = list(ff_back(wide, d_pre1, w_in, 1, t_own, t_got))
    parts[1], dq1, hidden1, b_other1 = tie(parts[1], dq1, hidden1, b_other1)
    back1 = return_list(parts)
    own_w1, part_w1 = attn_weights((own1, other1), (cot, cot_other), dq1, dk1, dv1, attended1)
    keep1, send1 = ff_weights(place, own1, g_all1, d_pre1, hidden1)
    x_bit, y_bit, core = lax.axis_index("batch"), head_place >> 1, (head_place & 1) == 1
    cut = 2 * group
    flat = lambda v: v.reshape(-1, width)

    def first_sends(own_w, part_w):
        own_w, part_w = flat(own_w), flat(part_w)
        keep_own, send_own = half_of(own_w[cut:], x_bit)
        keep_part, send_part = half_of(part_w[cut:], x_bit)
        return part_w[:cut], jnp.concatenate([send_own, send_part]), own_w[:cut], keep_own, keep_part

    def second_sends(got_y, got_x, own_qk, keep_own, keep_part):
        keep_qk, send_qk = half_of(own_qk + got_y.astype(F32), x_bit)
        half = keep_own.shape[0]
        return send_qk, sum_of(keep_part, [got_x[half:]]).astype(BF), keep_qk, sum_of(keep_own, [got_x[:half]])

    y_send, x_send, *kept_w1 = first_sends(own_w1, part_w1)
    got_y, got_x = turn_high(y_send), turn_batch(x_send)
    b_got1 = turn_low(b_other1)
    back1[1], b_got1 = tie(back1[1], b_got1)
    delta1, low, gain1 = norm_back_call(place, cotangent, gains, 1, stream1, back1)

    low_other = turn_low(low)
    gs = gather_list(low)
    low_other, got_y, got_x = tie(low_other, got_y, got_x)
    x_send, y_send, keep_qk, keep_vo = second_sends(got_y, got_x, *kept_w1)
    got_x1, got_y1 = turn_batch(x_send), turn_high(y_send)
    dq, dk, dv, t_own, t_other = attn(
        "back", wide, 0, w_qkv, w_att, part0[:3], part0[3], qid, kid, grads=(low, low_other), kept=(q, k, v, stats)
    )
    t_other, got_x1, got_y1 = tie(t_other, got_x1, got_y1)
    t_got = turn_low(t_other)
    mine_w1 = jnp.concatenate([sum_of(keep_qk, [got_x1]), sum_of(keep_vo, [got_y1])])
    own_w0, part_w0 = attn_weights(acts0, (low, low_other), dq, dk, dv, attended0)
    gs[1], own_w0, part_w0 = tie(gs[1], own_w0, part_w0)
    d_pre0, g_all0 = ff_slope(gs, w_mlp, 0, slope0)
    parts = list(ff_back(wide, d_pre0, w_in, 0, t_own, t_got))
    parts[1], hidden0, own_w0, part_w0 = tie(parts[1], hidden0, own_w0, part_w0)
    back0 = return_list(parts)
    y_send, x_send, *kept_w0 = first_sends(own_w0, part_w0)
    got_y, got_x = turn_high(y_send), turn_batch(x_send)
    keep0, send0 = ff_weights(place, own0, g_all0, d_pre0, hidden0)
    back0[1], keep0 = tie(back0[1], keep0)
    delta0, low0, gain0 = norm_back_call(place, cotangent, gains, 0, tokens, back0, delta1)

    order = (wide_place - jnp.arange(wide)) % wide
    blocks = jnp.stack([out_parts[0].astype(BF), *out_parts[1:]])[order]
    last = lax.psum_scatter(blocks, "wide", scatter_dimension=0, tiled=False)
    tok = lax.dynamic_index_in_dim(tokens, head_place, 0, keepdims=False).astype(F32)
    b_got1, last, stream1, low0 = tie(b_got1, last, stream1, low0)
    delta_out = (stream1 - tok + sum_of(b_own1, [b_got1, last])).astype(BF)
    ends2 = jnp.concatenate([delta_out, low0], axis=1)

    x_send, y_send, keep_qk, keep_vo = second_sends(got_y, got_x, *kept_w0)
    keep_f = jnp.concatenate([keep0, keep1], axis=1)
    send_f = jnp.concatenate([send0, send1], axis=1)
    gain = jnp.concatenate([gain0, gain1])
    got_x, got_y, got_f, got_g, ends_y = together(
        (x_send, turn_batch), (y_send, turn_high), (send_f, turn_low), (gain, turn_low), (ends2, turn_high)
    )
    gain = gain + got_g
    mine_w0 = jnp.concatenate([sum_of(keep_qk, [got_x]), sum_of(keep_vo, [got_y])])
    own_b0, send_b0 = blocks_of(mine_w0)
    own_b1, send_b1 = blocks_of(mine_w1)
    keep_f, send_f = half_of(sum_of(keep_f, [got_f]), y_bit)
    *got_b, got_f = together(
        *[(jnp.concatenate([p, q]), f) for p, q, f in zip(send_b0, send_b1, shifts(-1))], (send_f, turn_high)
    )
    block = sum_of(jnp.concatenate([own_b0, own_b1]), got_b).astype(BF)
    size = block.shape[0] // 2
    keep_f, send_f = half_of(sum_of(keep_f, [got_f]), x_bit)
    *got_b1, got_f, got_g = together(
        *[(block[size:], f) for f in shifts(1)], (send_f, turn_batch), (gain, turn_high)
    )
    gain = gain + got_g
    full1 = laid([block[size:], *got_b1])
    quarter = sum_of(keep_f, [got_f]).astype(BF)
    *got_b0, got_w1, got_f = together(
        *[(block[:size], f) for f in shifts(1)], (full1, turn_batch), (quarter, turn_batch)
    )
    full0 = laid([block[:size], *got_b0])
    half_f = jnp.concatenate(ordered(quarter, got_f, x_bit))
    ends4 = jnp.concatenate([ends2, ends_y])
    got_w0, got_f, got_g, ends_core = together(
        (full0, turn_batch), (half_f, turn_high), (gain, turn_batch), (ends4, turn_low)
    )
    gain = gain + got_g
    full_f = jnp.concatenate(ordered(half_f, got_f, y_bit))
    *got_g, got_f = together(*[(gain, f) for f in shifts(1)], (full_f, turn_low))
    d_gains = sum_of(gain, got_g)
    ins, mlps = jnp.where(core, got_f, full_f), jnp.where(core, full_f, got_f)
    in0, in1, mlp0, mlp1 = ins[:, :width], ins[:, width:], mlps[:, :width], mlps[:, width:]

    def heads_of(full, got):
        q_, k_ = ordered(full[:group], got[:group], x_bit)
        v_, o_ = ordered(full[group:], got[group:], x_bit)
        return jnp.stack([q_, k_, v_, o_])

    attn0, attn1 = heads_of(full0, got_w0), heads_of(full1, got_w1)
    quads = (ends2, ends_core[:n], ends_y, ends_core[n:])
    out = spread(place, tokens, quads, 0)
    d_tokens = spread(place, cotangent, quads, 1)
    return (
        out.reshape(shape),
        d_tokens.reshape(shape),
        jnp.stack([attn0[:3], attn1[:3]]).astype(F32),
        jnp.stack([attn0[3], attn1[3]]).astype(F32),
        jnp.stack([in0, in1]).astype(F32),
        jnp.stack([mlp0, mlp1]).astype(F32),
        d_gains,
    )


def solution(mesh):
    def local(*arrays):
        tokens, w_qkv = arrays[0], arrays[2]
        small = tokens.shape[0] == 2 and lax.axis_size("wide") <= DIRECT and w_qkv.shape[0] == 2
        return (fast if small else general)(*arrays)

    return jax.shard_map(
        local,
        mesh=mesh,
        in_specs=(
            P("batch", "wide", None),
            P("batch", None),
            P(None, None, "head", None),
            P(None, "head", None),
            P(None, "wide", None),
            P(None, "wide", None),
            P(),
            P("batch", "wide", None),
        ),
        out_specs=(
            P("batch", "wide", None),
            P("batch", "wide", None),
            P(None, None, "head", None),
            P(None, "head", None),
            P(None, "wide", None),
            P(None, "wide", None),
            P(),
        ),
        check_vma=False,
    )
```

```python
import functools

import jax
import jax.numpy as jnp
from jax import lax
from jax.experimental import pallas as pl
from jax.experimental.pallas import tpu as pltpu
from jax.sharding import PartitionSpec as P

HEAD_DIM = 64
EPS = 1e-06
NEGATIVE = -1e30
BF = jnp.bfloat16
F32 = jnp.float32
DIRECT = 8


def norm_parts(stream):
    centre = jnp.mean(stream, axis=-1, keepdims=True)
    centred = stream - centre
    spread = jnp.mean(centred * centred, axis=-1, keepdims=True)
    rstd = lax.rsqrt(spread + EPS)
    return centred * rstd, rstd


def norm_back(d_act, xhat, rstd, gain_row):
    dxh = d_act * gain_row
    m1 = jnp.mean(dxh, axis=-1, keepdims=True)
    m2 = jnp.mean(dxh * xhat, axis=-1, keepdims=True)
    return (dxh - m1 - xhat * m2) * rstd


def trans_dot(left, right):
    return lax.dot_general(left, right, (((0,), (0,)), ((), ())), preferred_element_type=F32)


def right_dot(left, right):
    return lax.dot_general(left, right, (((1,), (1,)), ((), ())), preferred_element_type=F32)


def plain_dot(left, right):
    return jnp.dot(left, right, preferred_element_type=F32)


def swap(x, bit):
    size = lax.axis_size("head")
    return lax.ppermute(x, "head", [(i, i ^ bit) for i in range(size)])


def shift(x, step):
    size = lax.axis_size("wide")
    return lax.ppermute(x, "wide", [(i, (i + step) % size) for i in range(size)])


def gather_wide(x):
    size = lax.axis_size("wide")
    if size <= DIRECT:
        return jnp.concatenate([x] + [shift(x, s) for s in range(1, size)], axis=0)
    whole = lax.all_gather(x, "wide", axis=0, tiled=False)
    order = (lax.axis_index("wide") - jnp.arange(size)) % size
    return whole[order].reshape(size * x.shape[0], *x.shape[1:])


def scatter_wide(parts):
    size = lax.axis_size("wide")
    rows = parts.shape[0] // size
    if size <= DIRECT:
        total = parts[:rows]
        low = [shift(parts[s * rows : (s + 1) * rows].astype(BF), -s) for s in range(1, size)]
        for piece in low:
            total = total + piece.astype(F32)
        return total
    order = (lax.axis_index("wide") - jnp.arange(size)) % size
    blocks = parts.astype(BF).reshape(size, rows, -1)[order]
    return lax.psum_scatter(blocks, "wide", scatter_dimension=0, tiled=False).astype(F32)


def gather_head(x):
    place = lax.axis_index("head")
    a = x
    b = swap(x, 2)
    c = swap(a, 1)
    d = swap(b, 1)
    low_bit = (place & 1) == 1
    high_bit = (place & 2) == 2
    a, c = jnp.where(low_bit, c, a), jnp.where(low_bit, a, c)
    b, d = jnp.where(low_bit, d, b), jnp.where(low_bit, b, d)
    a, b = jnp.where(high_bit, b, a), jnp.where(high_bit, a, b)
    c, d = jnp.where(high_bit, d, c), jnp.where(high_bit, c, d)
    return jnp.stack([a, c, b, d])


PAIR = 2 * HEAD_DIM
FLOOR = -1e29


def head_softmax(q, k, allowed):
    s = jnp.where(allowed, right_dot(q, k), NEGATIVE)
    top = jnp.maximum(jnp.max(s, axis=-1, keepdims=True), FLOOR)
    expo = jnp.exp(s - top)
    inverse = 1.0 / jnp.maximum(jnp.sum(expo, axis=-1, keepdims=True), 1.0)
    return expo * inverse, top, inverse


def attend_kernel(q_ref, k_ref, v_ref, qid_ref, kid_ref, o_ref, stat_ref):
    allowed = qid_ref[0] == kid_ref[0]
    q = q_ref[0] * jnp.asarray(HEAD_DIM ** (-0.5), BF)
    k, v = k_ref[0], v_ref[0]
    lane = lax.broadcasted_iota(jnp.int32, (q.shape[0], PAIR), 1)
    stats = jnp.zeros((q.shape[0], PAIR), F32)
    outs = []
    for j in range(2):
        cut = slice(j * HEAD_DIM, (j + 1) * HEAD_DIM)
        probs, top, inverse = head_softmax(q[:, cut], k[:, cut], allowed)
        outs.append(plain_dot(probs.astype(BF), v[:, cut]))
        stats = jnp.where(lane == 2 * j, top, jnp.where(lane == 2 * j + 1, inverse, stats))
    o_ref[0] = jnp.concatenate(outs, axis=1).astype(BF)
    stat_ref[0, 0] = stats


def attend_back_kernel(saved, q_ref, k_ref, v_ref, g_ref, qid_ref, kid_ref, *refs):
    if saved:
        stat_ref, dq_ref, dk_ref, dv_ref = refs
    else:
        o_ref, dq_ref, dk_ref, dv_ref = refs
    allowed = qid_ref[0] == kid_ref[0]
    scale = HEAD_DIM ** (-0.5)
    q = q_ref[0] * jnp.asarray(scale, BF)
    k, v, g = k_ref[0], v_ref[0], g_ref[0]
    outs, dqs, dks, dvs = [], [], [], []
    for j in range(2):
        cut = slice(j * HEAD_DIM, (j + 1) * HEAD_DIM)
        qj, kj, vj, gj = q[:, cut], k[:, cut], v[:, cut], g[:, cut]
        if saved:
            top = stat_ref[0, 0, :, 2 * j : 2 * j + 1]
            inverse = stat_ref[0, 0, :, 2 * j + 1 : 2 * j + 2]
            probs = jnp.exp(jnp.where(allowed, right_dot(qj, kj), NEGATIVE) - top) * inverse
        else:
            probs, top, inverse = head_softmax(qj, kj, allowed)
        low = probs.astype(BF)
        if not saved:
            outs.append(plain_dot(low, vj))
        dp = right_dot(gj, vj)
        ds = (probs * (dp - jnp.sum(probs * dp, axis=-1, keepdims=True))).astype(BF)
        dqs.append(plain_dot(ds, kj) * scale)
        dks.append(trans_dot(ds, qj))
        dvs.append(trans_dot(low, gj))
    if not saved:
        o_ref[0] = jnp.concatenate(outs, axis=1).astype(BF)
    dq_ref[0] = jnp.concatenate(dqs, axis=1).astype(BF)
    dk_ref[0] = jnp.concatenate(dks, axis=1).astype(BF)
    dv_ref[0] = jnp.concatenate(dvs, axis=1).astype(BF)


def attend_specs(q, k):
    rows, tq, width = q.shape
    tk = k.shape[1]
    q_spec = pl.BlockSpec((1, tq, PAIR), lambda r, j: (r, 0, j))
    k_spec = pl.BlockSpec((1, tk, PAIR), lambda r, j: (r, 0, j))
    qid_spec = pl.BlockSpec((1, tq, 1), lambda r, j: (r, 0, 0))
    kid_spec = pl.BlockSpec((1, 1, tk), lambda r, j: (r, 0, 0))
    stat_spec = pl.BlockSpec((1, 1, tq, PAIR), lambda r, j: (r, j, 0, 0))
    work = rows * tq * tk * width
    return (rows, width // PAIR), q_spec, k_spec, qid_spec, kid_spec, stat_spec, work


def attend(q, k, v, qid, kid):
    grid, q_spec, k_spec, qid_spec, kid_spec, stat_spec, work = attend_specs(q, k)
    return pl.pallas_call(
        attend_kernel,
        grid=grid,
        in_specs=[q_spec, k_spec, k_spec, qid_spec, kid_spec],
        out_specs=[q_spec, stat_spec],
        out_shape=[
            jax.ShapeDtypeStruct(q.shape, BF),
            jax.ShapeDtypeStruct((*grid, q.shape[1], PAIR), F32),
        ],
        cost_estimate=pl.CostEstimate(flops=16 * work, bytes_accessed=4 * k.size * 2, transcendentals=work // HEAD_DIM),
        compiler_params=pltpu.CompilerParams(vmem_limit_bytes=40 * 2**20),
    )(q, k, v, qid, kid)


def attend_back(q, k, v, g, qid, kid, stats=None):
    grid, q_spec, k_spec, qid_spec, kid_spec, stat_spec, work = attend_specs(q, k)
    saved = stats is not None
    low = lambda v: jax.ShapeDtypeStruct(v.shape, BF)
    return pl.pallas_call(
        functools.partial(attend_back_kernel, saved),
        grid=grid,
        in_specs=[q_spec, k_spec, k_spec, q_spec, qid_spec, kid_spec] + ([stat_spec] if saved else []),
        out_specs=([] if saved else [q_spec]) + [q_spec, k_spec, k_spec],
        out_shape=([] if saved else [low(q)]) + [low(q), low(k), low(v)],
        cost_estimate=pl.CostEstimate(flops=48 * work, bytes_accessed=6 * k.size * 2, transcendentals=work // HEAD_DIM),
        compiler_params=pltpu.CompilerParams(vmem_limit_bytes=40 * 2**20),
    )(q, k, v, g, qid, kid, *([stats] if saved else []))


def tie(x, *deps):
    return lax.optimization_barrier((x, *deps))


def turn_batch(x):
    size = lax.axis_size("batch")
    return lax.ppermute(x, "batch", [(i, size - 1 - i) for i in range(size)])


def turn_low(x):
    return swap(x, 1)


def turn_high(x):
    return swap(x, 2)


def halve(x, turn, bit):
    halves = x.reshape(2, x.shape[0] // 2, x.shape[1])
    send = lax.dynamic_index_in_dim(halves, 1 - bit, 0, keepdims=False).astype(BF)
    keep = lax.dynamic_index_in_dim(halves, bit, 0, keepdims=False)
    return keep.astype(F32) + turn(send).astype(F32)


def join(x, turn, bit):
    x = x.astype(BF)
    other = turn(x)
    return jnp.concatenate([jnp.where(bit == 0, x, other), jnp.where(bit == 0, other, x)], axis=0)


def reduce_ff(d_in, d_mlp):
    place = lax.axis_index("head")
    x_bit, y_bit = lax.axis_index("batch"), place >> 1
    core = (place & 1) == 1
    d_in, d_mlp = d_in.astype(BF), d_mlp.astype(BF)
    mine = jnp.where(core, d_mlp, d_in).astype(F32) + turn_low(jnp.where(core, d_in, d_mlp)).astype(F32)
    cut = mine.shape[0] // 2
    a, b = mine[:cut], mine[cut:]
    a, b = halve(a, turn_batch, x_bit), halve(b, turn_high, y_bit)
    a, b = halve(a, turn_high, y_bit), halve(b, turn_batch, x_bit)
    a, b = join(a, turn_high, y_bit), join(b, turn_batch, x_bit)
    a, b = join(a, turn_batch, x_bit), join(b, turn_high, y_bit)
    full = jnp.concatenate([a, b], axis=0)
    other = turn_low(full)
    return jnp.where(core, other, full).astype(F32), jnp.where(core, full, other).astype(F32)


def reduce_attn(own, partner):
    batch = lax.axis_index("batch")
    wide = lax.axis_index("wide")
    size = lax.axis_size("wide")
    own = own + turn_high(partner.astype(BF)).astype(F32)
    rows, width = own.shape
    mine = halve(own, turn_batch, batch)
    blocks = mine.reshape(size, -1, width)
    if size <= DIRECT:
        pick = lambda s: lax.dynamic_index_in_dim(blocks, (wide - s) % size, 0, keepdims=False)
        arrived = [shift(pick(s).astype(BF), -s) for s in range(1, size)]
        total = pick(0)
        for piece in arrived:
            total = total + piece.astype(F32)
        total = total.astype(BF)
        full = jnp.zeros(blocks.shape, BF)
        for s in range(size):
            piece = shift(total, s) if s else total
            full = lax.dynamic_update_index_in_dim(full, piece, (wide - s) % size, 0)
    else:
        total = lax.psum_scatter(blocks.astype(BF), "wide", scatter_dimension=0, tiled=False)
        full = lax.all_gather(total, "wide", axis=0, tiled=False)
    return join(full.reshape(rows // 2, width), turn_batch, batch).astype(F32)


def sum_all(x):
    x = x + turn_low(x)
    x = x + turn_high(x)
    x = x + turn_batch(x)
    size = lax.axis_size("wide")
    if size > DIRECT:
        return lax.psum(x, "wide")
    total = x
    for s in range(1, size):
        total = total + shift(x, s)
    return total


def general(tokens, patches, w_qkv, w_att, w_in, w_mlp, gains, cotangent):
    rows_all, slots, width = tokens.shape
    wide = lax.axis_size("wide")
    place = lax.axis_index("head")
    wide_place = lax.axis_index("wide")
    levels = w_qkv.shape[0]
    group = w_att.shape[1]
    n = rows_all * slots // 4
    rows = rows_all // 2

    def assemble(own, other, count):
        if rows == 1:
            return jnp.concatenate([own, other], axis=0)[None]
        half = rows // 2
        def turn(v):
            v = v.reshape(count, half, slots, *v.shape[1:])
            return jnp.moveaxis(v, 1, 0).reshape(half, count * slots, *v.shape[3:])
        return jnp.concatenate([turn(own), turn(other)], axis=0)

    def take_apart(v, count):
        if rows == 1:
            return v[0, : count * n], v[0, count * n :]
        half = rows // 2
        def turn(u):
            u = u.reshape(half, count, slots, *u.shape[2:])
            return jnp.moveaxis(u, 1, 0).reshape(count * n, *u.shape[3:])
        return turn(v[:half]), turn(v[half:])

    ends = jnp.cumsum(patches, axis=1)
    slot_index = jnp.arange(slots * wide, dtype=jnp.int32)
    image = jnp.sum((slot_index[None, :, None] >= ends[:, None, :]).astype(jnp.int32), axis=2)
    image = jnp.where(slot_index[None, :] < ends[:, -1:], image, -1)
    image = image.reshape(rows_all, wide, slots).transpose(1, 0, 2).reshape(wide, 4, n)
    order = (wide_place - jnp.arange(wide)) % wide
    image = image[order]
    own_image = lax.dynamic_index_in_dim(image, place, 1, keepdims=False)
    other_image = lax.dynamic_index_in_dim(image, place ^ 1, 1, keepdims=False)
    key_image = assemble(own_image.reshape(-1), other_image.reshape(-1), wide)
    query_image = assemble(own_image[0], other_image[0], 1)
    key_id = key_image[:, None, :]
    query_id = jnp.where(query_image >= 0, query_image, -2)[:, :, None]

    own = lax.dynamic_index_in_dim(tokens.reshape(4, n, width), place, 0, keepdims=False)
    cot = lax.dynamic_index_in_dim(cotangent.reshape(4, n, width), place, 0, keepdims=False)
    cot_other = lax.dynamic_index_in_dim(cotangent.reshape(4, n, width), place ^ 1, 0, keepdims=False)

    project = lambda act, w: jnp.einsum("rse,ce->rsc", act, w, preferred_element_type=F32).astype(BF)
    pull_back = lambda d, w: jnp.einsum("rkc,ce->rke", d, w, preferred_element_type=F32)
    weigh = lambda d, act: jnp.einsum("rqc,rqe->ce", d, act, preferred_element_type=F32)

    qkv_ws = [swap(w_qkv[l], 2) for l in range(levels)]
    att_ws = [swap(w_att[l], 2) for l in range(levels)]

    def weights(l, qkv_part, att_part):
        return jnp.concatenate([w_qkv[l], qkv_part], axis=1), jnp.concatenate([w_att[l], att_part], axis=0)

    def branch_of(attended, att_w):
        att_own, att_other = take_apart(
            jnp.einsum("rqc,ce->rqe", attended, att_w, preferred_element_type=F32), 1
        )
        return att_own + turn_low(att_other.astype(BF)).astype(F32)

    def act_terms(dq, dk, dv, qkv_w):
        d_act_kv = pull_back(dk, qkv_w[1]) + pull_back(dv, qkv_w[2])
        kv_own, kv_other = take_apart(d_act_kv, wide)
        q_own, q_other = take_apart(pull_back(dq, qkv_w[0]), 1)
        kv_other = kv_other.at[:n].add(q_other).astype(BF)
        return kv_own.at[:n].add(q_own) + turn_low(kv_other).astype(F32)

    def ff_back(pre, ff_grad, l):
        d_hidden = right_dot(ff_grad, w_mlp[l])
        unused, pull = jax.vjp(jax.nn.gelu, pre)
        return pull(d_hidden)[0].astype(BF)

    stream = own.astype(F32)
    saved = []
    for l in range(levels - 1):
        xhat, rstd = norm_parts(stream)
        act = (xhat * gains[l]).astype(BF)
        ff_act = gather_wide(act)
        other_act = turn_low(ff_act)
        pre = right_dot(ff_act, w_in[l])
        hidden = jax.nn.gelu(pre).astype(BF)
        parts = plain_dot(hidden, w_mlp[l])
        parts, ff_act, other_act = tie(parts, ff_act, other_act)
        branch = scatter_wide(parts)
        qkv_w, att_w = weights(l, qkv_ws[l], att_ws[l])
        key_act = assemble(ff_act, other_act, wide)
        query_act = assemble(act, other_act[:n], 1)
        q, k, v = project(query_act, qkv_w[0]), project(key_act, qkv_w[1]), project(key_act, qkv_w[2])
        attended, stats = attend(q, k, v, query_id, key_id)
        branch = branch + branch_of(attended, att_w)
        branch, qkv_ws[l + 1], att_ws[l + 1] = tie(branch, qkv_ws[l + 1], att_ws[l + 1])
        saved.append((xhat, rstd, ff_act, key_act, query_act, qkv_w, att_w, pre, hidden, q, k, v, attended, stats))
        stream = stream + branch

    l = levels - 1
    xhat, rstd = norm_parts(stream)
    act = (xhat * gains[l]).astype(BF)
    qkv_w, att_w = weights(l, qkv_ws[l], att_ws[l])
    query_grad = assemble(cot, cot_other, 1)
    d_attended = project(query_grad, att_w)
    ff_act = gather_wide(act)
    ff_act, cot, d_attended = tie(ff_act, cot, d_attended)
    ff_grad = gather_wide(cot)
    other_act = turn_low(ff_act)
    pre = right_dot(ff_act, w_in[l])
    hidden = jax.nn.gelu(pre).astype(BF)
    key_act = assemble(ff_act, other_act, wide)
    query_act = assemble(act, other_act[:n], 1)
    q, k, v = project(query_act, qkv_w[0]), project(key_act, qkv_w[1]), project(key_act, qkv_w[2])
    attended, dq, dk, dv = attend_back(q, k, v, d_attended, query_id, key_id)
    terms = act_terms(dq, dk, dv, qkv_w)
    d_pre = ff_back(pre, ff_grad, l)
    parts = terms + plain_dot(d_pre, w_in[l])
    parts, hidden, d_pre, dq, dk, dv, attended = tie(parts, hidden, d_pre, dq, dk, dv, attended)
    d_act = scatter_wide(parts)
    pieces = [weigh(dq, query_act), weigh(dk, key_act), weigh(dv, key_act), weigh(attended, query_grad)]
    last_attn = jnp.concatenate([t[:group] for t in pieces]) + turn_high(
        jnp.concatenate([t[group:] for t in pieces]).astype(BF)
    ).astype(F32)
    last_ff = jnp.concatenate([trans_dot(d_pre, ff_act), trans_dot(hidden, ff_grad)]).astype(BF)
    last_branch = branch_of(attended, att_w)
    last_parts = plain_dot(hidden, w_mlp[l])
    d_act, last_parts, last_attn, last_ff = tie(d_act, last_parts, last_attn, last_ff)
    gain_last = jnp.sum(d_act * xhat, axis=0)
    grad = cot.astype(F32) + norm_back(d_act, xhat, rstd, gains[l])
    last_attn = lax.psum(last_attn.astype(BF), ("batch", "wide"))
    last_ff = lax.psum(last_ff, ("batch", "head"))

    assert levels == 2
    l = 0
    xhat, rstd, ff_act, key_act, query_act, qkv_w, att_w, pre, hidden, q, k, v, attended, stats = saved[0]
    low = grad.astype(BF)
    other_low = turn_low(low)
    ff_grad = gather_wide(low)
    query_grad = assemble(low, other_low, 1)
    d_attended = project(query_grad, att_w)
    dq, dk, dv = attend_back(q, k, v, d_attended, query_id, key_id, stats)
    terms = act_terms(dq, dk, dv, qkv_w)
    piece_o, piece_v = weigh(attended, query_grad), weigh(dv, key_act)
    piece_q, piece_k = weigh(dq, query_act), weigh(dk, key_act)
    first_ov = reduce_attn(
        jnp.concatenate([piece_o[:group], piece_v[:group]]), jnp.concatenate([piece_o[group:], piece_v[group:]])
    )
    first_qk = reduce_attn(
        jnp.concatenate([piece_q[:group], piece_k[:group]]), jnp.concatenate([piece_q[group:], piece_k[group:]])
    )
    d_pre = ff_back(pre, ff_grad, l)
    parts = terms + plain_dot(d_pre, w_in[l])
    parts, hidden, d_pre = tie(parts, hidden, d_pre)
    d_act = scatter_wide(parts)
    first_in, first_mlp = reduce_ff(trans_dot(d_pre, ff_act), trans_dot(hidden, ff_grad))
    d_act, last_parts = tie(d_act, last_parts)
    gain_first = jnp.sum(d_act * xhat, axis=0)
    grad = grad + norm_back(d_act, xhat, rstd, gains[l])
    delta = gather_head((grad - cot.astype(F32)).astype(BF))
    d_tokens = cotangent.astype(F32) + delta.reshape(tokens.shape).astype(F32)
    d_gains = sum_all(jnp.stack([gain_first, gain_last]))
    stream = stream + last_branch + scatter_wide(last_parts)
    delta = gather_head((stream - own.astype(F32)).astype(BF))
    out = tokens.astype(F32) + delta.reshape(tokens.shape).astype(F32)
    last_attn = last_attn.astype(F32).reshape(4, group, width)
    last_in, last_mlp = last_ff[: last_ff.shape[0] // 2].astype(F32), last_ff[last_ff.shape[0] // 2 :].astype(F32)
    d_qkv = jnp.stack([jnp.stack([first_qk[:group], first_qk[group:], first_ov[group:]]), last_attn[:3]])
    return (
        out,
        d_tokens,
        d_qkv,
        jnp.stack([first_ov[:group], last_attn[3]]),
        jnp.stack([first_in, last_in]),
        jnp.stack([first_mlp, last_mlp]),
        d_gains,
    )


COST = 2 * 10**10
LIMIT = 28
SMALL = 16
MIDDLE = 24
CORE, X_BIT, Y_BIT, WIDE, PLACE = range(5)


def full_spec(x):
    return pl.BlockSpec(x.shape, lambda i, *_, nd=x.ndim: (0,) * nd)


def layer_spec(x, l):
    return pl.BlockSpec((1, *x.shape[1:]), lambda i, *_, nd=x.ndim: (l,) + (0,) * (nd - 1))


def call(kernel, grid, ins, outs, scratch=(), prefetch=(), limit=SMALL, cost=COST):
    return pl.pallas_call(
        kernel,
        grid_spec=pltpu.PrefetchScalarGridSpec(
            num_scalar_prefetch=len(prefetch),
            grid=(grid,),
            in_specs=[spec for _, spec in ins],
            out_specs=[spec for _, _, spec in outs],
            scratch_shapes=list(scratch),
        ),
        out_shape=[jax.ShapeDtypeStruct(shape, kind) for shape, kind, _ in outs],
        cost_estimate=pl.CostEstimate(flops=cost, bytes_accessed=0, transcendentals=0),
        compiler_params=pltpu.CompilerParams(vmem_limit_bytes=limit * 2**20),
    )(*prefetch, *[x for x, _ in ins])


def far(x):
    return pltpu.with_memory_space_constraint(x, pltpu.HBM)


def whole_out(shape, kind):
    return (shape, kind, pl.BlockSpec(shape, lambda i, *_, nd=len(shape): (0,) * nd))


def total_of(refs):
    total = refs[0][...].astype(F32)
    for ref in refs[1:]:
        total = total + ref[...].astype(F32)
    return total


def start_norm_kernel(place_ref, tok_ref, gain_ref, act_ref):
    xhat, unused = norm_parts(tok_ref[...].astype(F32))
    act_ref[...] = (xhat * gain_ref[0]).astype(BF)


def start_norm(place, tokens, gains):
    n, width = tokens.shape
    return call(
        start_norm_kernel,
        1,
        [(tokens, full_spec(tokens)), (gains, layer_spec(gains, 0))],
        [whole_out((n, width), BF)],
        prefetch=(place,),
    )[0]


def norm_kernel(place_ref, tok_ref, gain_ref, *refs):
    stream_ref, act_ref = refs[-2:]
    stream = tok_ref[...].astype(F32) + total_of(refs[:-2])
    xhat, unused = norm_parts(stream)
    stream_ref[...] = stream
    act_ref[...] = (xhat * gain_ref[0]).astype(BF)


def norm(place, tokens, gains, l, terms):
    n, width = tokens.shape
    return call(
        norm_kernel,
        1,
        [(tokens, full_spec(tokens)), (gains, layer_spec(gains, l))]
        + [(t, full_spec(t)) for t in terms],
        [whole_out((n, width), F32), whole_out((n, width), BF)],
        prefetch=(place,),
    )


def norm_back_kernel(first, place_ref, cot_ref, gain_ref, stream_ref, *refs):
    *refs, delta_ref, low_ref, gain_out = refs
    if not first:
        earlier, *refs = refs
    d_act = total_of(refs)
    xhat, rstd = norm_parts(stream_ref[...].astype(F32))
    gain_out[...] = jnp.sum(d_act * xhat, axis=0, keepdims=True)
    delta = norm_back(d_act, xhat, rstd, gain_ref[0])
    if not first:
        delta = delta + earlier[...]
        low_ref[...] = delta.astype(BF)
    else:
        low_ref[...] = (cot_ref[...].astype(F32) + delta).astype(BF)
    delta_ref[...] = delta


def norm_back_call(place, cotangent, gains, l, stream, terms, earlier=None):
    n, width = cotangent.shape
    first = earlier is None
    return call(
        functools.partial(norm_back_kernel, first),
        1,
        [(cotangent, full_spec(cotangent)), (gains, layer_spec(gains, l)), (stream, full_spec(stream))]
        + ([] if first else [(earlier, full_spec(earlier))])
        + [(t, full_spec(t)) for t in terms],
        [whole_out((n, width), F32), whole_out((n, width), BF), whole_out((1, width), F32)],
        prefetch=(place,),
    )


GELU_A = 0.7978845608028654
GELU_B = 0.044715


def gelu_both(x):
    square = x * x
    t = jnp.tanh(GELU_A * (x + GELU_B * (square * x)))
    value = 0.5 * x * (1.0 + t)
    slope = 0.5 * (1.0 + t) + 0.5 * x * (1.0 - t * t) * (GELU_A * (1.0 + 3.0 * GELU_B * square))
    return value, slope


def chunks_of(total):
    step = 256 if total % 256 == 0 else total
    return [slice(i, i + step) for i in range(0, total, step)]


def write_parts(total, n, part_refs):
    for s, ref in enumerate(part_refs):
        ref[...] = total[s * n : (s + 1) * n].astype(ref.dtype)


def ff_kernel(count, spot_ref, *refs):
    x_refs, (in_ref, mlp_ref, slope_ref, hidden_ref, all_ref), part_refs = refs[:count], refs[count : count + 5], refs[count + 5 :]
    n = x_refs[0].shape[0]
    x = jnp.concatenate([r[...] for r in x_refs], axis=0)
    all_ref[...] = x
    total = None
    for cut in chunks_of(in_ref.shape[1]):
        value, slope = gelu_both(right_dot(x, in_ref[0, cut, :]))
        low = value.astype(BF)
        slope_ref[:, cut] = slope
        hidden_ref[:, cut] = low
        term = plain_dot(low, mlp_ref[0, cut, :])
        total = term if total is None else total + term
    if len(part_refs) == 1:
        for s in range(count):
            part_refs[0][lax.rem(spot_ref[WIDE] - s + count, count)] = total[s * n : (s + 1) * n].astype(BF)
    else:
        write_parts(total, n, part_refs)


def part_outs(count, n, width):
    return [whole_out((n, width), F32 if s == 0 else BF) for s in range(count)]


def ff(spot, xs, w_in, w_mlp, l, blocks=False):
    count, (n, width) = len(xs), xs[0].shape
    w_in, w_mlp = w_in[l], w_mlp[l]
    hidden = w_in.shape[1]
    slope, low, x_all, *parts = call(
        functools.partial(ff_kernel, count),
        1,
        [(x, full_spec(x)) for x in (*xs, w_in, w_mlp)],
        [whole_out((count * n, hidden), F32), whole_out((count * n, hidden), BF), whole_out((count * n, width), BF)]
        + ([whole_out((count, n, width), BF)] if blocks else part_outs(count, n, width)),
        prefetch=(spot,),
    )
    return slope, low, x_all, parts[0] if blocks else parts


def ff_slope_kernel(count, *refs):
    g_refs, (mlp_ref, slope_ref, d_pre_ref, all_ref) = refs[:count], refs[count:]
    g = jnp.concatenate([r[...] for r in g_refs], axis=0)
    all_ref[...] = g
    for cut in chunks_of(mlp_ref.shape[1]):
        d_pre_ref[:, cut] = (slope_ref[:, cut] * right_dot(g, mlp_ref[0, cut, :])).astype(BF)


def ff_slope(gs, w_mlp, l, slope):
    count, (n, width) = len(gs), gs[0].shape
    return call(
        functools.partial(ff_slope_kernel, count),
        1,
        [(g, full_spec(g)) for g in (*gs, w_mlp[l], slope)],
        [whole_out(slope.shape, BF), whole_out((count * n, width), BF)],
    )


def ff_back_kernel(n, d_pre_ref, in_ref, own_ref, got_ref, *part_refs):
    total = own_ref[...] + got_ref[...].astype(F32) + plain_dot(d_pre_ref[...], in_ref[0])
    write_parts(total, n, part_refs)


def ff_back(count, d_pre, w_in, l, own, got):
    n, width = d_pre.shape[0] // count, w_in[l].shape[2]
    return call(
        functools.partial(ff_back_kernel, n),
        1,
        [(x, full_spec(x)) for x in (d_pre, w_in[l], own, got)],
        part_outs(count, n, width),
    )


def ff_weights_kernel(outer, spot_ref, x_ref, g_ref, d_pre_ref, hidden_ref, keep_ref, send_ref):
    core = spot_ref[CORE] == 1
    d_in = trans_dot(d_pre_ref[...], x_ref[...])
    d_mlp = trans_dot(hidden_ref[...], g_ref[...])
    half = d_in.shape[0] // 2
    keep, send = jnp.where(core, d_mlp, d_in), jnp.where(core, d_in, d_mlp).astype(BF)
    for j in range(2):
        at = j ^ spot_ref[Y_BIT if outer == X_BIT else X_BIT]
        keep_ref[0, at] = keep[j * half : (j + 1) * half]
        send_ref[0, at] = send[j * half : (j + 1) * half]


def ff_weights(spot, xs, gs, d_pre, hidden, outer):
    width = xs.shape[1]
    tokens, size = d_pre.shape
    cut = pl.BlockSpec((tokens, size // 2), lambda i, p: (0, i))
    shape = (2, 2, size // 4, width)
    out = pl.BlockSpec((1, *shape[1:]), lambda i, p: (i ^ p[outer], 0, 0, 0))
    return call(
        functools.partial(ff_weights_kernel, outer),
        2,
        [(x, full_spec(x)) for x in (xs, gs)] + [(d_pre, cut), (hidden, cut)],
        [(shape, F32, out), (shape, BF, out)],
        prefetch=(spot,),
        cost=COST // 4,
    )


def ff_finish_kernel(spot_ref, *refs):
    *refs, in_ref, mlp_ref = refs
    core = spot_ref[CORE] == 1
    for l in range(2):
        mine, got = refs[2 * l][0].astype(F32), refs[2 * l + 1][0].astype(F32)
        in_ref[l] = jnp.where(core, got, mine)
        mlp_ref[l] = jnp.where(core, mine, got)


def ff_finish(spot, pairs, outers):
    unused, rows, width = pairs[0][0].shape
    ins = []
    for (mine, got), outer in zip(pairs, outers):
        inner = Y_BIT if outer == X_BIT else X_BIT
        spec = pl.BlockSpec((1, rows, width), lambda i, p, o=outer, n=inner: (i ^ (2 * p[o] + p[n]), 0, 0))
        ins += [(mine, spec), (got, spec)]
    out = ((2, 4 * rows, width), F32, pl.BlockSpec((2, rows, width), lambda i, p: (0, i, 0)))
    return call(ff_finish_kernel, 4, ins, [out, out], prefetch=(spot,))


def attn_kernel(mode, count, *refs):
    refs = list(refs)
    take = lambda k: [refs.pop(0) for _ in range(k)]
    if mode != "back":
        act_refs = take(2)
    if mode != "fwd":
        g_refs = take(2)
    w_own, a_own, p_qk, p_vo, qid_ref, kid_ref = take(6)
    if mode == "back":
        q_ref, k_ref, v_ref, stat_ref = take(4)
    step = pl.program_id(0)
    scale = HEAD_DIM ** (-0.5)
    n = qid_ref.shape[0] // 2
    half = count * n
    if mode == "fwd":
        q_out, k_out, v_out, o_out, stat_out, b_own, b_other, act_all, branch = refs
    elif mode == "both":
        q_out, k_out, v_out, o_out, t_own, t_other, b_own, b_other, act_all, branch, terms = refs
    else:
        q_out, k_out, v_out, t_own, t_other, terms = refs
    if mode != "back":

        @pl.when(step == 0)
        def _():
            act_all[:half, :] = act_refs[0][...]
            act_all[half:, :] = act_refs[1][...]

    w_kv = jnp.concatenate([w_own[0, 1], p_qk[1], w_own[0, 2], p_vo[0]], axis=0)
    w_q = jnp.concatenate([w_own[0, 0], p_qk[0]], axis=0)
    w_o = jnp.concatenate([a_own[0], p_vo[1]], axis=0)
    if mode != "back":
        kv = right_dot(act_all[...], w_kv).astype(BF)
        k, v = kv[:, :PAIR], kv[:, PAIR:]
        q_in = jnp.concatenate([act_refs[0][:n, :], act_refs[1][:n, :]], axis=0)
        q = right_dot(q_in, w_q).astype(BF)
    else:
        q, k, v = q_ref[...], k_ref[...], v_ref[...]
    if mode == "fwd":
        q_out[...], k_out[...], v_out[...] = q, k, v
    q = q * jnp.asarray(scale, BF)
    allowed = qid_ref[...] == kid_ref[...]
    if mode != "fwd":
        g = right_dot(jnp.concatenate([r[...] for r in g_refs], axis=0), w_o).astype(BF)
    lane = lax.broadcasted_iota(jnp.int32, (2 * n, PAIR), 1)
    stats = jnp.zeros((2 * n, PAIR), F32)
    outs, dqs, dks, dvs = [], [], [], []
    for j in range(2):
        cut = slice(j * HEAD_DIM, (j + 1) * HEAD_DIM)
        qj, kj, vj = q[:, cut], k[:, cut], v[:, cut]
        if mode == "back":
            top, inverse = stat_ref[0, :, 2 * j : 2 * j + 1], stat_ref[0, :, 2 * j + 1 : 2 * j + 2]
            probs = jnp.exp(jnp.where(allowed, right_dot(qj, kj), NEGATIVE) - top) * inverse
        else:
            probs, top, inverse = head_softmax(qj, kj, allowed)
            stats = jnp.where(lane == 2 * j, top, jnp.where(lane == 2 * j + 1, inverse, stats))
        low = probs.astype(BF)
        if mode != "back":
            outs.append(plain_dot(low, vj))
        if mode != "fwd":
            gj = g[:, cut]
            dp = right_dot(gj, vj)
            ds = (probs * (dp - jnp.sum(probs * dp, axis=-1, keepdims=True))).astype(BF)
            dqs.append(plain_dot(ds, kj) * scale)
            dks.append(trans_dot(ds, qj))
            dvs.append(trans_dot(low, gj))
    last = step == pl.num_programs(0) - 1
    if mode != "back":
        attended = jnp.concatenate(outs, axis=1).astype(BF)
        o_out[...] = attended
        term = plain_dot(attended, w_o)

        @pl.when(step == 0)
        def _():
            branch[...] = term

        @pl.when(step > 0)
        def _():
            branch[...] += term

        @pl.when(last)
        def _():
            b_own[...] = branch[:n, :]
            b_other[...] = branch[n:, :].astype(BF)

    if mode == "fwd":
        stat_out[0] = stats
    else:
        dq = jnp.concatenate(dqs, axis=1).astype(BF)
        dkv = jnp.concatenate(dks + dvs, axis=1).astype(BF)
        q_out[...], k_out[...], v_out[...] = dq, dkv[:, :PAIR], dkv[:, PAIR:]
        term_kv = plain_dot(dkv, w_kv)
        term_q = plain_dot(dq, w_q)

        @pl.when(step == 0)
        def _():
            terms[...] = term_kv

        @pl.when(step > 0)
        def _():
            terms[...] += term_kv

        terms[:n, :] += term_q[:n]
        terms[half : half + n, :] += term_q[n:]

        @pl.when(last)
        def _():
            t_own[...] = terms[:half, :]
            t_other[...] = terms[half:, :].astype(BF)


def attn(mode, count, l, w_qkv, w_att, part, qid, kid, acts=(), grads=(), kept=()):
    group, width = part.shape[1:]
    n = qid.shape[0] // 2
    tq, tk = 2 * n, 2 * count * n
    steps = group // HEAD_DIM
    pair_q = pl.BlockSpec((tq, PAIR), lambda i: (0, i))
    pair_k = pl.BlockSpec((tk, PAIR), lambda i: (0, i))
    stat = pl.BlockSpec((1, tq, PAIR), lambda i: (i, 0, 0))
    ins = [(x, full_spec(x)) for x in (*acts, *grads)] + [
        (w_qkv, pl.BlockSpec((1, 3, HEAD_DIM, width), lambda i: (l, 0, i, 0))),
        (w_att, pl.BlockSpec((1, HEAD_DIM, width), lambda i: (l, i, 0))),
        *[(part, pl.BlockSpec((2, HEAD_DIM, width), lambda i, h=h: (h, i, 0))) for h in range(2)],
        (qid, full_spec(qid)),
        (kid, full_spec(kid)),
    ]
    if mode == "back":
        q, k, v, stats = kept
        ins += [(far(q), pair_q), (far(k), pair_k), (far(v), pair_k), (far(stats), stat)]
    q_shape, k_shape = (tq, 2 * group), (tk, 2 * group)
    outs = [(q_shape, BF, pair_q), (k_shape, BF, pair_k), (k_shape, BF, pair_k)]
    scratch = []
    if mode != "back":
        outs += [(q_shape, BF, pair_q)]
        scratch += [pltpu.VMEM((tk, width), BF), pltpu.VMEM((tq, width), F32)]
    if mode == "fwd":
        outs += [((steps, tq, PAIR), F32, stat)]
    else:
        outs += [whole_out((tk // 2, width), F32), whole_out((tk // 2, width), BF)]
        scratch += [pltpu.VMEM((tk, width), F32)]
    if mode != "back":
        outs += [whole_out((n, width), F32), whole_out((n, width), BF)]
    return call(functools.partial(attn_kernel, mode, count), steps, ins, outs, scratch, limit=LIMIT)


def attn_weights_kernel(spot_ref, own_act, other_act, g_own, g_other, dq_ref, dk_ref, dv_ref, o_ref, own_ref, part_ref, act_all):
    n = g_own.shape[0]
    half = act_all.shape[0] // 2
    step = pl.program_id(0)

    @pl.when(step == 0)
    def _():
        act_all[:half, :] = own_act[...]
        act_all[half:, :] = other_act[...]

    q_in = jnp.concatenate([own_act[:n, :], other_act[:n, :]], axis=0)
    g_in = jnp.concatenate([g_own[...], g_other[...]], axis=0)
    kv = trans_dot(jnp.concatenate([dk_ref[...], dv_ref[...]], axis=1), act_all[...])
    pairs = (trans_dot(dq_ref[...], q_in), kv[:PAIR], kv[PAIR:], trans_dot(o_ref[...], g_in))
    rows = own_ref.shape[2]
    for i in range(2 * rows // HEAD_DIM):

        @pl.when(step == i)
        def _():
            for t, pair in enumerate(pairs):
                back = lax.rem(spot_ref[WIDE] - t + 4, 4)
                low = i * HEAD_DIM
                while low < (i + 1) * HEAD_DIM:
                    high = min((i + 1) * HEAD_DIM, (low // rows + 1) * rows)
                    at = (low // rows) ^ spot_ref[X_BIT]
                    dest = slice(low % rows, low % rows + high - low)
                    source = slice(low - i * HEAD_DIM, high - i * HEAD_DIM)
                    own_ref[at, back, dest, :] = pair[:HEAD_DIM][source]
                    part_ref[at, back, dest, :] = pair[HEAD_DIM:][source].astype(BF)
                    low = high


def attn_weights(spot, acts, grads, dq, dk, dv, attended):
    n, width = grads[0].shape
    tq, tk, group = 2 * n, 2 * acts[0].shape[0], dq.shape[1] // 2
    pair_q = pl.BlockSpec((tq, PAIR), lambda i, p: (0, i))
    pair_k = pl.BlockSpec((tk, PAIR), lambda i, p: (0, i))
    shape = (2, 4, group // 2, width)
    return call(
        attn_weights_kernel,
        group // HEAD_DIM,
        [(x, full_spec(x)) for x in (*acts, *grads)] + [(dq, pair_q), (dk, pair_k), (dv, pair_k), (attended, pair_q)],
        [whole_out(shape, F32), whole_out(shape, BF)],
        [pltpu.VMEM((tk, width), BF)],
        (spot,),
        limit=MIDDLE,
        cost=COST // 4,
    )


def attn_finish_kernel(spot_ref, *refs):
    *refs, qkv_ref, att_ref = refs
    matrix = pl.program_id(0)
    second = spot_ref[X_BIT] == 1
    for l in range(2):
        mine, got = refs[2 * l][0].astype(F32), refs[2 * l + 1][0].astype(F32)
        whole = jnp.concatenate([jnp.where(second, got, mine), jnp.where(second, mine, got)], axis=0)

        @pl.when(matrix < 3)
        def _():
            qkv_ref[l, 0] = whole

        @pl.when(matrix == 3)
        def _():
            att_ref[l] = whole


def attn_finish(spot, pairs):
    unused, rows, width = pairs[0][0].shape
    spec = pl.BlockSpec((1, rows, width), lambda i, p: (lax.rem(p[WIDE] - i + 4, 4), 0, 0))
    return call(
        attn_finish_kernel,
        4,
        [(x, spec) for pair in pairs for x in pair],
        [
            ((2, 3, 2 * rows, width), F32, pl.BlockSpec((2, 1, 2 * rows, width), lambda i, p: (0, jnp.minimum(i, 2), 0, 0))),
            whole_out((2, 2 * rows, width), F32),
        ],
        prefetch=(spot,),
    )


def gather_list(x):
    return [x] + [shift(x, s) for s in range(1, lax.axis_size("wide"))]


def return_list(parts):
    return [parts[0]] + [shift(p, -s) for s, p in enumerate(parts) if s]


def reduce_ff_rest(keep, got):
    x_bit, y_bit = lax.axis_index("batch"), lax.axis_index("head") >> 1
    core = (lax.axis_index("head") & 1) == 1
    mine = keep + got.astype(F32)
    cut = mine.shape[0] // 2
    a, b = mine[:cut], mine[cut:]
    a, b = halve(a, turn_batch, x_bit), halve(b, turn_high, y_bit)
    a, b = halve(a, turn_high, y_bit), halve(b, turn_batch, x_bit)
    a, b = join(a, turn_high, y_bit), join(b, turn_batch, x_bit)
    a, b = join(a, turn_batch, x_bit), join(b, turn_high, y_bit)
    full = jnp.concatenate([a, b], axis=0)
    other = turn_low(full)
    return jnp.where(core, other, full), jnp.where(core, full, other)


def together(*pairs):
    sent = tie(*[x for x, _ in pairs])
    return tie(*[f(x) for x, (_, f) in zip(sent, pairs)])


def half_of(x, bit):
    halves = x.reshape(2, x.shape[0] // 2, x.shape[1])
    return (
        lax.dynamic_index_in_dim(halves, bit, 0, keepdims=False),
        lax.dynamic_index_in_dim(halves, 1 - bit, 0, keepdims=False).astype(BF),
    )


def shifts(sign):
    return [functools.partial(shift, step=sign * s) for s in range(1, lax.axis_size("wide"))]


def blocks_of(x):
    wide, size = lax.axis_index("wide"), lax.axis_size("wide")
    blocks = x.reshape(size, -1, x.shape[1])
    own, *others = [lax.dynamic_index_in_dim(blocks, (wide - s) % size, 0, keepdims=False) for s in range(size)]
    return own, [o.astype(BF) for o in others]


def laid(pieces):
    wide, size = lax.axis_index("wide"), lax.axis_size("wide")
    full = jnp.zeros((size, *pieces[0].shape), pieces[0].dtype)
    for s, piece in enumerate(pieces):
        full = lax.dynamic_update_index_in_dim(full, piece, (wide - s) % size, 0)
    return full.reshape(-1, pieces[0].shape[1])


def ordered(mine, other, bit):
    return jnp.where(bit == 0, mine, other), jnp.where(bit == 0, other, mine)


def sum_of(first, pieces):
    total = first.astype(F32)
    for piece in pieces:
        total = total + piece.astype(F32)
    return total


def fast(tokens, patches, w_qkv, w_att, w_in, w_mlp, gains, cotangent):
    rows_all, slots, width = tokens.shape
    shape = tokens.shape
    wide = lax.axis_size("wide")
    head_place, wide_place = lax.axis_index("head"), lax.axis_index("wide")
    x_bit, y_bit, core = lax.axis_index("batch"), head_place >> 1, head_place & 1
    spot = jnp.stack([core, x_bit, y_bit, wide_place, head_place]).astype(jnp.int32)
    group = w_att.shape[1]
    n = rows_all * slots // 4
    tokens, cotangent = tokens.reshape(4, n, width), cotangent.reshape(4, n, width)
    gains = gains[:, None, :]
    w_in, w_mlp = [w_in[l : l + 1] for l in range(2)], [w_mlp[l : l + 1] for l in range(2)]

    own_ws = [jnp.concatenate([w_qkv[l], w_att[l][None]]) for l in range(2)]
    tok = lax.dynamic_index_in_dim(tokens, head_place, 0, keepdims=False)
    act = start_norm(spot, tok, gains)
    xs = gather_list(act)
    part0 = turn_high(own_ws[0])

    ends = jnp.cumsum(patches, axis=1)
    slot_index = jnp.arange(slots * wide, dtype=jnp.int32)
    image = jnp.sum((slot_index[None, :, None] >= ends[:, None, :]).astype(jnp.int32), axis=2)
    image = jnp.where(slot_index[None, :] < ends[:, -1:], image, -1)
    image = image.reshape(rows_all, wide, slots).transpose(1, 0, 2).reshape(wide, 4, n)
    order = (wide_place - jnp.arange(wide)) % wide
    image = image[order]
    own_image = lax.dynamic_index_in_dim(image, head_place, 1, keepdims=False)
    other_image = lax.dynamic_index_in_dim(image, head_place ^ 1, 1, keepdims=False)
    kid = jnp.concatenate([own_image.reshape(-1), other_image.reshape(-1)])[None, :]
    qid = jnp.concatenate([own_image[0], other_image[0]])
    qid = jnp.where(qid >= 0, qid, -2)[:, None]
    cot = lax.dynamic_index_in_dim(cotangent, head_place, 0, keepdims=False)
    cot_other = lax.dynamic_index_in_dim(cotangent, head_place ^ 1, 0, keepdims=False)

    xs[1], kid, qid, own_ws[1], cot, cot_other = tie(xs[1], kid, qid, own_ws[1], cot, cot_other)

    slope0, hidden0, own0, parts = ff(spot, xs, w_in, w_mlp, 0)
    terms = return_list(parts)
    acts0 = (own0, turn_low(own0))
    part0, next_w = tie(part0, own_ws[1])
    part1 = turn_high(next_w)
    q, k, v, attended0, stats, b_own, b_other = attn("fwd", wide, 0, w_qkv, w_att, part0, qid, kid, acts=acts0)
    b_got = turn_low(b_other)
    stream1, act = norm(spot, tok, gains, 1, [*terms, b_own, b_got])

    xs1 = gather_list(act)
    slope1, hidden1, own1, out_parts = ff(spot, xs1, w_in, w_mlp, 1, True)
    other1 = turn_low(own1)
    cot_tied, unused = tie(cot, own1)
    gs1 = gather_list(cot_tied)
    dq1, dk1, dv1, attended1, t_own, t_other, b_own1, b_other1 = attn(
        "both", wide, 1, w_qkv, w_att, part1, qid, kid, acts=(own1, other1), grads=(cot, cot_other)
    )
    t_got = turn_low(t_other)
    d_pre1, g_all1 = ff_slope(gs1, w_mlp, 1, slope1)
    parts = list(ff_back(wide, d_pre1, w_in, 1, t_own, t_got))
    parts[1], dq1, hidden1, b_other1 = tie(parts[1], dq1, hidden1, b_other1)
    back1 = return_list(parts)
    own_w1, part_w1 = attn_weights(spot, (own1, other1), (cot, cot_other), dq1, dk1, dv1, attended1)
    keep_f1, send_f1 = ff_weights(spot, own1, g_all1, d_pre1, hidden1, X_BIT)
    b_got1 = turn_low(b_other1)
    back1[1], b_got1, send_f1, keep_f1, own_w1, part_w1 = tie(back1[1], b_got1, send_f1, keep_f1, own_w1, part_w1)
    got_f1 = turn_low(send_f1)
    got_w1 = turn_high(part_w1)
    delta1, low, gain1 = norm_back_call(spot, cot, gains, 1, stream1, back1)

    low_other = turn_low(low)
    gs = gather_list(low)
    dq, dk, dv, t_own, t_other = attn(
        "back", wide, 0, w_qkv, w_att, part0, qid, kid, grads=(low, low_other), kept=(q, k, v, stats)
    )
    t_got = turn_low(t_other)
    own_w0, part_w0 = attn_weights(spot, acts0, (low, low_other), dq, dk, dv, attended0)
    got_f1, part_w0, own_w0 = tie(got_f1, part_w0, own_w0)
    got_x1 = turn_batch((keep_f1[1] + got_f1[1].astype(F32)).astype(BF))
    got_w0 = turn_high(part_w0)
    gs[1], own_w0, part_w0 = tie(gs[1], own_w0, part_w0)
    d_pre0, g_all0 = ff_slope(gs, w_mlp, 0, slope0)
    parts = list(ff_back(wide, d_pre0, w_in, 0, t_own, t_got))
    parts[1], hidden0 = tie(parts[1], hidden0)
    back0 = return_list(parts)
    keep_f0, send_f0 = ff_weights(spot, own0, g_all0, d_pre0, hidden0, Y_BIT)
    got_w1, got_x1, keep_f0 = tie(got_w1, got_x1, keep_f0)
    sum_w1 = own_w1 + got_w1.astype(F32)
    got_w1 = turn_batch(sum_w1[1].astype(BF))
    back0[1], keep_f0, send_f0 = tie(back0[1], keep_f0, send_f0)
    half_w1 = sum_w1[0] + got_w1.astype(F32)
    half_f1 = sum_of(keep_f1[0], [got_f1[0], got_x1])
    delta0, low0, gain0 = norm_back_call(spot, cot, gains, 0, tok, back0, delta1)

    last = lax.psum_scatter(out_parts, "wide", scatter_dimension=0, tiled=False)
    b_got1, last, stream1, low0 = tie(b_got1, last, stream1, low0)
    half_w1, half_f1, last = tie(half_w1, half_f1, last)
    delta_out = (stream1 - tok.astype(F32) + sum_of(b_own1, [b_got1, last])).astype(BF)
    ends = lax.all_gather(jnp.concatenate([delta_out, low0], axis=1), "head", axis=0, tiled=False)

    gain = jnp.concatenate([gain0, gain1, jnp.zeros((6, width), F32)])

    def with_gain(x, gain):
        high = gain.astype(BF)
        return jnp.concatenate([x.reshape(-1, width).astype(BF), high, (gain - high.astype(F32)).astype(BF)])

    def gain_of(got):
        return got[-16:-8].astype(F32) + got[-8:].astype(F32)

    got_w0, half_w1, half_f1 = tie(got_w0, half_w1, half_f1)
    sum_w0 = own_w0 + got_w0.astype(F32)
    got_w0, got_f0, *got_b1 = together(
        (sum_w0[1].astype(BF), turn_batch),
        (send_f0, turn_low),
        *[(half_w1[s + 1].astype(BF), f) for s, f in enumerate(shifts(-1))],
    )
    block_w1 = sum_of(half_w1[0], got_b1).astype(BF)
    half_w0 = sum_w0[0] + got_w0.astype(F32)
    sum_f0 = keep_f0 + got_f0.astype(F32)
    rows_f = sum_f0.shape[2]
    got_f0, got_f1, *got_b0 = together(
        (with_gain(sum_f0[1], gain), turn_high),
        (half_f1[1].astype(BF), turn_high),
        *[(half_w0[s + 1].astype(BF), f) for s, f in enumerate(shifts(-1))],
    )
    gain = gain + gain_of(got_f0)
    block_w0 = sum_of(half_w0[0], got_b0)
    half_f0 = sum_f0[0] + got_f0[: 2 * rows_f].reshape(2, rows_f, width).astype(F32)
    block_f1 = (half_f1[0] + got_f1.astype(F32)).astype(BF)
    got_f0, got_f1, *got_b1 = together(
        (with_gain(half_f0[1], gain), turn_batch), (block_f1, turn_batch), *[(block_w1, f) for f in shifts(1)]
    )
    gain = gain + gain_of(got_f0)
    block_f0 = (half_f0[0] + got_f0[:rows_f].astype(F32)).astype(BF)
    pair_f1 = jnp.stack([block_f1, got_f1])
    mine_w1 = jnp.stack([block_w1, *got_b1])
    block_w0 = with_gain(block_w0, gain)
    got_f0, got_f1, *got_b0 = together(
        (block_f0, turn_batch), (pair_f1, turn_high), *[(block_w0, f) for f in shifts(1)]
    )
    gain = sum_of(gain, [gain_of(g) for g in got_b0])
    pair_f0 = jnp.stack([block_f0, got_f0])
    full_f1 = jnp.stack([pair_f1, got_f1], axis=1).reshape(4, rows_f, width)
    rows_w = half_w0.shape[1]
    mine_w0 = jnp.stack([g[:rows_w] for g in (block_w0, *got_b0)])
    mine_w0, ends = tie(mine_w0, ends)
    got_w0, got_w1, got_f0, got_g, got_f1 = together(
        (mine_w0, turn_batch), (mine_w1, turn_batch), (pair_f0, turn_high), (gain, turn_low), (full_f1, turn_low)
    )
    full_f0 = jnp.concatenate([pair_f0, got_f0])
    got_f0 = turn_low(full_f0)
    d_gains = (gain + got_g)[:2]
    d_in, d_mlp = ff_finish(spot, ((full_f0, got_f0), (full_f1, got_f1)), (Y_BIT, X_BIT))
    out = tokens.astype(F32) + ends[:, :, :width].astype(F32)
    d_tokens = cotangent.astype(F32) + ends[:, :, width:].astype(F32)
    d_qkv, d_att = attn_finish(spot, ((mine_w0, got_w0), (mine_w1, got_w1)))
    return (out.reshape(shape), d_tokens.reshape(shape), d_qkv, d_att, d_in, d_mlp, d_gains)


def solution(mesh):
    def local(*arrays):
        tokens, w_qkv = arrays[0], arrays[2]
        small = tokens.shape[0] == 2 and lax.axis_size("wide") == 4 and w_qkv.shape[0] == 2
        return (fast if small else general)(*arrays)

    return jax.shard_map(
        local,
        mesh=mesh,
        in_specs=(
            P("batch", "wide", None),
            P("batch", None),
            P(None, None, "head", None),
            P(None, "head", None),
            P(None, "wide", None),
            P(None, "wide", None),
            P(),
            P("batch", "wide", None),
        ),
        out_specs=(
            P("batch", "wide", None),
            P("batch", "wide", None),
            P(None, None, "head", None),
            P(None, "head", None),
            P(None, "wide", None),
            P(None, "wide", None),
            P(),
        ),
        check_vma=False,
    )
```

```python
import functools

import jax
import jax.numpy as jnp
from jax import lax
from jax.experimental import pallas as pl
from jax.experimental.pallas import tpu as pltpu
from jax.sharding import PartitionSpec as P

HEAD_DIM = 64
EPS = 1e-06
NEGATIVE = -1e30
BF = jnp.bfloat16
F32 = jnp.float32
DIRECT = 8


def norm_parts(stream):
    centre = jnp.mean(stream, axis=-1, keepdims=True)
    centred = stream - centre
    spread = jnp.mean(centred * centred, axis=-1, keepdims=True)
    rstd = lax.rsqrt(spread + EPS)
    return centred * rstd, rstd


def norm_back(d_act, xhat, rstd, gain_row):
    dxh = d_act * gain_row
    m1 = jnp.mean(dxh, axis=-1, keepdims=True)
    m2 = jnp.mean(dxh * xhat, axis=-1, keepdims=True)
    return (dxh - m1 - xhat * m2) * rstd


def trans_dot(left, right):
    return lax.dot_general(left, right, (((0,), (0,)), ((), ())), preferred_element_type=F32)


def right_dot(left, right):
    return lax.dot_general(left, right, (((1,), (1,)), ((), ())), preferred_element_type=F32)


def plain_dot(left, right):
    return jnp.dot(left, right, preferred_element_type=F32)


def swap(x, bit):
    size = lax.axis_size("head")
    return lax.ppermute(x, "head", [(i, i ^ bit) for i in range(size)])


def shift(x, step):
    size = lax.axis_size("wide")
    return lax.ppermute(x, "wide", [(i, (i + step) % size) for i in range(size)])


def gather_wide(x):
    size = lax.axis_size("wide")
    if size <= DIRECT:
        return jnp.concatenate([x] + [shift(x, s) for s in range(1, size)], axis=0)
    whole = lax.all_gather(x, "wide", axis=0, tiled=False)
    order = (lax.axis_index("wide") - jnp.arange(size)) % size
    return whole[order].reshape(size * x.shape[0], *x.shape[1:])


def scatter_wide(parts):
    size = lax.axis_size("wide")
    rows = parts.shape[0] // size
    if size <= DIRECT:
        total = parts[:rows]
        low = [shift(parts[s * rows : (s + 1) * rows].astype(BF), -s) for s in range(1, size)]
        for piece in low:
            total = total + piece.astype(F32)
        return total
    order = (lax.axis_index("wide") - jnp.arange(size)) % size
    blocks = parts.astype(BF).reshape(size, rows, -1)[order]
    return lax.psum_scatter(blocks, "wide", scatter_dimension=0, tiled=False).astype(F32)


def gather_head(x):
    place = lax.axis_index("head")
    a = x
    b = swap(x, 2)
    c = swap(a, 1)
    d = swap(b, 1)
    low_bit = (place & 1) == 1
    high_bit = (place & 2) == 2
    a, c = jnp.where(low_bit, c, a), jnp.where(low_bit, a, c)
    b, d = jnp.where(low_bit, d, b), jnp.where(low_bit, b, d)
    a, b = jnp.where(high_bit, b, a), jnp.where(high_bit, a, b)
    c, d = jnp.where(high_bit, d, c), jnp.where(high_bit, c, d)
    return jnp.stack([a, c, b, d])


PAIR = 2 * HEAD_DIM
FLOOR = -1e29


def head_softmax(q, k, allowed):
    s = jnp.where(allowed, right_dot(q, k), NEGATIVE)
    top = jnp.maximum(jnp.max(s, axis=-1, keepdims=True), FLOOR)
    expo = jnp.exp(s - top)
    inverse = 1.0 / jnp.maximum(jnp.sum(expo, axis=-1, keepdims=True), 1.0)
    return expo * inverse, top, inverse


def attend_kernel(q_ref, k_ref, v_ref, qid_ref, kid_ref, o_ref, stat_ref):
    allowed = qid_ref[0] == kid_ref[0]
    q = q_ref[0] * jnp.asarray(HEAD_DIM ** (-0.5), BF)
    k, v = k_ref[0], v_ref[0]
    lane = lax.broadcasted_iota(jnp.int32, (q.shape[0], PAIR), 1)
    stats = jnp.zeros((q.shape[0], PAIR), F32)
    outs = []
    for j in range(2):
        cut = slice(j * HEAD_DIM, (j + 1) * HEAD_DIM)
        probs, top, inverse = head_softmax(q[:, cut], k[:, cut], allowed)
        outs.append(plain_dot(probs.astype(BF), v[:, cut]))
        stats = jnp.where(lane == 2 * j, top, jnp.where(lane == 2 * j + 1, inverse, stats))
    o_ref[0] = jnp.concatenate(outs, axis=1).astype(BF)
    stat_ref[0, 0] = stats


def attend_back_kernel(saved, q_ref, k_ref, v_ref, g_ref, qid_ref, kid_ref, *refs):
    if saved:
        stat_ref, dq_ref, dk_ref, dv_ref = refs
    else:
        o_ref, dq_ref, dk_ref, dv_ref = refs
    allowed = qid_ref[0] == kid_ref[0]
    scale = HEAD_DIM ** (-0.5)
    q = q_ref[0] * jnp.asarray(scale, BF)
    k, v, g = k_ref[0], v_ref[0], g_ref[0]
    outs, dqs, dks, dvs = [], [], [], []
    for j in range(2):
        cut = slice(j * HEAD_DIM, (j + 1) * HEAD_DIM)
        qj, kj, vj, gj = q[:, cut], k[:, cut], v[:, cut], g[:, cut]
        if saved:
            top = stat_ref[0, 0, :, 2 * j : 2 * j + 1]
            inverse = stat_ref[0, 0, :, 2 * j + 1 : 2 * j + 2]
            probs = jnp.exp(jnp.where(allowed, right_dot(qj, kj), NEGATIVE) - top) * inverse
        else:
            probs, top, inverse = head_softmax(qj, kj, allowed)
        low = probs.astype(BF)
        if not saved:
            outs.append(plain_dot(low, vj))
        dp = right_dot(gj, vj)
        ds = (probs * (dp - jnp.sum(probs * dp, axis=-1, keepdims=True))).astype(BF)
        dqs.append(plain_dot(ds, kj) * scale)
        dks.append(trans_dot(ds, qj))
        dvs.append(trans_dot(low, gj))
    if not saved:
        o_ref[0] = jnp.concatenate(outs, axis=1).astype(BF)
    dq_ref[0] = jnp.concatenate(dqs, axis=1).astype(BF)
    dk_ref[0] = jnp.concatenate(dks, axis=1).astype(BF)
    dv_ref[0] = jnp.concatenate(dvs, axis=1).astype(BF)


def attend_specs(q, k):
    rows, tq, width = q.shape
    tk = k.shape[1]
    q_spec = pl.BlockSpec((1, tq, PAIR), lambda r, j: (r, 0, j))
    k_spec = pl.BlockSpec((1, tk, PAIR), lambda r, j: (r, 0, j))
    qid_spec = pl.BlockSpec((1, tq, 1), lambda r, j: (r, 0, 0))
    kid_spec = pl.BlockSpec((1, 1, tk), lambda r, j: (r, 0, 0))
    stat_spec = pl.BlockSpec((1, 1, tq, PAIR), lambda r, j: (r, j, 0, 0))
    work = rows * tq * tk * width
    return (rows, width // PAIR), q_spec, k_spec, qid_spec, kid_spec, stat_spec, work


def attend(q, k, v, qid, kid):
    grid, q_spec, k_spec, qid_spec, kid_spec, stat_spec, work = attend_specs(q, k)
    return pl.pallas_call(
        attend_kernel,
        grid=grid,
        in_specs=[q_spec, k_spec, k_spec, qid_spec, kid_spec],
        out_specs=[q_spec, stat_spec],
        out_shape=[
            jax.ShapeDtypeStruct(q.shape, BF),
            jax.ShapeDtypeStruct((*grid, q.shape[1], PAIR), F32),
        ],
        cost_estimate=pl.CostEstimate(flops=16 * work, bytes_accessed=4 * k.size * 2, transcendentals=work // HEAD_DIM),
        compiler_params=pltpu.CompilerParams(vmem_limit_bytes=40 * 2**20),
    )(q, k, v, qid, kid)


def attend_back(q, k, v, g, qid, kid, stats=None):
    grid, q_spec, k_spec, qid_spec, kid_spec, stat_spec, work = attend_specs(q, k)
    saved = stats is not None
    low = lambda v: jax.ShapeDtypeStruct(v.shape, BF)
    return pl.pallas_call(
        functools.partial(attend_back_kernel, saved),
        grid=grid,
        in_specs=[q_spec, k_spec, k_spec, q_spec, qid_spec, kid_spec] + ([stat_spec] if saved else []),
        out_specs=([] if saved else [q_spec]) + [q_spec, k_spec, k_spec],
        out_shape=([] if saved else [low(q)]) + [low(q), low(k), low(v)],
        cost_estimate=pl.CostEstimate(flops=48 * work, bytes_accessed=6 * k.size * 2, transcendentals=work // HEAD_DIM),
        compiler_params=pltpu.CompilerParams(vmem_limit_bytes=40 * 2**20),
    )(q, k, v, g, qid, kid, *([stats] if saved else []))


def tie(x, *deps):
    return lax.optimization_barrier((x, *deps))


def turn_batch(x):
    size = lax.axis_size("batch")
    return lax.ppermute(x, "batch", [(i, size - 1 - i) for i in range(size)])


def turn_low(x):
    return swap(x, 1)


def turn_high(x):
    return swap(x, 2)


def halve(x, turn, bit):
    halves = x.reshape(2, x.shape[0] // 2, x.shape[1])
    send = lax.dynamic_index_in_dim(halves, 1 - bit, 0, keepdims=False).astype(BF)
    keep = lax.dynamic_index_in_dim(halves, bit, 0, keepdims=False)
    return keep.astype(F32) + turn(send).astype(F32)


def join(x, turn, bit):
    x = x.astype(BF)
    other = turn(x)
    return jnp.concatenate([jnp.where(bit == 0, x, other), jnp.where(bit == 0, other, x)], axis=0)


def reduce_ff(d_in, d_mlp):
    place = lax.axis_index("head")
    x_bit, y_bit = lax.axis_index("batch"), place >> 1
    core = (place & 1) == 1
    d_in, d_mlp = d_in.astype(BF), d_mlp.astype(BF)
    mine = jnp.where(core, d_mlp, d_in).astype(F32) + turn_low(jnp.where(core, d_in, d_mlp)).astype(F32)
    cut = mine.shape[0] // 2
    a, b = mine[:cut], mine[cut:]
    a, b = halve(a, turn_batch, x_bit), halve(b, turn_high, y_bit)
    a, b = halve(a, turn_high, y_bit), halve(b, turn_batch, x_bit)
    a, b = join(a, turn_high, y_bit), join(b, turn_batch, x_bit)
    a, b = join(a, turn_batch, x_bit), join(b, turn_high, y_bit)
    full = jnp.concatenate([a, b], axis=0)
    other = turn_low(full)
    return jnp.where(core, other, full).astype(F32), jnp.where(core, full, other).astype(F32)


def reduce_attn(own, partner):
    batch = lax.axis_index("batch")
    wide = lax.axis_index("wide")
    size = lax.axis_size("wide")
    own = own + turn_high(partner.astype(BF)).astype(F32)
    rows, width = own.shape
    mine = halve(own, turn_batch, batch)
    blocks = mine.reshape(size, -1, width)
    if size <= DIRECT:
        pick = lambda s: lax.dynamic_index_in_dim(blocks, (wide - s) % size, 0, keepdims=False)
        arrived = [shift(pick(s).astype(BF), -s) for s in range(1, size)]
        total = pick(0)
        for piece in arrived:
            total = total + piece.astype(F32)
        total = total.astype(BF)
        full = jnp.zeros(blocks.shape, BF)
        for s in range(size):
            piece = shift(total, s) if s else total
            full = lax.dynamic_update_index_in_dim(full, piece, (wide - s) % size, 0)
    else:
        total = lax.psum_scatter(blocks.astype(BF), "wide", scatter_dimension=0, tiled=False)
        full = lax.all_gather(total, "wide", axis=0, tiled=False)
    return join(full.reshape(rows // 2, width), turn_batch, batch).astype(F32)


def sum_all(x):
    x = x + turn_low(x)
    x = x + turn_high(x)
    x = x + turn_batch(x)
    size = lax.axis_size("wide")
    if size > DIRECT:
        return lax.psum(x, "wide")
    total = x
    for s in range(1, size):
        total = total + shift(x, s)
    return total


def general(tokens, patches, w_qkv, w_att, w_in, w_mlp, gains, cotangent):
    rows_all, slots, width = tokens.shape
    wide = lax.axis_size("wide")
    place = lax.axis_index("head")
    wide_place = lax.axis_index("wide")
    levels = w_qkv.shape[0]
    group = w_att.shape[1]
    n = rows_all * slots // 4
    rows = rows_all // 2

    def assemble(own, other, count):
        if rows == 1:
            return jnp.concatenate([own, other], axis=0)[None]
        half = rows // 2
        def turn(v):
            v = v.reshape(count, half, slots, *v.shape[1:])
            return jnp.moveaxis(v, 1, 0).reshape(half, count * slots, *v.shape[3:])
        return jnp.concatenate([turn(own), turn(other)], axis=0)

    def take_apart(v, count):
        if rows == 1:
            return v[0, : count * n], v[0, count * n :]
        half = rows // 2
        def turn(u):
            u = u.reshape(half, count, slots, *u.shape[2:])
            return jnp.moveaxis(u, 1, 0).reshape(count * n, *u.shape[3:])
        return turn(v[:half]), turn(v[half:])

    ends = jnp.cumsum(patches, axis=1)
    slot_index = jnp.arange(slots * wide, dtype=jnp.int32)
    image = jnp.sum((slot_index[None, :, None] >= ends[:, None, :]).astype(jnp.int32), axis=2)
    image = jnp.where(slot_index[None, :] < ends[:, -1:], image, -1)
    image = image.reshape(rows_all, wide, slots).transpose(1, 0, 2).reshape(wide, 4, n)
    order = (wide_place - jnp.arange(wide)) % wide
    image = image[order]
    own_image = lax.dynamic_index_in_dim(image, place, 1, keepdims=False)
    other_image = lax.dynamic_index_in_dim(image, place ^ 1, 1, keepdims=False)
    key_image = assemble(own_image.reshape(-1), other_image.reshape(-1), wide)
    query_image = assemble(own_image[0], other_image[0], 1)
    key_id = key_image[:, None, :]
    query_id = jnp.where(query_image >= 0, query_image, -2)[:, :, None]

    own = lax.dynamic_index_in_dim(tokens.reshape(4, n, width), place, 0, keepdims=False)
    cot = lax.dynamic_index_in_dim(cotangent.reshape(4, n, width), place, 0, keepdims=False)
    cot_other = lax.dynamic_index_in_dim(cotangent.reshape(4, n, width), place ^ 1, 0, keepdims=False)

    project = lambda act, w: jnp.einsum("rse,ce->rsc", act, w, preferred_element_type=F32).astype(BF)
    pull_back = lambda d, w: jnp.einsum("rkc,ce->rke", d, w, preferred_element_type=F32)
    weigh = lambda d, act: jnp.einsum("rqc,rqe->ce", d, act, preferred_element_type=F32)

    qkv_ws = [swap(w_qkv[l], 2) for l in range(levels)]
    att_ws = [swap(w_att[l], 2) for l in range(levels)]

    def weights(l, qkv_part, att_part):
        return jnp.concatenate([w_qkv[l], qkv_part], axis=1), jnp.concatenate([w_att[l], att_part], axis=0)

    def branch_of(attended, att_w):
        att_own, att_other = take_apart(
            jnp.einsum("rqc,ce->rqe", attended, att_w, preferred_element_type=F32), 1
        )
        return att_own + turn_low(att_other.astype(BF)).astype(F32)

    def act_terms(dq, dk, dv, qkv_w):
        d_act_kv = pull_back(dk, qkv_w[1]) + pull_back(dv, qkv_w[2])
        kv_own, kv_other = take_apart(d_act_kv, wide)
        q_own, q_other = take_apart(pull_back(dq, qkv_w[0]), 1)
        kv_other = kv_other.at[:n].add(q_other).astype(BF)
        return kv_own.at[:n].add(q_own) + turn_low(kv_other).astype(F32)

    def ff_back(pre, ff_grad, l):
        d_hidden = right_dot(ff_grad, w_mlp[l])
        unused, pull = jax.vjp(jax.nn.gelu, pre)
        return pull(d_hidden)[0].astype(BF)

    stream = own.astype(F32)
    saved = []
    for l in range(levels - 1):
        xhat, rstd = norm_parts(stream)
        act = (xhat * gains[l]).astype(BF)
        ff_act = gather_wide(act)
        other_act = turn_low(ff_act)
        pre = right_dot(ff_act, w_in[l])
        hidden = jax.nn.gelu(pre).astype(BF)
        parts = plain_dot(hidden, w_mlp[l])
        parts, ff_act, other_act = tie(parts, ff_act, other_act)
        branch = scatter_wide(parts)
        qkv_w, att_w = weights(l, qkv_ws[l], att_ws[l])
        key_act = assemble(ff_act, other_act, wide)
        query_act = assemble(act, other_act[:n], 1)
        q, k, v = project(query_act, qkv_w[0]), project(key_act, qkv_w[1]), project(key_act, qkv_w[2])
        attended, stats = attend(q, k, v, query_id, key_id)
        branch = branch + branch_of(attended, att_w)
        branch, qkv_ws[l + 1], att_ws[l + 1] = tie(branch, qkv_ws[l + 1], att_ws[l + 1])
        saved.append((xhat, rstd, ff_act, key_act, query_act, qkv_w, att_w, pre, hidden, q, k, v, attended, stats))
        stream = stream + branch

    l = levels - 1
    xhat, rstd = norm_parts(stream)
    act = (xhat * gains[l]).astype(BF)
    qkv_w, att_w = weights(l, qkv_ws[l], att_ws[l])
    query_grad = assemble(cot, cot_other, 1)
    d_attended = project(query_grad, att_w)
    ff_act = gather_wide(act)
    ff_act, cot, d_attended = tie(ff_act, cot, d_attended)
    ff_grad = gather_wide(cot)
    other_act = turn_low(ff_act)
    pre = right_dot(ff_act, w_in[l])
    hidden = jax.nn.gelu(pre).astype(BF)
    key_act = assemble(ff_act, other_act, wide)
    query_act = assemble(act, other_act[:n], 1)
    q, k, v = project(query_act, qkv_w[0]), project(key_act, qkv_w[1]), project(key_act, qkv_w[2])
    attended, dq, dk, dv = attend_back(q, k, v, d_attended, query_id, key_id)
    terms = act_terms(dq, dk, dv, qkv_w)
    d_pre = ff_back(pre, ff_grad, l)
    parts = terms + plain_dot(d_pre, w_in[l])
    parts, hidden, d_pre, dq, dk, dv, attended = tie(parts, hidden, d_pre, dq, dk, dv, attended)
    d_act = scatter_wide(parts)
    pieces = [weigh(dq, query_act), weigh(dk, key_act), weigh(dv, key_act), weigh(attended, query_grad)]
    last_attn = jnp.concatenate([t[:group] for t in pieces]) + turn_high(
        jnp.concatenate([t[group:] for t in pieces]).astype(BF)
    ).astype(F32)
    last_ff = jnp.concatenate([trans_dot(d_pre, ff_act), trans_dot(hidden, ff_grad)]).astype(BF)
    last_branch = branch_of(attended, att_w)
    last_parts = plain_dot(hidden, w_mlp[l])
    d_act, last_parts, last_attn, last_ff = tie(d_act, last_parts, last_attn, last_ff)
    gain_last = jnp.sum(d_act * xhat, axis=0)
    grad = cot.astype(F32) + norm_back(d_act, xhat, rstd, gains[l])
    last_attn = lax.psum(last_attn.astype(BF), ("batch", "wide"))
    last_ff = lax.psum(last_ff, ("batch", "head"))

    assert levels == 2
    l = 0
    xhat, rstd, ff_act, key_act, query_act, qkv_w, att_w, pre, hidden, q, k, v, attended, stats = saved[0]
    low = grad.astype(BF)
    other_low = turn_low(low)
    ff_grad = gather_wide(low)
    query_grad = assemble(low, other_low, 1)
    d_attended = project(query_grad, att_w)
    dq, dk, dv = attend_back(q, k, v, d_attended, query_id, key_id, stats)
    terms = act_terms(dq, dk, dv, qkv_w)
    piece_o, piece_v = weigh(attended, query_grad), weigh(dv, key_act)
    piece_q, piece_k = weigh(dq, query_act), weigh(dk, key_act)
    first_ov = reduce_attn(
        jnp.concatenate([piece_o[:group], piece_v[:group]]), jnp.concatenate([piece_o[group:], piece_v[group:]])
    )
    first_qk = reduce_attn(
        jnp.concatenate([piece_q[:group], piece_k[:group]]), jnp.concatenate([piece_q[group:], piece_k[group:]])
    )
    d_pre = ff_back(pre, ff_grad, l)
    parts = terms + plain_dot(d_pre, w_in[l])
    parts, hidden, d_pre = tie(parts, hidden, d_pre)
    d_act = scatter_wide(parts)
    first_in, first_mlp = reduce_ff(trans_dot(d_pre, ff_act), trans_dot(hidden, ff_grad))
    d_act, last_parts = tie(d_act, last_parts)
    gain_first = jnp.sum(d_act * xhat, axis=0)
    grad = grad + norm_back(d_act, xhat, rstd, gains[l])
    delta = gather_head((grad - cot.astype(F32)).astype(BF))
    d_tokens = cotangent.astype(F32) + delta.reshape(tokens.shape).astype(F32)
    d_gains = sum_all(jnp.stack([gain_first, gain_last]))
    stream = stream + last_branch + scatter_wide(last_parts)
    delta = gather_head((stream - own.astype(F32)).astype(BF))
    out = tokens.astype(F32) + delta.reshape(tokens.shape).astype(F32)
    last_attn = last_attn.astype(F32).reshape(4, group, width)
    last_in, last_mlp = last_ff[: last_ff.shape[0] // 2].astype(F32), last_ff[last_ff.shape[0] // 2 :].astype(F32)
    d_qkv = jnp.stack([jnp.stack([first_qk[:group], first_qk[group:], first_ov[group:]]), last_attn[:3]])
    return (
        out,
        d_tokens,
        d_qkv,
        jnp.stack([first_ov[:group], last_attn[3]]),
        jnp.stack([first_in, last_in]),
        jnp.stack([first_mlp, last_mlp]),
        d_gains,
    )


COST = 2 * 10**10
BACK_COST = COST
FF_COST = 10**8
NORM_COST = COST
LIMIT = 28
SMALL = 16
MIDDLE = 24
CORE, X_BIT, Y_BIT, WIDE, PLACE = range(5)


def full_spec(x):
    return pl.BlockSpec(x.shape, lambda i, *_, nd=x.ndim: (0,) * nd)


def layer_spec(x, l):
    return pl.BlockSpec((1, *x.shape[1:]), lambda i, *_, nd=x.ndim: (l,) + (0,) * (nd - 1))


def call(kernel, grid, ins, outs, scratch=(), prefetch=(), limit=SMALL, cost=COST, earlier=()):
    first = len(prefetch) + len(ins)
    ins = [*ins, *[(x, pl.BlockSpec(memory_space=pl.ANY)) for x in earlier]]
    return pl.pallas_call(
        kernel,
        grid_spec=pltpu.PrefetchScalarGridSpec(
            num_scalar_prefetch=len(prefetch),
            grid=(grid,),
            in_specs=[spec for _, spec in ins],
            out_specs=[spec for _, _, spec in outs],
            scratch_shapes=list(scratch),
        ),
        out_shape=[jax.ShapeDtypeStruct(shape, kind) for shape, kind, _ in outs],
        input_output_aliases={first + i: i for i in range(len(earlier))},
        cost_estimate=pl.CostEstimate(flops=cost, bytes_accessed=0, transcendentals=0),
        compiler_params=pltpu.CompilerParams(vmem_limit_bytes=limit * 2**20),
    )(*prefetch, *[x for x, _ in ins])


def far(x):
    return pltpu.with_memory_space_constraint(x, pltpu.HBM)


def whole_out(shape, kind):
    return (shape, kind, pl.BlockSpec(shape, lambda i, *_, nd=len(shape): (0,) * nd))


def total_of(refs):
    total = refs[0][...].astype(F32)
    for ref in refs[1:]:
        total = total + ref[...].astype(F32)
    return total


def start_norm_kernel(place_ref, tok_ref, gain_ref, act_ref):
    xhat, unused = norm_parts(tok_ref[...].astype(F32))
    act_ref[...] = (xhat * gain_ref[0]).astype(BF)


def start_norm(place, tokens, gains):
    n, width = tokens.shape
    return call(
        start_norm_kernel,
        1,
        [(tokens, full_spec(tokens)), (gains, layer_spec(gains, 0))],
        [whole_out((n, width), BF)],
        prefetch=(place,),
    )[0]


def norm_kernel(place_ref, tok_ref, gain_ref, *refs):
    stream_ref, act_ref = refs[-2:]
    stream = tok_ref[...].astype(F32) + total_of(refs[:-2])
    xhat, unused = norm_parts(stream)
    stream_ref[...] = stream
    act_ref[...] = (xhat * gain_ref[0]).astype(BF)


def norm(place, tokens, gains, l, terms):
    n, width = tokens.shape
    return call(
        norm_kernel,
        1,
        [(tokens, full_spec(tokens)), (gains, layer_spec(gains, l))]
        + [(t, full_spec(t)) for t in terms],
        [whole_out((n, width), F32), whole_out((n, width), BF)],
        prefetch=(place,),
        cost=FF_COST,
    )


def norm_back_kernel(first, place_ref, cot_ref, gain_ref, stream_ref, *refs):
    *refs, delta_ref, low_ref, gain_out = refs
    if not first:
        earlier, *refs = refs
    d_act = total_of(refs)
    xhat, rstd = norm_parts(stream_ref[...].astype(F32))
    gain_out[...] = jnp.sum(d_act * xhat, axis=0, keepdims=True)
    delta = norm_back(d_act, xhat, rstd, gain_ref[0])
    if not first:
        delta = delta + earlier[...]
        low_ref[...] = delta.astype(BF)
    else:
        low_ref[...] = (cot_ref[...].astype(F32) + delta).astype(BF)
    delta_ref[...] = delta


def norm_back_call(place, cotangent, gains, l, stream, terms, earlier=None):
    n, width = cotangent.shape
    first = earlier is None
    return call(
        functools.partial(norm_back_kernel, first),
        1,
        [(cotangent, full_spec(cotangent)), (gains, layer_spec(gains, l)), (stream, full_spec(stream))]
        + ([] if first else [(earlier, full_spec(earlier))])
        + [(t, full_spec(t)) for t in terms],
        [whole_out((n, width), F32), whole_out((n, width), BF), whole_out((1, width), F32)],
        prefetch=(place,),
        cost=NORM_COST,
    )


GELU_A = 0.7978845608028654
GELU_B = 0.044715


def gelu_both(x):
    square = x * x
    t = jnp.tanh(GELU_A * (x + GELU_B * (square * x)))
    value = 0.5 * x * (1.0 + t)
    slope = 0.5 * (1.0 + t) + 0.5 * x * (1.0 - t * t) * (GELU_A * (1.0 + 3.0 * GELU_B * square))
    return value, slope


def chunks_of(total):
    step = 256 if total % 256 == 0 else total
    return [slice(i, i + step) for i in range(0, total, step)]


def write_parts(total, n, part_refs):
    for s, ref in enumerate(part_refs):
        ref[...] = total[s * n : (s + 1) * n].astype(ref.dtype)


def ff_kernel(count, spot_ref, *refs):
    x_refs, (in_ref, mlp_ref, slope_ref, hidden_ref, all_ref), part_refs = refs[:count], refs[count : count + 5], refs[count + 5 :]
    n = x_refs[0].shape[0]
    x = jnp.concatenate([r[...] for r in x_refs], axis=0)
    all_ref[...] = x
    total = None
    for cut in chunks_of(in_ref.shape[1]):
        value, slope = gelu_both(right_dot(x, in_ref[0, cut, :]))
        low = value.astype(BF)
        slope_ref[:, cut] = slope
        hidden_ref[:, cut] = low
        term = plain_dot(low, mlp_ref[0, cut, :])
        total = term if total is None else total + term
    if len(part_refs) == 1:
        for s in range(count):
            part_refs[0][lax.rem(spot_ref[WIDE] - s + count, count)] = total[s * n : (s + 1) * n].astype(BF)
    else:
        write_parts(total, n, part_refs)


def part_outs(count, n, width):
    return [whole_out((n, width), F32 if s == 0 else BF) for s in range(count)]


def ff(spot, xs, w_in, w_mlp, l, blocks=False):
    count, (n, width) = len(xs), xs[0].shape
    w_in, w_mlp = w_in[l], w_mlp[l]
    hidden = w_in.shape[1]
    slope, low, x_all, *parts = call(
        functools.partial(ff_kernel, count),
        1,
        [(x, full_spec(x)) for x in (*xs, w_in, w_mlp)],
        [whole_out((count * n, hidden), F32), whole_out((count * n, hidden), BF), whole_out((count * n, width), BF)]
        + ([whole_out((count, n, width), BF)] if blocks else part_outs(count, n, width)),
        prefetch=(spot,),
        cost=FF_COST,
    )
    return slope, low, x_all, parts[0] if blocks else parts


def ff_slope_kernel(count, *refs):
    g_refs, (mlp_ref, slope_ref, d_pre_ref, all_ref) = refs[:count], refs[count:]
    g = jnp.concatenate([r[...] for r in g_refs], axis=0)
    all_ref[...] = g
    for cut in chunks_of(mlp_ref.shape[1]):
        d_pre_ref[:, cut] = (slope_ref[:, cut] * right_dot(g, mlp_ref[0, cut, :])).astype(BF)


def ff_slope(gs, w_mlp, l, slope):
    count, (n, width) = len(gs), gs[0].shape
    return call(
        functools.partial(ff_slope_kernel, count),
        1,
        [(g, full_spec(g)) for g in (*gs, w_mlp[l], slope)],
        [whole_out(slope.shape, BF), whole_out((count * n, width), BF)],
    )


def ff_back_kernel(n, d_pre_ref, in_ref, own_ref, got_ref, *part_refs):
    total = own_ref[...] + got_ref[...].astype(F32) + plain_dot(d_pre_ref[...], in_ref[0])
    write_parts(total, n, part_refs)


def ff_back(count, d_pre, w_in, l, own, got):
    n, width = d_pre.shape[0] // count, w_in[l].shape[2]
    return call(
        functools.partial(ff_back_kernel, n),
        1,
        [(x, full_spec(x)) for x in (d_pre, w_in[l], own, got)],
        part_outs(count, n, width),
    )


def ff_weights_kernel(outer, spot_ref, x_ref, g_ref, d_pre_ref, hidden_ref, keep_ref, send_ref):
    core = spot_ref[CORE] == 1
    d_in = trans_dot(d_pre_ref[...], x_ref[...])
    d_mlp = trans_dot(hidden_ref[...], g_ref[...])
    half = d_in.shape[0] // 2
    keep, send = jnp.where(core, d_mlp, d_in), jnp.where(core, d_in, d_mlp).astype(BF)
    for j in range(2):
        at = j ^ spot_ref[Y_BIT if outer == X_BIT else X_BIT]
        keep_ref[0, at] = keep[j * half : (j + 1) * half]
        send_ref[0, at] = send[j * half : (j + 1) * half]


def ff_weights(spot, xs, gs, d_pre, hidden, outer):
    width = xs.shape[1]
    tokens, size = d_pre.shape
    cut = pl.BlockSpec((tokens, size // 2), lambda i, p: (0, i))
    shape = (2, 2, size // 4, width)
    out = pl.BlockSpec((1, *shape[1:]), lambda i, p: (i ^ p[outer], 0, 0, 0))
    return call(
        functools.partial(ff_weights_kernel, outer),
        2,
        [(far(x), full_spec(x)) for x in (xs, gs)] + [(far(d_pre), cut), (far(hidden), cut)],
        [(shape, F32, out), (shape, BF, out)],
        prefetch=(spot,),
        cost=COST // 4,
    )


def ff_finish_kernel(spot_ref, mine_ref, got_ref, *refs):
    in_ref, mlp_ref = refs[-2:]
    core = spot_ref[CORE] == 1
    mine, got = mine_ref[0].astype(F32), got_ref[0].astype(F32)
    in_ref[0] = jnp.where(core, got, mine)
    mlp_ref[0] = jnp.where(core, mine, got)


def ff_finish(spot, l, mine, got, outer, earlier=()):
    unused, rows, width = mine.shape
    inner = Y_BIT if outer == X_BIT else X_BIT
    spec = pl.BlockSpec((1, rows, width), lambda i, p: (i ^ (2 * p[outer] + p[inner]), 0, 0))
    out = ((2, 4 * rows, width), F32, pl.BlockSpec((1, rows, width), lambda i, p: (l, i, 0)))
    return call(ff_finish_kernel, 4, [(mine, spec), (got, spec)], [out, out], prefetch=(spot,), earlier=earlier)


def attn_kernel(mode, count, *refs):
    refs = list(refs)
    take = lambda k: [refs.pop(0) for _ in range(k)]
    if mode != "back":
        act_refs = take(2)
    if mode != "fwd":
        g_refs = take(2)
    w_own, a_own, p_qk, p_vo, qid_ref, kid_ref = take(6)
    if mode == "back":
        q_ref, k_ref, v_ref, stat_ref = take(4)
    step = pl.program_id(0)
    scale = HEAD_DIM ** (-0.5)
    n = qid_ref.shape[0] // 2
    half = count * n
    if mode == "fwd":
        q_out, k_out, v_out, o_out, stat_out, b_own, b_other, act_all, branch = refs
    elif mode == "both":
        q_out, k_out, v_out, o_out, t_own, t_other, b_own, b_other, act_all, branch, terms = refs
    else:
        q_out, k_out, v_out, t_own, t_other, terms = refs
    if mode != "back":

        @pl.when(step == 0)
        def _():
            act_all[:half, :] = act_refs[0][...]
            act_all[half:, :] = act_refs[1][...]

    w_kv = jnp.concatenate([w_own[0, 1], p_qk[1], w_own[0, 2], p_vo[0]], axis=0)
    w_q = jnp.concatenate([w_own[0, 0], p_qk[0]], axis=0)
    w_o = jnp.concatenate([a_own[0], p_vo[1]], axis=0)
    if mode != "back":
        kv = right_dot(act_all[...], w_kv).astype(BF)
        k, v = kv[:, :PAIR], kv[:, PAIR:]
        q_in = jnp.concatenate([act_refs[0][:n, :], act_refs[1][:n, :]], axis=0)
        q = right_dot(q_in, w_q).astype(BF)
    else:
        q, k, v = q_ref[...], k_ref[...], v_ref[...]
    if mode == "fwd":
        q_out[...], k_out[...], v_out[...] = q, k, v
    q = q * jnp.asarray(scale, BF)
    allowed = qid_ref[...] == kid_ref[...]
    if mode != "fwd":
        g = right_dot(jnp.concatenate([r[...] for r in g_refs], axis=0), w_o).astype(BF)
    lane = lax.broadcasted_iota(jnp.int32, (2 * n, PAIR), 1)
    stats = jnp.zeros((2 * n, PAIR), F32)
    outs, dqs, dks, dvs = [], [], [], []
    for j in range(2):
        cut = slice(j * HEAD_DIM, (j + 1) * HEAD_DIM)
        qj, kj, vj = q[:, cut], k[:, cut], v[:, cut]
        if mode == "back":
            top, inverse = stat_ref[0, :, 2 * j : 2 * j + 1], stat_ref[0, :, 2 * j + 1 : 2 * j + 2]
            probs = jnp.exp(jnp.where(allowed, right_dot(qj, kj), NEGATIVE) - top) * inverse
        else:
            probs, top, inverse = head_softmax(qj, kj, allowed)
            stats = jnp.where(lane == 2 * j, top, jnp.where(lane == 2 * j + 1, inverse, stats))
        low = probs.astype(BF)
        if mode != "back":
            outs.append(plain_dot(low, vj))
        if mode != "fwd":
            gj = g[:, cut]
            dp = right_dot(gj, vj)
            ds = (probs * (dp - jnp.sum(probs * dp, axis=-1, keepdims=True))).astype(BF)
            dqs.append(plain_dot(ds, kj) * scale)
            dks.append(trans_dot(ds, qj))
            dvs.append(trans_dot(low, gj))
    last = step == pl.num_programs(0) - 1
    if mode != "back":
        attended = jnp.concatenate(outs, axis=1).astype(BF)
        o_out[...] = attended
        term = plain_dot(attended, w_o)

        @pl.when(step == 0)
        def _():
            branch[...] = term

        @pl.when(step > 0)
        def _():
            branch[...] += term

        @pl.when(last)
        def _():
            b_own[...] = branch[:n, :]
            b_other[...] = branch[n:, :].astype(BF)

    if mode == "fwd":
        stat_out[0] = stats
    else:
        dq = jnp.concatenate(dqs, axis=1).astype(BF)
        dkv = jnp.concatenate(dks + dvs, axis=1).astype(BF)
        q_out[...], k_out[...], v_out[...] = dq, dkv[:, :PAIR], dkv[:, PAIR:]
        term_kv = plain_dot(dkv, w_kv)
        term_q = plain_dot(dq, w_q)

        @pl.when(step == 0)
        def _():
            terms[...] = term_kv

        @pl.when(step > 0)
        def _():
            terms[...] += term_kv

        terms[:n, :] += term_q[:n]
        terms[half : half + n, :] += term_q[n:]

        @pl.when(last)
        def _():
            t_own[...] = terms[:half, :]
            t_other[...] = terms[half:, :].astype(BF)


def attn(mode, count, l, w_qkv, w_att, part, qid, kid, acts=(), grads=(), kept=()):
    group, width = part.shape[1:]
    n = qid.shape[0] // 2
    tq, tk = 2 * n, 2 * count * n
    steps = group // HEAD_DIM
    pair_q = pl.BlockSpec((tq, PAIR), lambda i: (0, i))
    pair_k = pl.BlockSpec((tk, PAIR), lambda i: (0, i))
    stat = pl.BlockSpec((1, tq, PAIR), lambda i: (i, 0, 0))
    ins = [(x, full_spec(x)) for x in (*acts, *grads)] + [
        (far(w_qkv), pl.BlockSpec((1, 3, HEAD_DIM, width), lambda i: (l, 0, i, 0))),
        (far(w_att), pl.BlockSpec((1, HEAD_DIM, width), lambda i: (l, i, 0))),
        *[(far(part), pl.BlockSpec((2, HEAD_DIM, width), lambda i, h=h: (h, i, 0))) for h in range(2)],
        (qid, full_spec(qid)),
        (kid, full_spec(kid)),
    ]
    if mode == "back":
        q, k, v, stats = kept
        ins += [(far(q), pair_q), (far(k), pair_k), (far(v), pair_k), (far(stats), stat)]
    q_shape, k_shape = (tq, 2 * group), (tk, 2 * group)
    outs = [(q_shape, BF, pair_q), (k_shape, BF, pair_k), (k_shape, BF, pair_k)]
    scratch = []
    if mode != "back":
        outs += [(q_shape, BF, pair_q)]
        scratch += [pltpu.VMEM((tk, width), BF), pltpu.VMEM((tq, width), F32)]
    if mode == "fwd":
        outs += [((steps, tq, PAIR), F32, stat)]
    else:
        outs += [whole_out((tk // 2, width), F32), whole_out((tk // 2, width), BF)]
        scratch += [pltpu.VMEM((tk, width), F32)]
    if mode != "back":
        outs += [whole_out((n, width), F32), whole_out((n, width), BF)]
    cost = BACK_COST if mode == "back" else COST
    return call(functools.partial(attn_kernel, mode, count), steps, ins, outs, scratch, limit=LIMIT, cost=cost)


def attn_weights_kernel(spot_ref, own_act, other_act, g_own, g_other, dq_ref, dk_ref, dv_ref, o_ref, own_ref, part_ref, act_all):
    n = g_own.shape[0]
    half = act_all.shape[0] // 2
    step = pl.program_id(0)

    @pl.when(step == 0)
    def _():
        act_all[:half, :] = own_act[...]
        act_all[half:, :] = other_act[...]

    q_in = jnp.concatenate([own_act[:n, :], other_act[:n, :]], axis=0)
    g_in = jnp.concatenate([g_own[...], g_other[...]], axis=0)
    kv = trans_dot(jnp.concatenate([dk_ref[...], dv_ref[...]], axis=1), act_all[...])
    pairs = (trans_dot(dq_ref[...], q_in), kv[:PAIR], kv[PAIR:], trans_dot(o_ref[...], g_in))
    rows = own_ref.shape[2]
    for i in range(2 * rows // HEAD_DIM):

        @pl.when(step == i)
        def _():
            for t, pair in enumerate(pairs):
                back = lax.rem(spot_ref[WIDE] - t + 4, 4)
                low = i * HEAD_DIM
                while low < (i + 1) * HEAD_DIM:
                    high = min((i + 1) * HEAD_DIM, (low // rows + 1) * rows)
                    at = (low // rows) ^ spot_ref[X_BIT]
                    dest = slice(low % rows, low % rows + high - low)
                    source = slice(low - i * HEAD_DIM, high - i * HEAD_DIM)
                    own_ref[at, back, dest, :] = pair[:HEAD_DIM][source]
                    part_ref[at, back, dest, :] = pair[HEAD_DIM:][source].astype(BF)
                    low = high


def attn_weights(spot, acts, grads, dq, dk, dv, attended):
    n, width = grads[0].shape
    tq, tk, group = 2 * n, 2 * acts[0].shape[0], dq.shape[1] // 2
    pair_q = pl.BlockSpec((tq, PAIR), lambda i, p: (0, i))
    pair_k = pl.BlockSpec((tk, PAIR), lambda i, p: (0, i))
    shape = (2, 4, group // 2, width)
    return call(
        attn_weights_kernel,
        group // HEAD_DIM,
        [(x, full_spec(x)) for x in (*acts, *grads)] + [(dq, pair_q), (dk, pair_k), (dv, pair_k), (attended, pair_q)],
        [whole_out(shape, F32), whole_out(shape, BF)],
        [pltpu.VMEM((tk, width), BF)],
        (spot,),
        limit=MIDDLE,
        cost=COST // 4,
    )


def attn_finish_kernel(spot_ref, mine_ref, got_ref, *refs):
    qkv_ref, att_ref = refs[-2:]
    matrix = pl.program_id(0)
    second = spot_ref[X_BIT] == 1
    mine, got = mine_ref[0].astype(F32), got_ref[0].astype(F32)
    whole = jnp.concatenate([jnp.where(second, got, mine), jnp.where(second, mine, got)], axis=0)

    @pl.when(matrix < 3)
    def _():
        qkv_ref[0, 0] = whole

    @pl.when(matrix == 3)
    def _():
        att_ref[0] = whole


def attn_finish(spot, l, mine, got, earlier=()):
    unused, rows, width = mine.shape
    spec = pl.BlockSpec((1, rows, width), lambda i, p: (lax.rem(p[WIDE] - i + 4, 4), 0, 0))
    return call(
        attn_finish_kernel,
        4,
        [(mine, spec), (got, spec)],
        [
            ((2, 3, 2 * rows, width), F32, pl.BlockSpec((1, 1, 2 * rows, width), lambda i, p: (l, jnp.minimum(i, 2), 0, 0))),
            ((2, 2 * rows, width), F32, pl.BlockSpec((1, 2 * rows, width), lambda i, p: (l, 0, 0))),
        ],
        prefetch=(spot,),
        earlier=earlier,
    )


def gather_list(x):
    return [x] + [shift(x, s) for s in range(1, lax.axis_size("wide"))]


def return_list(parts):
    return [parts[0]] + [shift(p, -s) for s, p in enumerate(parts) if s]


def reduce_ff_rest(keep, got):
    x_bit, y_bit = lax.axis_index("batch"), lax.axis_index("head") >> 1
    core = (lax.axis_index("head") & 1) == 1
    mine = keep + got.astype(F32)
    cut = mine.shape[0] // 2
    a, b = mine[:cut], mine[cut:]
    a, b = halve(a, turn_batch, x_bit), halve(b, turn_high, y_bit)
    a, b = halve(a, turn_high, y_bit), halve(b, turn_batch, x_bit)
    a, b = join(a, turn_high, y_bit), join(b, turn_batch, x_bit)
    a, b = join(a, turn_batch, x_bit), join(b, turn_high, y_bit)
    full = jnp.concatenate([a, b], axis=0)
    other = turn_low(full)
    return jnp.where(core, other, full), jnp.where(core, full, other)


def together(*pairs):
    sent = tie(*[x for x, _ in pairs])
    return tie(*[f(x) for x, (_, f) in zip(sent, pairs)])


def half_of(x, bit):
    halves = x.reshape(2, x.shape[0] // 2, x.shape[1])
    return (
        lax.dynamic_index_in_dim(halves, bit, 0, keepdims=False),
        lax.dynamic_index_in_dim(halves, 1 - bit, 0, keepdims=False).astype(BF),
    )


def shifts(sign):
    return [functools.partial(shift, step=sign * s) for s in range(1, lax.axis_size("wide"))]


def blocks_of(x):
    wide, size = lax.axis_index("wide"), lax.axis_size("wide")
    blocks = x.reshape(size, -1, x.shape[1])
    own, *others = [lax.dynamic_index_in_dim(blocks, (wide - s) % size, 0, keepdims=False) for s in range(size)]
    return own, [o.astype(BF) for o in others]


def laid(pieces):
    wide, size = lax.axis_index("wide"), lax.axis_size("wide")
    full = jnp.zeros((size, *pieces[0].shape), pieces[0].dtype)
    for s, piece in enumerate(pieces):
        full = lax.dynamic_update_index_in_dim(full, piece, (wide - s) % size, 0)
    return full.reshape(-1, pieces[0].shape[1])


def ordered(mine, other, bit):
    return jnp.where(bit == 0, mine, other), jnp.where(bit == 0, other, mine)


def sum_of(first, pieces):
    total = first.astype(F32)
    for piece in pieces:
        total = total + piece.astype(F32)
    return total


def fast(tokens, patches, w_qkv, w_att, w_in, w_mlp, gains, cotangent):
    rows_all, slots, width = tokens.shape
    shape = tokens.shape
    wide = lax.axis_size("wide")
    head_place, wide_place = lax.axis_index("head"), lax.axis_index("wide")
    x_bit, y_bit, core = lax.axis_index("batch"), head_place >> 1, head_place & 1
    spot = jnp.stack([core, x_bit, y_bit, wide_place, head_place]).astype(jnp.int32)
    group = w_att.shape[1]
    n = rows_all * slots // 4
    tokens, cotangent = tokens.reshape(4, n, width), cotangent.reshape(4, n, width)
    gains = gains[:, None, :]
    w_in, w_mlp = [w_in[l : l + 1] for l in range(2)], [w_mlp[l : l + 1] for l in range(2)]

    own_ws = [jnp.concatenate([w_qkv[l], w_att[l][None]]) for l in range(2)]
    tok = lax.dynamic_index_in_dim(tokens, head_place, 0, keepdims=False)
    act = start_norm(spot, tok, gains)
    xs = gather_list(act)
    part0 = turn_high(own_ws[0])

    ends = jnp.cumsum(patches, axis=1)
    slot_index = jnp.arange(slots * wide, dtype=jnp.int32)
    image = jnp.sum((slot_index[None, :, None] >= ends[:, None, :]).astype(jnp.int32), axis=2)
    image = jnp.where(slot_index[None, :] < ends[:, -1:], image, -1)
    image = image.reshape(rows_all, wide, slots).transpose(1, 0, 2).reshape(wide, 4, n)
    order = (wide_place - jnp.arange(wide)) % wide
    image = image[order]
    own_image = lax.dynamic_index_in_dim(image, head_place, 1, keepdims=False)
    other_image = lax.dynamic_index_in_dim(image, head_place ^ 1, 1, keepdims=False)
    kid = jnp.concatenate([own_image.reshape(-1), other_image.reshape(-1)])[None, :]
    qid = jnp.concatenate([own_image[0], other_image[0]])
    qid = jnp.where(qid >= 0, qid, -2)[:, None]
    cot = lax.dynamic_index_in_dim(cotangent, head_place, 0, keepdims=False)
    cot_other = lax.dynamic_index_in_dim(cotangent, head_place ^ 1, 0, keepdims=False)

    xs[1], kid, qid, own_ws[1], cot, cot_other = tie(xs[1], kid, qid, own_ws[1], cot, cot_other)

    slope0, hidden0, own0, parts = ff(spot, xs, w_in, w_mlp, 0)
    terms = return_list(parts)
    acts0 = (own0, turn_low(own0))
    part0, next_w = tie(part0, own_ws[1])
    part1 = turn_high(next_w)
    q, k, v, attended0, stats, b_own, b_other = attn("fwd", wide, 0, w_qkv, w_att, part0, qid, kid, acts=acts0)
    b_got = turn_low(b_other)
    stream1, act = norm(spot, tok, gains, 1, [*terms, b_own, b_got])

    xs1 = gather_list(act)
    slope1, hidden1, own1, out_parts = ff(spot, xs1, w_in, w_mlp, 1, True)
    other1 = turn_low(own1)
    cot_tied, unused = tie(cot, own1)
    gs1 = gather_list(cot_tied)
    dq1, dk1, dv1, attended1, t_own, t_other, b_own1, b_other1 = attn(
        "both", wide, 1, w_qkv, w_att, part1, qid, kid, acts=(own1, other1), grads=(cot, cot_other)
    )
    t_got = turn_low(t_other)
    d_pre1, g_all1 = ff_slope(gs1, w_mlp, 1, slope1)
    parts = list(ff_back(wide, d_pre1, w_in, 1, t_own, t_got))
    parts[1], dq1, hidden1, b_other1 = tie(parts[1], dq1, hidden1, b_other1)
    back1 = return_list(parts)
    own_w1, part_w1 = attn_weights(spot, (own1, other1), (cot, cot_other), dq1, dk1, dv1, attended1)
    keep_f1, send_f1 = ff_weights(spot, own1, g_all1, d_pre1, hidden1, X_BIT)
    b_got1 = turn_low(b_other1)
    back1[1], b_got1, send_f1, keep_f1, own_w1, part_w1 = tie(back1[1], b_got1, send_f1, keep_f1, own_w1, part_w1)
    got_f1 = turn_low(send_f1)
    got_w1 = turn_high(part_w1)
    delta1, low, gain1 = norm_back_call(spot, cot, gains, 1, stream1, back1)

    low_other = turn_low(low)
    gs = gather_list(low)
    dq, dk, dv, t_own, t_other = attn(
        "back", wide, 0, w_qkv, w_att, part0, qid, kid, grads=(low, low_other), kept=(q, k, v, stats)
    )
    t_got = turn_low(t_other)
    own_w0, part_w0 = attn_weights(spot, acts0, (low, low_other), dq, dk, dv, attended0)
    got_f1, part_w0, own_w0 = tie(got_f1, part_w0, own_w0)
    got_x1 = turn_batch((keep_f1[1] + got_f1[1].astype(F32)).astype(BF))
    got_w0 = turn_high(part_w0)
    gs[1], own_w0, part_w0 = tie(gs[1], own_w0, part_w0)
    d_pre0, g_all0 = ff_slope(gs, w_mlp, 0, slope0)
    parts = list(ff_back(wide, d_pre0, w_in, 0, t_own, t_got))
    parts[1], hidden0 = tie(parts[1], hidden0)
    back0 = return_list(parts)
    keep_f0, send_f0 = ff_weights(spot, own0, g_all0, d_pre0, hidden0, Y_BIT)
    got_w1, got_x1, keep_f0 = tie(got_w1, got_x1, keep_f0)
    sum_w1 = own_w1 + got_w1.astype(F32)
    got_w1 = turn_batch(sum_w1[1].astype(BF))
    back0[1], keep_f0, send_f0 = tie(back0[1], keep_f0, send_f0)
    half_w1 = sum_w1[0] + got_w1.astype(F32)
    half_f1 = sum_of(keep_f1[0], [got_f1[0], got_x1])
    delta0, low0, gain0 = norm_back_call(spot, cot, gains, 0, tok, back0, delta1)

    last = lax.psum_scatter(out_parts, "wide", scatter_dimension=0, tiled=False)
    b_got1, last, stream1, low0 = tie(b_got1, last, stream1, low0)
    half_w1, half_f1, last = tie(half_w1, half_f1, last)
    delta_out = (stream1 - tok.astype(F32) + sum_of(b_own1, [b_got1, last])).astype(BF)
    ends = lax.all_gather(jnp.concatenate([delta_out, low0], axis=1), "head", axis=0, tiled=False)

    gain = jnp.concatenate([gain0, gain1, jnp.zeros((6, width), F32)])

    def with_gain(x, gain):
        high = gain.astype(BF)
        return jnp.concatenate([x.reshape(-1, width).astype(BF), high, (gain - high.astype(F32)).astype(BF)])

    def gain_of(got):
        return got[-16:-8].astype(F32) + got[-8:].astype(F32)

    got_f0 = turn_low(send_f0)
    got_w0, half_w1, half_f1, got_f0 = tie(got_w0, half_w1, half_f1, got_f0)
    sum_w0 = own_w0 + got_w0.astype(F32)
    got_w0, got_f1, *got_b1 = together(
        (sum_w0[1].astype(BF), turn_batch),
        (half_f1[1].astype(BF), turn_high),
        *[(half_w1[s + 1].astype(BF), f) for s, f in enumerate(shifts(-1))],
    )
    block_w1 = sum_of(half_w1[0], got_b1).astype(BF)
    half_w0 = sum_w0[0] + got_w0.astype(F32)
    block_f1 = (half_f1[0] + got_f1.astype(F32)).astype(BF)
    sum_f0 = keep_f0 + got_f0.astype(F32)
    rows_f = sum_f0.shape[2]
    got_f0, got_f1, *got_b0 = together(
        (with_gain(sum_f0[1], gain), turn_high),
        (block_f1, turn_batch),
        *[(half_w0[s + 1].astype(BF), f) for s, f in enumerate(shifts(-1))],
    )
    gain = gain + gain_of(got_f0)
    block_w0 = sum_of(half_w0[0], got_b0)
    half_f0 = sum_f0[0] + got_f0[: 2 * rows_f].reshape(2, rows_f, width).astype(F32)
    pair_f1 = jnp.stack([block_f1, got_f1])
    got_f0, got_f1, *got_b1 = together(
        (with_gain(half_f0[1], gain), turn_batch), (pair_f1, turn_high), *[(block_w1, f) for f in shifts(1)]
    )
    gain = gain + gain_of(got_f0)
    block_f0 = (half_f0[0] + got_f0[:rows_f].astype(F32)).astype(BF)
    full_f1 = jnp.stack([pair_f1, got_f1], axis=1).reshape(4, rows_f, width)
    mine_w1 = jnp.stack([block_w1, *got_b1])
    block_w0 = with_gain(block_w0, gain)
    got_f0, got_w1, *got_b0 = together(
        (block_f0, turn_batch), (mine_w1, turn_batch), *[(block_w0, f) for f in shifts(1)]
    )
    gain = sum_of(gain, [gain_of(g) for g in got_b0])
    pair_f0 = jnp.stack([block_f0, got_f0])
    rows_w = half_w0.shape[1]
    mine_w0 = jnp.stack([g[:rows_w] for g in (block_w0, *got_b0)])
    mine_w0, ends = tie(mine_w0, ends)
    got_w0, got_f0, got_g, got_f1 = together(
        (mine_w0, turn_batch), (pair_f0, turn_high), (gain, turn_low), (full_f1, turn_low)
    )
    full_f0 = jnp.concatenate([pair_f0, got_f0])
    got_f0 = turn_low(full_f0)
    d_gains = (gain + got_g)[:2]
    late = ff_finish(spot, 1, full_f1, got_f1, X_BIT)
    d_in, d_mlp = ff_finish(spot, 0, full_f0, got_f0, Y_BIT, late)
    out = tokens.astype(F32) + ends[:, :, :width].astype(F32)
    d_tokens = cotangent.astype(F32) + ends[:, :, width:].astype(F32)
    d_qkv, d_att = attn_finish(spot, 0, mine_w0, got_w0, attn_finish(spot, 1, mine_w1, got_w1))
    return (out.reshape(shape), d_tokens.reshape(shape), d_qkv, d_att, d_in, d_mlp, d_gains)


def solution(mesh):
    def local(*arrays):
        tokens, w_qkv = arrays[0], arrays[2]
        small = tokens.shape[0] == 2 and lax.axis_size("wide") == 4 and w_qkv.shape[0] == 2
        return (fast if small else general)(*arrays)

    return jax.shard_map(
        local,
        mesh=mesh,
        in_specs=(
            P("batch", "wide", None),
            P("batch", None),
            P(None, None, "head", None),
            P(None, "head", None),
            P(None, "wide", None),
            P(None, "wide", None),
            P(),
            P("batch", "wide", None),
        ),
        out_specs=(
            P("batch", "wide", None),
            P("batch", "wide", None),
            P(None, None, "head", None),
            P(None, "head", None),
            P(None, "wide", None),
            P(None, "wide", None),
            P(),
        ),
        check_vma=False,
    )
```

```python
import functools

import jax
import jax.numpy as jnp
from jax import lax
from jax.experimental import pallas as pl
from jax.experimental.pallas import tpu as pltpu
from jax.sharding import PartitionSpec as P

HEAD_DIM = 64
EPS = 1e-06
NEGATIVE = -1e30
BF = jnp.bfloat16
F32 = jnp.float32
DIRECT = 8


def norm_parts(stream):
    centre = jnp.mean(stream, axis=-1, keepdims=True)
    centred = stream - centre
    spread = jnp.mean(centred * centred, axis=-1, keepdims=True)
    rstd = lax.rsqrt(spread + EPS)
    return centred * rstd, rstd


def norm_back(d_act, xhat, rstd, gain_row):
    dxh = d_act * gain_row
    m1 = jnp.mean(dxh, axis=-1, keepdims=True)
    m2 = jnp.mean(dxh * xhat, axis=-1, keepdims=True)
    return (dxh - m1 - xhat * m2) * rstd


def trans_dot(left, right):
    return lax.dot_general(left, right, (((0,), (0,)), ((), ())), preferred_element_type=F32)


def right_dot(left, right):
    return lax.dot_general(left, right, (((1,), (1,)), ((), ())), preferred_element_type=F32)


def plain_dot(left, right):
    return jnp.dot(left, right, preferred_element_type=F32)


def swap(x, bit):
    size = lax.axis_size("head")
    return lax.ppermute(x, "head", [(i, i ^ bit) for i in range(size)])


def shift(x, step):
    size = lax.axis_size("wide")
    return lax.ppermute(x, "wide", [(i, (i + step) % size) for i in range(size)])


def gather_wide(x):
    size = lax.axis_size("wide")
    if size <= DIRECT:
        return jnp.concatenate([x] + [shift(x, s) for s in range(1, size)], axis=0)
    whole = lax.all_gather(x, "wide", axis=0, tiled=False)
    order = (lax.axis_index("wide") - jnp.arange(size)) % size
    return whole[order].reshape(size * x.shape[0], *x.shape[1:])


def scatter_wide(parts):
    size = lax.axis_size("wide")
    rows = parts.shape[0] // size
    if size <= DIRECT:
        total = parts[:rows]
        low = [shift(parts[s * rows : (s + 1) * rows].astype(BF), -s) for s in range(1, size)]
        for piece in low:
            total = total + piece.astype(F32)
        return total
    order = (lax.axis_index("wide") - jnp.arange(size)) % size
    blocks = parts.astype(BF).reshape(size, rows, -1)[order]
    return lax.psum_scatter(blocks, "wide", scatter_dimension=0, tiled=False).astype(F32)


def gather_head(x):
    place = lax.axis_index("head")
    a = x
    b = swap(x, 2)
    c = swap(a, 1)
    d = swap(b, 1)
    low_bit = (place & 1) == 1
    high_bit = (place & 2) == 2
    a, c = jnp.where(low_bit, c, a), jnp.where(low_bit, a, c)
    b, d = jnp.where(low_bit, d, b), jnp.where(low_bit, b, d)
    a, b = jnp.where(high_bit, b, a), jnp.where(high_bit, a, b)
    c, d = jnp.where(high_bit, d, c), jnp.where(high_bit, c, d)
    return jnp.stack([a, c, b, d])


PAIR = 2 * HEAD_DIM
FLOOR = -1e29


def head_softmax(q, k, allowed):
    s = jnp.where(allowed, right_dot(q, k), NEGATIVE)
    top = jnp.maximum(jnp.max(s, axis=-1, keepdims=True), FLOOR)
    expo = jnp.exp(s - top)
    inverse = 1.0 / jnp.maximum(jnp.sum(expo, axis=-1, keepdims=True), 1.0)
    return expo * inverse, top, inverse


def attend_kernel(q_ref, k_ref, v_ref, qid_ref, kid_ref, o_ref, stat_ref):
    allowed = qid_ref[0] == kid_ref[0]
    q = q_ref[0] * jnp.asarray(HEAD_DIM ** (-0.5), BF)
    k, v = k_ref[0], v_ref[0]
    lane = lax.broadcasted_iota(jnp.int32, (q.shape[0], PAIR), 1)
    stats = jnp.zeros((q.shape[0], PAIR), F32)
    outs = []
    for j in range(2):
        cut = slice(j * HEAD_DIM, (j + 1) * HEAD_DIM)
        probs, top, inverse = head_softmax(q[:, cut], k[:, cut], allowed)
        outs.append(plain_dot(probs.astype(BF), v[:, cut]))
        stats = jnp.where(lane == 2 * j, top, jnp.where(lane == 2 * j + 1, inverse, stats))
    o_ref[0] = jnp.concatenate(outs, axis=1).astype(BF)
    stat_ref[0, 0] = stats


def attend_back_kernel(saved, q_ref, k_ref, v_ref, g_ref, qid_ref, kid_ref, *refs):
    if saved:
        stat_ref, dq_ref, dk_ref, dv_ref = refs
    else:
        o_ref, dq_ref, dk_ref, dv_ref = refs
    allowed = qid_ref[0] == kid_ref[0]
    scale = HEAD_DIM ** (-0.5)
    q = q_ref[0] * jnp.asarray(scale, BF)
    k, v, g = k_ref[0], v_ref[0], g_ref[0]
    outs, dqs, dks, dvs = [], [], [], []
    for j in range(2):
        cut = slice(j * HEAD_DIM, (j + 1) * HEAD_DIM)
        qj, kj, vj, gj = q[:, cut], k[:, cut], v[:, cut], g[:, cut]
        if saved:
            top = stat_ref[0, 0, :, 2 * j : 2 * j + 1]
            inverse = stat_ref[0, 0, :, 2 * j + 1 : 2 * j + 2]
            probs = jnp.exp(jnp.where(allowed, right_dot(qj, kj), NEGATIVE) - top) * inverse
        else:
            probs, top, inverse = head_softmax(qj, kj, allowed)
        low = probs.astype(BF)
        if not saved:
            outs.append(plain_dot(low, vj))
        dp = right_dot(gj, vj)
        ds = (probs * (dp - jnp.sum(probs * dp, axis=-1, keepdims=True))).astype(BF)
        dqs.append(plain_dot(ds, kj) * scale)
        dks.append(trans_dot(ds, qj))
        dvs.append(trans_dot(low, gj))
    if not saved:
        o_ref[0] = jnp.concatenate(outs, axis=1).astype(BF)
    dq_ref[0] = jnp.concatenate(dqs, axis=1).astype(BF)
    dk_ref[0] = jnp.concatenate(dks, axis=1).astype(BF)
    dv_ref[0] = jnp.concatenate(dvs, axis=1).astype(BF)


def attend_specs(q, k):
    rows, tq, width = q.shape
    tk = k.shape[1]
    q_spec = pl.BlockSpec((1, tq, PAIR), lambda r, j: (r, 0, j))
    k_spec = pl.BlockSpec((1, tk, PAIR), lambda r, j: (r, 0, j))
    qid_spec = pl.BlockSpec((1, tq, 1), lambda r, j: (r, 0, 0))
    kid_spec = pl.BlockSpec((1, 1, tk), lambda r, j: (r, 0, 0))
    stat_spec = pl.BlockSpec((1, 1, tq, PAIR), lambda r, j: (r, j, 0, 0))
    work = rows * tq * tk * width
    return (rows, width // PAIR), q_spec, k_spec, qid_spec, kid_spec, stat_spec, work


def attend(q, k, v, qid, kid):
    grid, q_spec, k_spec, qid_spec, kid_spec, stat_spec, work = attend_specs(q, k)
    return pl.pallas_call(
        attend_kernel,
        grid=grid,
        in_specs=[q_spec, k_spec, k_spec, qid_spec, kid_spec],
        out_specs=[q_spec, stat_spec],
        out_shape=[
            jax.ShapeDtypeStruct(q.shape, BF),
            jax.ShapeDtypeStruct((*grid, q.shape[1], PAIR), F32),
        ],
        cost_estimate=pl.CostEstimate(flops=16 * work, bytes_accessed=4 * k.size * 2, transcendentals=work // HEAD_DIM),
        compiler_params=pltpu.CompilerParams(vmem_limit_bytes=40 * 2**20),
    )(q, k, v, qid, kid)


def attend_back(q, k, v, g, qid, kid, stats=None):
    grid, q_spec, k_spec, qid_spec, kid_spec, stat_spec, work = attend_specs(q, k)
    saved = stats is not None
    low = lambda v: jax.ShapeDtypeStruct(v.shape, BF)
    return pl.pallas_call(
        functools.partial(attend_back_kernel, saved),
        grid=grid,
        in_specs=[q_spec, k_spec, k_spec, q_spec, qid_spec, kid_spec] + ([stat_spec] if saved else []),
        out_specs=([] if saved else [q_spec]) + [q_spec, k_spec, k_spec],
        out_shape=([] if saved else [low(q)]) + [low(q), low(k), low(v)],
        cost_estimate=pl.CostEstimate(flops=48 * work, bytes_accessed=6 * k.size * 2, transcendentals=work // HEAD_DIM),
        compiler_params=pltpu.CompilerParams(vmem_limit_bytes=40 * 2**20),
    )(q, k, v, g, qid, kid, *([stats] if saved else []))


def tie(x, *deps):
    return lax.optimization_barrier((x, *deps))


def turn_batch(x):
    size = lax.axis_size("batch")
    return lax.ppermute(x, "batch", [(i, size - 1 - i) for i in range(size)])


def turn_low(x):
    return swap(x, 1)


def turn_high(x):
    return swap(x, 2)


def halve(x, turn, bit):
    halves = x.reshape(2, x.shape[0] // 2, x.shape[1])
    send = lax.dynamic_index_in_dim(halves, 1 - bit, 0, keepdims=False).astype(BF)
    keep = lax.dynamic_index_in_dim(halves, bit, 0, keepdims=False)
    return keep.astype(F32) + turn(send).astype(F32)


def join(x, turn, bit):
    x = x.astype(BF)
    other = turn(x)
    return jnp.concatenate([jnp.where(bit == 0, x, other), jnp.where(bit == 0, other, x)], axis=0)


def reduce_ff(d_in, d_mlp):
    place = lax.axis_index("head")
    x_bit, y_bit = lax.axis_index("batch"), place >> 1
    core = (place & 1) == 1
    d_in, d_mlp = d_in.astype(BF), d_mlp.astype(BF)
    mine = jnp.where(core, d_mlp, d_in).astype(F32) + turn_low(jnp.where(core, d_in, d_mlp)).astype(F32)
    cut = mine.shape[0] // 2
    a, b = mine[:cut], mine[cut:]
    a, b = halve(a, turn_batch, x_bit), halve(b, turn_high, y_bit)
    a, b = halve(a, turn_high, y_bit), halve(b, turn_batch, x_bit)
    a, b = join(a, turn_high, y_bit), join(b, turn_batch, x_bit)
    a, b = join(a, turn_batch, x_bit), join(b, turn_high, y_bit)
    full = jnp.concatenate([a, b], axis=0)
    other = turn_low(full)
    return jnp.where(core, other, full).astype(F32), jnp.where(core, full, other).astype(F32)


def reduce_attn(own, partner):
    batch = lax.axis_index("batch")
    wide = lax.axis_index("wide")
    size = lax.axis_size("wide")
    own = own + turn_high(partner.astype(BF)).astype(F32)
    rows, width = own.shape
    mine = halve(own, turn_batch, batch)
    blocks = mine.reshape(size, -1, width)
    if size <= DIRECT:
        pick = lambda s: lax.dynamic_index_in_dim(blocks, (wide - s) % size, 0, keepdims=False)
        arrived = [shift(pick(s).astype(BF), -s) for s in range(1, size)]
        total = pick(0)
        for piece in arrived:
            total = total + piece.astype(F32)
        total = total.astype(BF)
        full = jnp.zeros(blocks.shape, BF)
        for s in range(size):
            piece = shift(total, s) if s else total
            full = lax.dynamic_update_index_in_dim(full, piece, (wide - s) % size, 0)
    else:
        total = lax.psum_scatter(blocks.astype(BF), "wide", scatter_dimension=0, tiled=False)
        full = lax.all_gather(total, "wide", axis=0, tiled=False)
    return join(full.reshape(rows // 2, width), turn_batch, batch).astype(F32)


def sum_all(x):
    x = x + turn_low(x)
    x = x + turn_high(x)
    x = x + turn_batch(x)
    size = lax.axis_size("wide")
    if size > DIRECT:
        return lax.psum(x, "wide")
    total = x
    for s in range(1, size):
        total = total + shift(x, s)
    return total


def general(tokens, patches, w_qkv, w_att, w_in, w_mlp, gains, cotangent):
    rows_all, slots, width = tokens.shape
    wide = lax.axis_size("wide")
    place = lax.axis_index("head")
    wide_place = lax.axis_index("wide")
    levels = w_qkv.shape[0]
    group = w_att.shape[1]
    n = rows_all * slots // 4
    rows = rows_all // 2

    def assemble(own, other, count):
        if rows == 1:
            return jnp.concatenate([own, other], axis=0)[None]
        half = rows // 2
        def turn(v):
            v = v.reshape(count, half, slots, *v.shape[1:])
            return jnp.moveaxis(v, 1, 0).reshape(half, count * slots, *v.shape[3:])
        return jnp.concatenate([turn(own), turn(other)], axis=0)

    def take_apart(v, count):
        if rows == 1:
            return v[0, : count * n], v[0, count * n :]
        half = rows // 2
        def turn(u):
            u = u.reshape(half, count, slots, *u.shape[2:])
            return jnp.moveaxis(u, 1, 0).reshape(count * n, *u.shape[3:])
        return turn(v[:half]), turn(v[half:])

    ends = jnp.cumsum(patches, axis=1)
    slot_index = jnp.arange(slots * wide, dtype=jnp.int32)
    image = jnp.sum((slot_index[None, :, None] >= ends[:, None, :]).astype(jnp.int32), axis=2)
    image = jnp.where(slot_index[None, :] < ends[:, -1:], image, -1)
    image = image.reshape(rows_all, wide, slots).transpose(1, 0, 2).reshape(wide, 4, n)
    order = (wide_place - jnp.arange(wide)) % wide
    image = image[order]
    own_image = lax.dynamic_index_in_dim(image, place, 1, keepdims=False)
    other_image = lax.dynamic_index_in_dim(image, place ^ 1, 1, keepdims=False)
    key_image = assemble(own_image.reshape(-1), other_image.reshape(-1), wide)
    query_image = assemble(own_image[0], other_image[0], 1)
    key_id = key_image[:, None, :]
    query_id = jnp.where(query_image >= 0, query_image, -2)[:, :, None]

    own = lax.dynamic_index_in_dim(tokens.reshape(4, n, width), place, 0, keepdims=False)
    cot = lax.dynamic_index_in_dim(cotangent.reshape(4, n, width), place, 0, keepdims=False)
    cot_other = lax.dynamic_index_in_dim(cotangent.reshape(4, n, width), place ^ 1, 0, keepdims=False)

    project = lambda act, w: jnp.einsum("rse,ce->rsc", act, w, preferred_element_type=F32).astype(BF)
    pull_back = lambda d, w: jnp.einsum("rkc,ce->rke", d, w, preferred_element_type=F32)
    weigh = lambda d, act: jnp.einsum("rqc,rqe->ce", d, act, preferred_element_type=F32)

    qkv_ws = [swap(w_qkv[l], 2) for l in range(levels)]
    att_ws = [swap(w_att[l], 2) for l in range(levels)]

    def weights(l, qkv_part, att_part):
        return jnp.concatenate([w_qkv[l], qkv_part], axis=1), jnp.concatenate([w_att[l], att_part], axis=0)

    def branch_of(attended, att_w):
        att_own, att_other = take_apart(
            jnp.einsum("rqc,ce->rqe", attended, att_w, preferred_element_type=F32), 1
        )
        return att_own + turn_low(att_other.astype(BF)).astype(F32)

    def act_terms(dq, dk, dv, qkv_w):
        d_act_kv = pull_back(dk, qkv_w[1]) + pull_back(dv, qkv_w[2])
        kv_own, kv_other = take_apart(d_act_kv, wide)
        q_own, q_other = take_apart(pull_back(dq, qkv_w[0]), 1)
        kv_other = kv_other.at[:n].add(q_other).astype(BF)
        return kv_own.at[:n].add(q_own) + turn_low(kv_other).astype(F32)

    def ff_back(pre, ff_grad, l):
        d_hidden = right_dot(ff_grad, w_mlp[l])
        unused, pull = jax.vjp(jax.nn.gelu, pre)
        return pull(d_hidden)[0].astype(BF)

    stream = own.astype(F32)
    saved = []
    for l in range(levels - 1):
        xhat, rstd = norm_parts(stream)
        act = (xhat * gains[l]).astype(BF)
        ff_act = gather_wide(act)
        other_act = turn_low(ff_act)
        pre = right_dot(ff_act, w_in[l])
        hidden = jax.nn.gelu(pre).astype(BF)
        parts = plain_dot(hidden, w_mlp[l])
        parts, ff_act, other_act = tie(parts, ff_act, other_act)
        branch = scatter_wide(parts)
        qkv_w, att_w = weights(l, qkv_ws[l], att_ws[l])
        key_act = assemble(ff_act, other_act, wide)
        query_act = assemble(act, other_act[:n], 1)
        q, k, v = project(query_act, qkv_w[0]), project(key_act, qkv_w[1]), project(key_act, qkv_w[2])
        attended, stats = attend(q, k, v, query_id, key_id)
        branch = branch + branch_of(attended, att_w)
        branch, qkv_ws[l + 1], att_ws[l + 1] = tie(branch, qkv_ws[l + 1], att_ws[l + 1])
        saved.append((xhat, rstd, ff_act, key_act, query_act, qkv_w, att_w, pre, hidden, q, k, v, attended, stats))
        stream = stream + branch

    l = levels - 1
    xhat, rstd = norm_parts(stream)
    act = (xhat * gains[l]).astype(BF)
    qkv_w, att_w = weights(l, qkv_ws[l], att_ws[l])
    query_grad = assemble(cot, cot_other, 1)
    d_attended = project(query_grad, att_w)
    ff_act = gather_wide(act)
    ff_act, cot, d_attended = tie(ff_act, cot, d_attended)
    ff_grad = gather_wide(cot)
    other_act = turn_low(ff_act)
    pre = right_dot(ff_act, w_in[l])
    hidden = jax.nn.gelu(pre).astype(BF)
    key_act = assemble(ff_act, other_act, wide)
    query_act = assemble(act, other_act[:n], 1)
    q, k, v = project(query_act, qkv_w[0]), project(key_act, qkv_w[1]), project(key_act, qkv_w[2])
    attended, dq, dk, dv = attend_back(q, k, v, d_attended, query_id, key_id)
    terms = act_terms(dq, dk, dv, qkv_w)
    d_pre = ff_back(pre, ff_grad, l)
    parts = terms + plain_dot(d_pre, w_in[l])
    parts, hidden, d_pre, dq, dk, dv, attended = tie(parts, hidden, d_pre, dq, dk, dv, attended)
    d_act = scatter_wide(parts)
    pieces = [weigh(dq, query_act), weigh(dk, key_act), weigh(dv, key_act), weigh(attended, query_grad)]
    last_attn = jnp.concatenate([t[:group] for t in pieces]) + turn_high(
        jnp.concatenate([t[group:] for t in pieces]).astype(BF)
    ).astype(F32)
    last_ff = jnp.concatenate([trans_dot(d_pre, ff_act), trans_dot(hidden, ff_grad)]).astype(BF)
    last_branch = branch_of(attended, att_w)
    last_parts = plain_dot(hidden, w_mlp[l])
    d_act, last_parts, last_attn, last_ff = tie(d_act, last_parts, last_attn, last_ff)
    gain_last = jnp.sum(d_act * xhat, axis=0)
    grad = cot.astype(F32) + norm_back(d_act, xhat, rstd, gains[l])
    last_attn = lax.psum(last_attn.astype(BF), ("batch", "wide"))
    last_ff = lax.psum(last_ff, ("batch", "head"))

    assert levels == 2
    l = 0
    xhat, rstd, ff_act, key_act, query_act, qkv_w, att_w, pre, hidden, q, k, v, attended, stats = saved[0]
    low = grad.astype(BF)
    other_low = turn_low(low)
    ff_grad = gather_wide(low)
    query_grad = assemble(low, other_low, 1)
    d_attended = project(query_grad, att_w)
    dq, dk, dv = attend_back(q, k, v, d_attended, query_id, key_id, stats)
    terms = act_terms(dq, dk, dv, qkv_w)
    piece_o, piece_v = weigh(attended, query_grad), weigh(dv, key_act)
    piece_q, piece_k = weigh(dq, query_act), weigh(dk, key_act)
    first_ov = reduce_attn(
        jnp.concatenate([piece_o[:group], piece_v[:group]]), jnp.concatenate([piece_o[group:], piece_v[group:]])
    )
    first_qk = reduce_attn(
        jnp.concatenate([piece_q[:group], piece_k[:group]]), jnp.concatenate([piece_q[group:], piece_k[group:]])
    )
    d_pre = ff_back(pre, ff_grad, l)
    parts = terms + plain_dot(d_pre, w_in[l])
    parts, hidden, d_pre = tie(parts, hidden, d_pre)
    d_act = scatter_wide(parts)
    first_in, first_mlp = reduce_ff(trans_dot(d_pre, ff_act), trans_dot(hidden, ff_grad))
    d_act, last_parts = tie(d_act, last_parts)
    gain_first = jnp.sum(d_act * xhat, axis=0)
    grad = grad + norm_back(d_act, xhat, rstd, gains[l])
    delta = gather_head((grad - cot.astype(F32)).astype(BF))
    d_tokens = cotangent.astype(F32) + delta.reshape(tokens.shape).astype(F32)
    d_gains = sum_all(jnp.stack([gain_first, gain_last]))
    stream = stream + last_branch + scatter_wide(last_parts)
    delta = gather_head((stream - own.astype(F32)).astype(BF))
    out = tokens.astype(F32) + delta.reshape(tokens.shape).astype(F32)
    last_attn = last_attn.astype(F32).reshape(4, group, width)
    last_in, last_mlp = last_ff[: last_ff.shape[0] // 2].astype(F32), last_ff[last_ff.shape[0] // 2 :].astype(F32)
    d_qkv = jnp.stack([jnp.stack([first_qk[:group], first_qk[group:], first_ov[group:]]), last_attn[:3]])
    return (
        out,
        d_tokens,
        d_qkv,
        jnp.stack([first_ov[:group], last_attn[3]]),
        jnp.stack([first_in, last_in]),
        jnp.stack([first_mlp, last_mlp]),
        d_gains,
    )


COST = 2 * 10**10
BACK_COST = COST
FF_COST = 10**8
NORM_COST = COST
LIMIT = 28
SMALL = 16
MIDDLE = 24
CORE, X_BIT, Y_BIT, WIDE, PLACE = range(5)


def full_spec(x):
    return pl.BlockSpec(x.shape, lambda i, *_, nd=x.ndim: (0,) * nd)


def layer_spec(x, l):
    return pl.BlockSpec((1, *x.shape[1:]), lambda i, *_, nd=x.ndim: (l,) + (0,) * (nd - 1))


def call(kernel, grid, ins, outs, scratch=(), prefetch=(), limit=SMALL, cost=COST, earlier=()):
    first = len(prefetch) + len(ins)
    ins = [*ins, *[(x, pl.BlockSpec(memory_space=pl.ANY)) for x in earlier]]
    return pl.pallas_call(
        kernel,
        grid_spec=pltpu.PrefetchScalarGridSpec(
            num_scalar_prefetch=len(prefetch),
            grid=(grid,),
            in_specs=[spec for _, spec in ins],
            out_specs=[spec for _, _, spec in outs],
            scratch_shapes=list(scratch),
        ),
        out_shape=[jax.ShapeDtypeStruct(shape, kind) for shape, kind, _ in outs],
        input_output_aliases={first + i: i for i in range(len(earlier))},
        cost_estimate=pl.CostEstimate(flops=cost, bytes_accessed=0, transcendentals=0),
        compiler_params=pltpu.CompilerParams(vmem_limit_bytes=limit * 2**20),
    )(*prefetch, *[x for x, _ in ins])


def far(x):
    return pltpu.with_memory_space_constraint(x, pltpu.HBM)


def whole_out(shape, kind):
    return (shape, kind, pl.BlockSpec(shape, lambda i, *_, nd=len(shape): (0,) * nd))


def total_of(refs):
    total = refs[0][...].astype(F32)
    for ref in refs[1:]:
        total = total + ref[...].astype(F32)
    return total


def start_norm_kernel(place_ref, tok_ref, gain_ref, act_ref):
    xhat, unused = norm_parts(tok_ref[...].astype(F32))
    act_ref[...] = (xhat * gain_ref[0]).astype(BF)


def start_norm(place, tokens, gains):
    n, width = tokens.shape
    return call(
        start_norm_kernel,
        1,
        [(tokens, full_spec(tokens)), (gains, layer_spec(gains, 0))],
        [whole_out((n, width), BF)],
        prefetch=(place,),
    )[0]


def norm_kernel(place_ref, tok_ref, gain_ref, *refs):
    stream_ref, act_ref = refs[-2:]
    stream = tok_ref[...].astype(F32) + total_of(refs[:-2])
    xhat, unused = norm_parts(stream)
    stream_ref[...] = stream
    act_ref[...] = (xhat * gain_ref[0]).astype(BF)


def norm(place, tokens, gains, l, terms):
    n, width = tokens.shape
    return call(
        norm_kernel,
        1,
        [(tokens, full_spec(tokens)), (gains, layer_spec(gains, l))]
        + [(t, full_spec(t)) for t in terms],
        [whole_out((n, width), F32), whole_out((n, width), BF)],
        prefetch=(place,),
        cost=FF_COST,
    )


def norm_back_kernel(first, place_ref, cot_ref, gain_ref, stream_ref, *refs):
    *refs, delta_ref, low_ref, gain_out = refs
    if not first:
        earlier, *refs = refs
    d_act = total_of(refs)
    xhat, rstd = norm_parts(stream_ref[...].astype(F32))
    gain_out[...] = jnp.sum(d_act * xhat, axis=0, keepdims=True)
    delta = norm_back(d_act, xhat, rstd, gain_ref[0])
    if not first:
        delta = delta + earlier[...]
        low_ref[...] = delta.astype(BF)
    else:
        low_ref[...] = (cot_ref[...].astype(F32) + delta).astype(BF)
    delta_ref[...] = delta


def norm_back_call(place, cotangent, gains, l, stream, terms, earlier=None):
    n, width = cotangent.shape
    first = earlier is None
    return call(
        functools.partial(norm_back_kernel, first),
        1,
        [(cotangent, full_spec(cotangent)), (gains, layer_spec(gains, l)), (stream, full_spec(stream))]
        + ([] if first else [(earlier, full_spec(earlier))])
        + [(t, full_spec(t)) for t in terms],
        [whole_out((n, width), F32), whole_out((n, width), BF), whole_out((1, width), F32)],
        prefetch=(place,),
        cost=NORM_COST,
    )


GELU_A = 0.7978845608028654
GELU_B = 0.044715


def gelu_both(x):
    square = x * x
    t = jnp.tanh(GELU_A * (x + GELU_B * (square * x)))
    value = 0.5 * x * (1.0 + t)
    slope = 0.5 * (1.0 + t) + 0.5 * x * (1.0 - t * t) * (GELU_A * (1.0 + 3.0 * GELU_B * square))
    return value, slope


def chunks_of(total):
    step = 256 if total % 256 == 0 else total
    return [slice(i, i + step) for i in range(0, total, step)]


def write_parts(total, n, part_refs):
    for s, ref in enumerate(part_refs):
        ref[...] = total[s * n : (s + 1) * n].astype(ref.dtype)


def ff_kernel(count, spot_ref, *refs):
    x_refs, (in_ref, mlp_ref, slope_ref, hidden_ref, all_ref), part_refs = refs[:count], refs[count : count + 5], refs[count + 5 :]
    n = x_refs[0].shape[0]
    x = jnp.concatenate([r[...] for r in x_refs], axis=0)
    all_ref[...] = x
    total = None
    for cut in chunks_of(in_ref.shape[1]):
        value, slope = gelu_both(right_dot(x, in_ref[0, cut, :]))
        low = value.astype(BF)
        slope_ref[:, cut] = slope
        hidden_ref[:, cut] = low
        term = plain_dot(low, mlp_ref[0, cut, :])
        total = term if total is None else total + term
    if len(part_refs) == 1:
        for s in range(count):
            part_refs[0][lax.rem(spot_ref[WIDE] - s + count, count)] = total[s * n : (s + 1) * n].astype(BF)
    else:
        write_parts(total, n, part_refs)


def part_outs(count, n, width):
    return [whole_out((n, width), F32 if s == 0 else BF) for s in range(count)]


def ff(spot, xs, w_in, w_mlp, l, blocks=False):
    count, (n, width) = len(xs), xs[0].shape
    w_in, w_mlp = w_in[l], w_mlp[l]
    hidden = w_in.shape[1]
    slope, low, x_all, *parts = call(
        functools.partial(ff_kernel, count),
        1,
        [(x, full_spec(x)) for x in (*xs, w_in, w_mlp)],
        [whole_out((count * n, hidden), F32), whole_out((count * n, hidden), BF), whole_out((count * n, width), BF)]
        + ([whole_out((count, n, width), BF)] if blocks else part_outs(count, n, width)),
        prefetch=(spot,),
        cost=FF_COST,
    )
    return slope, low, x_all, parts[0] if blocks else parts


def ff_slope_kernel(count, *refs):
    g_refs, (mlp_ref, slope_ref, d_pre_ref, all_ref) = refs[:count], refs[count:]
    g = jnp.concatenate([r[...] for r in g_refs], axis=0)
    all_ref[...] = g
    for cut in chunks_of(mlp_ref.shape[1]):
        d_pre_ref[:, cut] = (slope_ref[:, cut] * right_dot(g, mlp_ref[0, cut, :])).astype(BF)


def ff_slope(gs, w_mlp, l, slope):
    count, (n, width) = len(gs), gs[0].shape
    return call(
        functools.partial(ff_slope_kernel, count),
        1,
        [(g, full_spec(g)) for g in (*gs, w_mlp[l], slope)],
        [whole_out(slope.shape, BF), whole_out((count * n, width), BF)],
    )


def ff_back_kernel(n, d_pre_ref, in_ref, own_ref, got_ref, *part_refs):
    total = own_ref[...] + got_ref[...].astype(F32) + plain_dot(d_pre_ref[...], in_ref[0])
    write_parts(total, n, part_refs)


def ff_back(count, d_pre, w_in, l, own, got):
    n, width = d_pre.shape[0] // count, w_in[l].shape[2]
    return call(
        functools.partial(ff_back_kernel, n),
        1,
        [(x, full_spec(x)) for x in (d_pre, w_in[l], own, got)],
        part_outs(count, n, width),
    )


def ff_weights_kernel(outer, spot_ref, x_ref, g_ref, d_pre_ref, hidden_ref, keep_ref, send_ref):
    core = spot_ref[CORE] == 1
    d_in = trans_dot(d_pre_ref[...], x_ref[...])
    d_mlp = trans_dot(hidden_ref[...], g_ref[...])
    half = d_in.shape[0] // 2
    keep, send = jnp.where(core, d_mlp, d_in), jnp.where(core, d_in, d_mlp).astype(BF)
    for j in range(2):
        at = j ^ spot_ref[Y_BIT if outer == X_BIT else X_BIT]
        keep_ref[0, at] = keep[j * half : (j + 1) * half]
        send_ref[0, at] = send[j * half : (j + 1) * half]


def ff_weights(spot, xs, gs, d_pre, hidden, outer):
    width = xs.shape[1]
    tokens, size = d_pre.shape
    cut = pl.BlockSpec((tokens, size // 2), lambda i, p: (0, i))
    shape = (2, 2, size // 4, width)
    out = pl.BlockSpec((1, *shape[1:]), lambda i, p: (i ^ p[outer], 0, 0, 0))
    return call(
        functools.partial(ff_weights_kernel, outer),
        2,
        [(far(x), full_spec(x)) for x in (xs, gs)] + [(far(d_pre), cut), (far(hidden), cut)],
        [(shape, F32, out), (shape, BF, out)],
        prefetch=(spot,),
        cost=COST // 4,
    )


def ff_finish_kernel(spot_ref, mine_ref, got_ref, *refs):
    in_ref, mlp_ref = refs[-2:]
    core = spot_ref[CORE] == 1
    mine, got = mine_ref[0].astype(F32), got_ref[0].astype(F32)
    in_ref[0] = jnp.where(core, got, mine)
    mlp_ref[0] = jnp.where(core, mine, got)


def ff_finish(spot, l, mine, got, outer, earlier=()):
    unused, rows, width = mine.shape
    inner = Y_BIT if outer == X_BIT else X_BIT
    spec = pl.BlockSpec((1, rows, width), lambda i, p: (i ^ (2 * p[outer] + p[inner]), 0, 0))
    out = ((2, 4 * rows, width), F32, pl.BlockSpec((1, rows, width), lambda i, p: (l, i, 0)))
    return call(ff_finish_kernel, 4, [(mine, spec), (got, spec)], [out, out], prefetch=(spot,), earlier=earlier)


def attn_kernel(mode, count, *refs):
    refs = list(refs)
    take = lambda k: [refs.pop(0) for _ in range(k)]
    if mode != "back":
        act_refs = take(2)
    if mode != "fwd":
        g_refs = take(2)
    w_own, a_own, p_qk, p_vo, qid_ref, kid_ref = take(6)
    if mode == "back":
        q_ref, k_ref, v_ref, stat_ref = take(4)
    step = pl.program_id(0)
    scale = HEAD_DIM ** (-0.5)
    n = qid_ref.shape[0] // 2
    half = count * n
    if mode == "fwd":
        q_out, k_out, v_out, o_out, stat_out, b_own, b_other, act_all, branch = refs
    elif mode == "both":
        q_out, k_out, v_out, o_out, t_own, t_other, b_own, b_other, act_all, branch, terms = refs
    else:
        q_out, k_out, v_out, t_own, t_other, terms = refs
    if mode != "back":

        @pl.when(step == 0)
        def _():
            act_all[:half, :] = act_refs[0][...]
            act_all[half:, :] = act_refs[1][...]

    w_kv = jnp.concatenate([w_own[0, 1], p_qk[1], w_own[0, 2], p_vo[0]], axis=0)
    w_q = jnp.concatenate([w_own[0, 0], p_qk[0]], axis=0)
    w_o = jnp.concatenate([a_own[0], p_vo[1]], axis=0)
    if mode != "back":
        kv = right_dot(act_all[...], w_kv).astype(BF)
        k, v = kv[:, :PAIR], kv[:, PAIR:]
        q_in = jnp.concatenate([act_refs[0][:n, :], act_refs[1][:n, :]], axis=0)
        q = right_dot(q_in, w_q).astype(BF)
    else:
        q, k, v = q_ref[...], k_ref[...], v_ref[...]
    if mode == "fwd":
        q_out[...], k_out[...], v_out[...] = q, k, v
    q = q * jnp.asarray(scale, BF)
    allowed = qid_ref[...] == kid_ref[...]
    if mode != "fwd":
        g = right_dot(jnp.concatenate([r[...] for r in g_refs], axis=0), w_o).astype(BF)
    lane = lax.broadcasted_iota(jnp.int32, (2 * n, PAIR), 1)
    stats = jnp.zeros((2 * n, PAIR), F32)
    outs, dqs, dks, dvs = [], [], [], []
    for j in range(2):
        cut = slice(j * HEAD_DIM, (j + 1) * HEAD_DIM)
        qj, kj, vj = q[:, cut], k[:, cut], v[:, cut]
        if mode == "back":
            top, inverse = stat_ref[0, :, 2 * j : 2 * j + 1], stat_ref[0, :, 2 * j + 1 : 2 * j + 2]
            probs = jnp.exp(jnp.where(allowed, right_dot(qj, kj), NEGATIVE) - top) * inverse
        else:
            probs, top, inverse = head_softmax(qj, kj, allowed)
            stats = jnp.where(lane == 2 * j, top, jnp.where(lane == 2 * j + 1, inverse, stats))
        low = probs.astype(BF)
        if mode != "back":
            outs.append(plain_dot(low, vj))
        if mode != "fwd":
            gj = g[:, cut]
            dp = right_dot(gj, vj)
            ds = (probs * (dp - jnp.sum(probs * dp, axis=-1, keepdims=True))).astype(BF)
            dqs.append(plain_dot(ds, kj) * scale)
            dks.append(trans_dot(ds, qj))
            dvs.append(trans_dot(low, gj))
    last = step == pl.num_programs(0) - 1
    if mode != "back":
        attended = jnp.concatenate(outs, axis=1).astype(BF)
        o_out[...] = attended
        term = plain_dot(attended, w_o)

        @pl.when(step == 0)
        def _():
            branch[...] = term

        @pl.when(step > 0)
        def _():
            branch[...] += term

        @pl.when(last)
        def _():
            b_own[...] = branch[:n, :]
            b_other[...] = branch[n:, :].astype(BF)

    if mode == "fwd":
        stat_out[0] = stats
    else:
        dq = jnp.concatenate(dqs, axis=1).astype(BF)
        dkv = jnp.concatenate(dks + dvs, axis=1).astype(BF)
        q_out[...], k_out[...], v_out[...] = dq, dkv[:, :PAIR], dkv[:, PAIR:]
        term_kv = plain_dot(dkv, w_kv)
        term_q = plain_dot(dq, w_q)

        @pl.when(step == 0)
        def _():
            terms[...] = term_kv

        @pl.when(step > 0)
        def _():
            terms[...] += term_kv

        terms[:n, :] += term_q[:n]
        terms[half : half + n, :] += term_q[n:]

        @pl.when(last)
        def _():
            t_own[...] = terms[:half, :]
            t_other[...] = terms[half:, :].astype(BF)


def attn(mode, count, l, w_qkv, w_att, part, qid, kid, acts=(), grads=(), kept=()):
    group, width = part.shape[1:]
    n = qid.shape[0] // 2
    tq, tk = 2 * n, 2 * count * n
    steps = group // HEAD_DIM
    pair_q = pl.BlockSpec((tq, PAIR), lambda i: (0, i))
    pair_k = pl.BlockSpec((tk, PAIR), lambda i: (0, i))
    stat = pl.BlockSpec((1, tq, PAIR), lambda i: (i, 0, 0))
    ins = [(x, full_spec(x)) for x in (*acts, *grads)] + [
        (far(w_qkv), pl.BlockSpec((1, 3, HEAD_DIM, width), lambda i: (l, 0, i, 0))),
        (far(w_att), pl.BlockSpec((1, HEAD_DIM, width), lambda i: (l, i, 0))),
        *[(far(part), pl.BlockSpec((2, HEAD_DIM, width), lambda i, h=h: (h, i, 0))) for h in range(2)],
        (qid, full_spec(qid)),
        (kid, full_spec(kid)),
    ]
    if mode == "back":
        q, k, v, stats = kept
        ins += [(far(q), pair_q), (far(k), pair_k), (far(v), pair_k), (far(stats), stat)]
    q_shape, k_shape = (tq, 2 * group), (tk, 2 * group)
    outs = [(q_shape, BF, pair_q), (k_shape, BF, pair_k), (k_shape, BF, pair_k)]
    scratch = []
    if mode != "back":
        outs += [(q_shape, BF, pair_q)]
        scratch += [pltpu.VMEM((tk, width), BF), pltpu.VMEM((tq, width), F32)]
    if mode == "fwd":
        outs += [((steps, tq, PAIR), F32, stat)]
    else:
        outs += [whole_out((tk // 2, width), F32), whole_out((tk // 2, width), BF)]
        scratch += [pltpu.VMEM((tk, width), F32)]
    if mode != "back":
        outs += [whole_out((n, width), F32), whole_out((n, width), BF)]
    cost = BACK_COST if mode == "back" else COST
    return call(functools.partial(attn_kernel, mode, count), steps, ins, outs, scratch, limit=LIMIT, cost=cost)


def attn_weights_kernel(spot_ref, own_act, other_act, g_own, g_other, dq_ref, dk_ref, dv_ref, o_ref, own_ref, part_ref, act_all):
    n = g_own.shape[0]
    half = act_all.shape[0] // 2
    step = pl.program_id(0)

    @pl.when(step == 0)
    def _():
        act_all[:half, :] = own_act[...]
        act_all[half:, :] = other_act[...]

    q_in = jnp.concatenate([own_act[:n, :], other_act[:n, :]], axis=0)
    g_in = jnp.concatenate([g_own[...], g_other[...]], axis=0)
    kv = trans_dot(jnp.concatenate([dk_ref[...], dv_ref[...]], axis=1), act_all[...])
    pairs = (trans_dot(dq_ref[...], q_in), kv[:PAIR], kv[PAIR:], trans_dot(o_ref[...], g_in))
    rows = own_ref.shape[2]
    for i in range(2 * rows // HEAD_DIM):

        @pl.when(step == i)
        def _():
            for t, pair in enumerate(pairs):
                back = lax.rem(spot_ref[WIDE] - t + 4, 4)
                low = i * HEAD_DIM
                while low < (i + 1) * HEAD_DIM:
                    high = min((i + 1) * HEAD_DIM, (low // rows + 1) * rows)
                    at = (low // rows) ^ spot_ref[X_BIT]
                    dest = slice(low % rows, low % rows + high - low)
                    source = slice(low - i * HEAD_DIM, high - i * HEAD_DIM)
                    own_ref[at, back, dest, :] = pair[:HEAD_DIM][source]
                    part_ref[at, back, dest, :] = pair[HEAD_DIM:][source].astype(BF)
                    low = high


def attn_weights(spot, acts, grads, dq, dk, dv, attended):
    n, width = grads[0].shape
    tq, tk, group = 2 * n, 2 * acts[0].shape[0], dq.shape[1] // 2
    pair_q = pl.BlockSpec((tq, PAIR), lambda i, p: (0, i))
    pair_k = pl.BlockSpec((tk, PAIR), lambda i, p: (0, i))
    shape = (2, 4, group // 2, width)
    return call(
        attn_weights_kernel,
        group // HEAD_DIM,
        [(x, full_spec(x)) for x in (*acts, *grads)] + [(dq, pair_q), (dk, pair_k), (dv, pair_k), (attended, pair_q)],
        [whole_out(shape, F32), whole_out(shape, BF)],
        [pltpu.VMEM((tk, width), BF)],
        (spot,),
        limit=MIDDLE,
        cost=COST // 4,
    )


def attn_finish_kernel(spot_ref, mine_ref, got_ref, *refs):
    qkv_ref, att_ref = refs[-2:]
    matrix = pl.program_id(0)
    second = spot_ref[X_BIT] == 1
    mine, got = mine_ref[0].astype(F32), got_ref[0].astype(F32)
    whole = jnp.concatenate([jnp.where(second, got, mine), jnp.where(second, mine, got)], axis=0)

    @pl.when(matrix < 3)
    def _():
        qkv_ref[0, 0] = whole

    @pl.when(matrix == 3)
    def _():
        att_ref[0] = whole


def attn_finish(spot, l, mine, got, earlier=()):
    unused, rows, width = mine.shape
    spec = pl.BlockSpec((1, rows, width), lambda i, p: (lax.rem(p[WIDE] - i + 4, 4), 0, 0))
    return call(
        attn_finish_kernel,
        4,
        [(mine, spec), (got, spec)],
        [
            ((2, 3, 2 * rows, width), F32, pl.BlockSpec((1, 1, 2 * rows, width), lambda i, p: (l, jnp.minimum(i, 2), 0, 0))),
            ((2, 2 * rows, width), F32, pl.BlockSpec((1, 2 * rows, width), lambda i, p: (l, 0, 0))),
        ],
        prefetch=(spot,),
        earlier=earlier,
    )


def gather_list(x):
    return [x] + [shift(x, s) for s in range(1, lax.axis_size("wide"))]


def return_list(parts):
    return [parts[0]] + [shift(p, -s) for s, p in enumerate(parts) if s]


def reduce_ff_rest(keep, got):
    x_bit, y_bit = lax.axis_index("batch"), lax.axis_index("head") >> 1
    core = (lax.axis_index("head") & 1) == 1
    mine = keep + got.astype(F32)
    cut = mine.shape[0] // 2
    a, b = mine[:cut], mine[cut:]
    a, b = halve(a, turn_batch, x_bit), halve(b, turn_high, y_bit)
    a, b = halve(a, turn_high, y_bit), halve(b, turn_batch, x_bit)
    a, b = join(a, turn_high, y_bit), join(b, turn_batch, x_bit)
    a, b = join(a, turn_batch, x_bit), join(b, turn_high, y_bit)
    full = jnp.concatenate([a, b], axis=0)
    other = turn_low(full)
    return jnp.where(core, other, full), jnp.where(core, full, other)


def together(*pairs):
    sent = tie(*[x for x, _ in pairs])
    return tie(*[f(x) for x, (_, f) in zip(sent, pairs)])


def half_of(x, bit):
    halves = x.reshape(2, x.shape[0] // 2, x.shape[1])
    return (
        lax.dynamic_index_in_dim(halves, bit, 0, keepdims=False),
        lax.dynamic_index_in_dim(halves, 1 - bit, 0, keepdims=False).astype(BF),
    )


def shifts(sign):
    return [functools.partial(shift, step=sign * s) for s in range(1, lax.axis_size("wide"))]


def blocks_of(x):
    wide, size = lax.axis_index("wide"), lax.axis_size("wide")
    blocks = x.reshape(size, -1, x.shape[1])
    own, *others = [lax.dynamic_index_in_dim(blocks, (wide - s) % size, 0, keepdims=False) for s in range(size)]
    return own, [o.astype(BF) for o in others]


def laid(pieces):
    wide, size = lax.axis_index("wide"), lax.axis_size("wide")
    full = jnp.zeros((size, *pieces[0].shape), pieces[0].dtype)
    for s, piece in enumerate(pieces):
        full = lax.dynamic_update_index_in_dim(full, piece, (wide - s) % size, 0)
    return full.reshape(-1, pieces[0].shape[1])


def ordered(mine, other, bit):
    return jnp.where(bit == 0, mine, other), jnp.where(bit == 0, other, mine)


def sum_of(first, pieces):
    total = first.astype(F32)
    for piece in pieces:
        total = total + piece.astype(F32)
    return total


def fast(tokens, patches, w_qkv, w_att, w_in, w_mlp, gains, cotangent):
    rows_all, slots, width = tokens.shape
    shape = tokens.shape
    wide = lax.axis_size("wide")
    head_place, wide_place = lax.axis_index("head"), lax.axis_index("wide")
    x_bit, y_bit, core = lax.axis_index("batch"), head_place >> 1, head_place & 1
    spot = jnp.stack([core, x_bit, y_bit, wide_place, head_place]).astype(jnp.int32)
    group = w_att.shape[1]
    n = rows_all * slots // 4
    tokens, cotangent = tokens.reshape(4, n, width), cotangent.reshape(4, n, width)
    gains = gains[:, None, :]
    w_in, w_mlp = [w_in[l : l + 1] for l in range(2)], [w_mlp[l : l + 1] for l in range(2)]

    own_ws = [jnp.concatenate([w_qkv[l], w_att[l][None]]) for l in range(2)]
    tok = lax.dynamic_index_in_dim(tokens, head_place, 0, keepdims=False)
    act = start_norm(spot, tok, gains)
    xs = gather_list(act)
    part0 = turn_high(own_ws[0])

    ends = jnp.cumsum(patches, axis=1)
    slot_index = jnp.arange(slots * wide, dtype=jnp.int32)
    image = jnp.sum((slot_index[None, :, None] >= ends[:, None, :]).astype(jnp.int32), axis=2)
    image = jnp.where(slot_index[None, :] < ends[:, -1:], image, -1)
    image = image.reshape(rows_all, wide, slots).transpose(1, 0, 2).reshape(wide, 4, n)
    order = (wide_place - jnp.arange(wide)) % wide
    image = image[order]
    own_image = lax.dynamic_index_in_dim(image, head_place, 1, keepdims=False)
    other_image = lax.dynamic_index_in_dim(image, head_place ^ 1, 1, keepdims=False)
    kid = jnp.concatenate([own_image.reshape(-1), other_image.reshape(-1)])[None, :]
    qid = jnp.concatenate([own_image[0], other_image[0]])
    qid = jnp.where(qid >= 0, qid, -2)[:, None]
    cot = lax.dynamic_index_in_dim(cotangent, head_place, 0, keepdims=False)
    cot_other = lax.dynamic_index_in_dim(cotangent, head_place ^ 1, 0, keepdims=False)

    xs[1], kid, qid, own_ws[1], cot, cot_other = tie(xs[1], kid, qid, own_ws[1], cot, cot_other)

    slope0, hidden0, own0, parts = ff(spot, xs, w_in, w_mlp, 0)
    terms = return_list(parts)
    acts0 = (own0, turn_low(own0))
    part0, next_w = tie(part0, own_ws[1])
    part1 = turn_high(next_w)
    q, k, v, attended0, stats, b_own, b_other = attn("fwd", wide, 0, w_qkv, w_att, part0, qid, kid, acts=acts0)
    b_got = turn_low(b_other)
    stream1, act = norm(spot, tok, gains, 1, [*terms, b_own, b_got])

    xs1 = gather_list(act)
    slope1, hidden1, own1, out_parts = ff(spot, xs1, w_in, w_mlp, 1)
    other1 = turn_low(own1)
    cot_tied, unused = tie(cot, own1)
    gs1 = gather_list(cot_tied)
    dq1, dk1, dv1, attended1, t_own, t_other, b_own1, b_other1 = attn(
        "both", wide, 1, w_qkv, w_att, part1, qid, kid, acts=(own1, other1), grads=(cot, cot_other)
    )
    t_got = turn_low(t_other)
    d_pre1, g_all1 = ff_slope(gs1, w_mlp, 1, slope1)
    parts = list(ff_back(wide, d_pre1, w_in, 1, t_own, t_got))
    parts[1], dq1, hidden1, b_other1 = tie(parts[1], dq1, hidden1, b_other1)
    back1 = return_list(parts)
    own_w1, part_w1 = attn_weights(spot, (own1, other1), (cot, cot_other), dq1, dk1, dv1, attended1)
    keep_f1, send_f1 = ff_weights(spot, own1, g_all1, d_pre1, hidden1, X_BIT)
    b_got1 = turn_low(b_other1)
    back1[1], b_got1, send_f1, keep_f1, own_w1, part_w1 = tie(back1[1], b_got1, send_f1, keep_f1, own_w1, part_w1)
    got_f1 = turn_low(send_f1)
    got_w1 = turn_high(part_w1)
    delta1, low, gain1 = norm_back_call(spot, cot, gains, 1, stream1, back1)

    low_other = turn_low(low)
    gs = gather_list(low)
    dq, dk, dv, t_own, t_other = attn(
        "back", wide, 0, w_qkv, w_att, part0, qid, kid, grads=(low, low_other), kept=(q, k, v, stats)
    )
    t_got = turn_low(t_other)
    own_w0, part_w0 = attn_weights(spot, acts0, (low, low_other), dq, dk, dv, attended0)
    got_f1, part_w0, own_w0 = tie(got_f1, part_w0, own_w0)
    got_x1 = turn_batch((keep_f1[1] + got_f1[1].astype(F32)).astype(BF))
    got_w0 = turn_high(part_w0)
    gs[1], own_w0, part_w0 = tie(gs[1], own_w0, part_w0)
    d_pre0, g_all0 = ff_slope(gs, w_mlp, 0, slope0)
    parts = list(ff_back(wide, d_pre0, w_in, 0, t_own, t_got))
    parts[1], hidden0 = tie(parts[1], hidden0)
    back0 = return_list(parts)
    keep_f0, send_f0 = ff_weights(spot, own0, g_all0, d_pre0, hidden0, Y_BIT)
    got_w1, got_x1, keep_f0 = tie(got_w1, got_x1, keep_f0)
    sum_w1 = own_w1 + got_w1.astype(F32)
    got_w1 = turn_batch(sum_w1[1].astype(BF))
    back0[1], keep_f0, send_f0 = tie(back0[1], keep_f0, send_f0)
    half_w1 = sum_w1[0] + got_w1.astype(F32)
    half_f1 = sum_of(keep_f1[0], [got_f1[0], got_x1])
    delta0, low0, gain0 = norm_back_call(spot, cot, gains, 0, tok, back0, delta1)

    low0, *sent = tie(low0, *out_parts[1:])
    last = [f(p) for p, f in zip(sent, shifts(-1))]

    gain = jnp.concatenate([gain0, gain1, jnp.zeros((6, width), F32)])

    def with_gain(x, gain):
        high = gain.astype(BF)
        return jnp.concatenate([x.reshape(-1, width).astype(BF), high, (gain - high.astype(F32)).astype(BF)])

    def gain_of(got):
        return got[-16:-8].astype(F32) + got[-8:].astype(F32)

    got_f0 = turn_low(send_f0)
    got_w0, half_w1, half_f1, got_f0, *last = tie(got_w0, half_w1, half_f1, got_f0, *last)
    delta_out = (stream1 - tok.astype(F32) + sum_of(b_own1, [b_got1, out_parts[0], *last])).astype(BF)
    ends = lax.all_gather(jnp.concatenate([delta_out, low0], axis=1), "head", axis=0, tiled=False)
    sum_w0 = own_w0 + got_w0.astype(F32)
    got_w0, got_f1, *got_b1 = together(
        (sum_w0[1].astype(BF), turn_batch),
        (half_f1[1].astype(BF), turn_high),
        *[(half_w1[s + 1].astype(BF), f) for s, f in enumerate(shifts(-1))],
    )
    block_w1 = sum_of(half_w1[0], got_b1).astype(BF)
    half_w0 = sum_w0[0] + got_w0.astype(F32)
    block_f1 = (half_f1[0] + got_f1.astype(F32)).astype(BF)
    sum_f0 = keep_f0 + got_f0.astype(F32)
    rows_f = sum_f0.shape[2]
    got_f0, got_f1, *got_b0 = together(
        (with_gain(sum_f0[1], gain), turn_high),
        (block_f1, turn_batch),
        *[(half_w0[s + 1].astype(BF), f) for s, f in enumerate(shifts(-1))],
    )
    gain = gain + gain_of(got_f0)
    block_w0 = sum_of(half_w0[0], got_b0)
    half_f0 = sum_f0[0] + got_f0[: 2 * rows_f].reshape(2, rows_f, width).astype(F32)
    pair_f1 = jnp.stack([block_f1, got_f1])
    got_f0, got_f1, *got_b1 = together(
        (with_gain(half_f0[1], gain), turn_batch), (pair_f1, turn_high), *[(block_w1, f) for f in shifts(1)]
    )
    gain = gain + gain_of(got_f0)
    block_f0 = (half_f0[0] + got_f0[:rows_f].astype(F32)).astype(BF)
    full_f1 = jnp.stack([pair_f1, got_f1], axis=1).reshape(4, rows_f, width)
    mine_w1 = jnp.stack([block_w1, *got_b1])
    block_w0 = with_gain(block_w0, gain)
    got_f0, got_w1, *got_b0 = together(
        (block_f0, turn_batch), (mine_w1, turn_batch), *[(block_w0, f) for f in shifts(1)]
    )
    gain = sum_of(gain, [gain_of(g) for g in got_b0])
    pair_f0 = jnp.stack([block_f0, got_f0])
    rows_w = half_w0.shape[1]
    mine_w0 = jnp.stack([g[:rows_w] for g in (block_w0, *got_b0)])
    mine_w0, ends = tie(mine_w0, ends)
    got_w0, got_f0, got_f1 = together((mine_w0, turn_batch), (pair_f0, turn_high), (full_f1, turn_low))
    full_f0 = jnp.concatenate([pair_f0, got_f0])
    got_f0, got_g = turn_low(full_f0), turn_low(gain)
    d_gains = (gain + got_g)[:2]
    late = ff_finish(spot, 1, full_f1, got_f1, X_BIT)
    d_in, d_mlp = ff_finish(spot, 0, full_f0, got_f0, Y_BIT, late)
    out = tokens.astype(F32) + ends[:, :, :width].astype(F32)
    d_tokens = cotangent.astype(F32) + ends[:, :, width:].astype(F32)
    d_qkv, d_att = attn_finish(spot, 0, mine_w0, got_w0, attn_finish(spot, 1, mine_w1, got_w1))
    return (out.reshape(shape), d_tokens.reshape(shape), d_qkv, d_att, d_in, d_mlp, d_gains)


def solution(mesh):
    def local(*arrays):
        tokens, w_qkv = arrays[0], arrays[2]
        small = tokens.shape[0] == 2 and lax.axis_size("wide") == 4 and w_qkv.shape[0] == 2
        return (fast if small else general)(*arrays)

    return jax.shard_map(
        local,
        mesh=mesh,
        in_specs=(
            P("batch", "wide", None),
            P("batch", None),
            P(None, None, "head", None),
            P(None, "head", None),
            P(None, "wide", None),
            P(None, "wide", None),
            P(),
            P("batch", "wide", None),
        ),
        out_specs=(
            P("batch", "wide", None),
            P("batch", "wide", None),
            P(None, None, "head", None),
            P(None, "head", None),
            P(None, "wide", None),
            P(None, "wide", None),
            P(),
        ),
        check_vma=False,
    )
```

```python
import functools

import jax
import jax.numpy as jnp
from jax import lax
from jax.experimental import pallas as pl
from jax.experimental.pallas import tpu as pltpu
from jax.sharding import PartitionSpec as P

HEAD_DIM = 64
EPS = 1e-06
NEGATIVE = -1e30
BF = jnp.bfloat16
F32 = jnp.float32
DIRECT = 8


def norm_parts(stream):
    centre = jnp.mean(stream, axis=-1, keepdims=True)
    centred = stream - centre
    spread = jnp.mean(centred * centred, axis=-1, keepdims=True)
    rstd = lax.rsqrt(spread + EPS)
    return centred * rstd, rstd


def norm_back(d_act, xhat, rstd, gain_row):
    dxh = d_act * gain_row
    m1 = jnp.mean(dxh, axis=-1, keepdims=True)
    m2 = jnp.mean(dxh * xhat, axis=-1, keepdims=True)
    return (dxh - m1 - xhat * m2) * rstd


def trans_dot(left, right):
    return lax.dot_general(left, right, (((0,), (0,)), ((), ())), preferred_element_type=F32)


def right_dot(left, right):
    return lax.dot_general(left, right, (((1,), (1,)), ((), ())), preferred_element_type=F32)


def plain_dot(left, right):
    return jnp.dot(left, right, preferred_element_type=F32)


def swap(x, bit):
    size = lax.axis_size("head")
    return lax.ppermute(x, "head", [(i, i ^ bit) for i in range(size)])


def shift(x, step):
    size = lax.axis_size("wide")
    return lax.ppermute(x, "wide", [(i, (i + step) % size) for i in range(size)])


def gather_wide(x):
    size = lax.axis_size("wide")
    if size <= DIRECT:
        return jnp.concatenate([x] + [shift(x, s) for s in range(1, size)], axis=0)
    whole = lax.all_gather(x, "wide", axis=0, tiled=False)
    order = (lax.axis_index("wide") - jnp.arange(size)) % size
    return whole[order].reshape(size * x.shape[0], *x.shape[1:])


def scatter_wide(parts):
    size = lax.axis_size("wide")
    rows = parts.shape[0] // size
    if size <= DIRECT:
        total = parts[:rows]
        low = [shift(parts[s * rows : (s + 1) * rows].astype(BF), -s) for s in range(1, size)]
        for piece in low:
            total = total + piece.astype(F32)
        return total
    order = (lax.axis_index("wide") - jnp.arange(size)) % size
    blocks = parts.astype(BF).reshape(size, rows, -1)[order]
    return lax.psum_scatter(blocks, "wide", scatter_dimension=0, tiled=False).astype(F32)


def gather_head(x):
    place = lax.axis_index("head")
    a = x
    b = swap(x, 2)
    c = swap(a, 1)
    d = swap(b, 1)
    low_bit = (place & 1) == 1
    high_bit = (place & 2) == 2
    a, c = jnp.where(low_bit, c, a), jnp.where(low_bit, a, c)
    b, d = jnp.where(low_bit, d, b), jnp.where(low_bit, b, d)
    a, b = jnp.where(high_bit, b, a), jnp.where(high_bit, a, b)
    c, d = jnp.where(high_bit, d, c), jnp.where(high_bit, c, d)
    return jnp.stack([a, c, b, d])


PAIR = 2 * HEAD_DIM
FLOOR = -1e29


def head_softmax(q, k, allowed):
    s = jnp.where(allowed, right_dot(q, k), NEGATIVE)
    top = jnp.maximum(jnp.max(s, axis=-1, keepdims=True), FLOOR)
    expo = jnp.exp(s - top)
    inverse = 1.0 / jnp.maximum(jnp.sum(expo, axis=-1, keepdims=True), 1.0)
    return expo * inverse, top, inverse


def attend_kernel(q_ref, k_ref, v_ref, qid_ref, kid_ref, o_ref, stat_ref):
    allowed = qid_ref[0] == kid_ref[0]
    q = q_ref[0] * jnp.asarray(HEAD_DIM ** (-0.5), BF)
    k, v = k_ref[0], v_ref[0]
    lane = lax.broadcasted_iota(jnp.int32, (q.shape[0], PAIR), 1)
    stats = jnp.zeros((q.shape[0], PAIR), F32)
    outs = []
    for j in range(2):
        cut = slice(j * HEAD_DIM, (j + 1) * HEAD_DIM)
        probs, top, inverse = head_softmax(q[:, cut], k[:, cut], allowed)
        outs.append(plain_dot(probs.astype(BF), v[:, cut]))
        stats = jnp.where(lane == 2 * j, top, jnp.where(lane == 2 * j + 1, inverse, stats))
    o_ref[0] = jnp.concatenate(outs, axis=1).astype(BF)
    stat_ref[0, 0] = stats


def attend_back_kernel(saved, q_ref, k_ref, v_ref, g_ref, qid_ref, kid_ref, *refs):
    if saved:
        stat_ref, dq_ref, dk_ref, dv_ref = refs
    else:
        o_ref, dq_ref, dk_ref, dv_ref = refs
    allowed = qid_ref[0] == kid_ref[0]
    scale = HEAD_DIM ** (-0.5)
    q = q_ref[0] * jnp.asarray(scale, BF)
    k, v, g = k_ref[0], v_ref[0], g_ref[0]
    outs, dqs, dks, dvs = [], [], [], []
    for j in range(2):
        cut = slice(j * HEAD_DIM, (j + 1) * HEAD_DIM)
        qj, kj, vj, gj = q[:, cut], k[:, cut], v[:, cut], g[:, cut]
        if saved:
            top = stat_ref[0, 0, :, 2 * j : 2 * j + 1]
            inverse = stat_ref[0, 0, :, 2 * j + 1 : 2 * j + 2]
            probs = jnp.exp(jnp.where(allowed, right_dot(qj, kj), NEGATIVE) - top) * inverse
        else:
            probs, top, inverse = head_softmax(qj, kj, allowed)
        low = probs.astype(BF)
        if not saved:
            outs.append(plain_dot(low, vj))
        dp = right_dot(gj, vj)
        ds = (probs * (dp - jnp.sum(probs * dp, axis=-1, keepdims=True))).astype(BF)
        dqs.append(plain_dot(ds, kj) * scale)
        dks.append(trans_dot(ds, qj))
        dvs.append(trans_dot(low, gj))
    if not saved:
        o_ref[0] = jnp.concatenate(outs, axis=1).astype(BF)
    dq_ref[0] = jnp.concatenate(dqs, axis=1).astype(BF)
    dk_ref[0] = jnp.concatenate(dks, axis=1).astype(BF)
    dv_ref[0] = jnp.concatenate(dvs, axis=1).astype(BF)


def attend_specs(q, k):
    rows, tq, width = q.shape
    tk = k.shape[1]
    q_spec = pl.BlockSpec((1, tq, PAIR), lambda r, j: (r, 0, j))
    k_spec = pl.BlockSpec((1, tk, PAIR), lambda r, j: (r, 0, j))
    qid_spec = pl.BlockSpec((1, tq, 1), lambda r, j: (r, 0, 0))
    kid_spec = pl.BlockSpec((1, 1, tk), lambda r, j: (r, 0, 0))
    stat_spec = pl.BlockSpec((1, 1, tq, PAIR), lambda r, j: (r, j, 0, 0))
    work = rows * tq * tk * width
    return (rows, width // PAIR), q_spec, k_spec, qid_spec, kid_spec, stat_spec, work


def attend(q, k, v, qid, kid):
    grid, q_spec, k_spec, qid_spec, kid_spec, stat_spec, work = attend_specs(q, k)
    return pl.pallas_call(
        attend_kernel,
        grid=grid,
        in_specs=[q_spec, k_spec, k_spec, qid_spec, kid_spec],
        out_specs=[q_spec, stat_spec],
        out_shape=[
            jax.ShapeDtypeStruct(q.shape, BF),
            jax.ShapeDtypeStruct((*grid, q.shape[1], PAIR), F32),
        ],
        cost_estimate=pl.CostEstimate(flops=16 * work, bytes_accessed=4 * k.size * 2, transcendentals=work // HEAD_DIM),
        compiler_params=pltpu.CompilerParams(vmem_limit_bytes=40 * 2**20),
    )(q, k, v, qid, kid)


def attend_back(q, k, v, g, qid, kid, stats=None):
    grid, q_spec, k_spec, qid_spec, kid_spec, stat_spec, work = attend_specs(q, k)
    saved = stats is not None
    low = lambda v: jax.ShapeDtypeStruct(v.shape, BF)
    return pl.pallas_call(
        functools.partial(attend_back_kernel, saved),
        grid=grid,
        in_specs=[q_spec, k_spec, k_spec, q_spec, qid_spec, kid_spec] + ([stat_spec] if saved else []),
        out_specs=([] if saved else [q_spec]) + [q_spec, k_spec, k_spec],
        out_shape=([] if saved else [low(q)]) + [low(q), low(k), low(v)],
        cost_estimate=pl.CostEstimate(flops=48 * work, bytes_accessed=6 * k.size * 2, transcendentals=work // HEAD_DIM),
        compiler_params=pltpu.CompilerParams(vmem_limit_bytes=40 * 2**20),
    )(q, k, v, g, qid, kid, *([stats] if saved else []))


def tie(x, *deps):
    return lax.optimization_barrier((x, *deps))


def turn_batch(x):
    size = lax.axis_size("batch")
    return lax.ppermute(x, "batch", [(i, size - 1 - i) for i in range(size)])


def turn_low(x):
    return swap(x, 1)


def turn_high(x):
    return swap(x, 2)


def halve(x, turn, bit):
    halves = x.reshape(2, x.shape[0] // 2, x.shape[1])
    send = lax.dynamic_index_in_dim(halves, 1 - bit, 0, keepdims=False).astype(BF)
    keep = lax.dynamic_index_in_dim(halves, bit, 0, keepdims=False)
    return keep.astype(F32) + turn(send).astype(F32)


def join(x, turn, bit):
    x = x.astype(BF)
    other = turn(x)
    return jnp.concatenate([jnp.where(bit == 0, x, other), jnp.where(bit == 0, other, x)], axis=0)


def reduce_ff(d_in, d_mlp):
    place = lax.axis_index("head")
    x_bit, y_bit = lax.axis_index("batch"), place >> 1
    core = (place & 1) == 1
    d_in, d_mlp = d_in.astype(BF), d_mlp.astype(BF)
    mine = jnp.where(core, d_mlp, d_in).astype(F32) + turn_low(jnp.where(core, d_in, d_mlp)).astype(F32)
    cut = mine.shape[0] // 2
    a, b = mine[:cut], mine[cut:]
    a, b = halve(a, turn_batch, x_bit), halve(b, turn_high, y_bit)
    a, b = halve(a, turn_high, y_bit), halve(b, turn_batch, x_bit)
    a, b = join(a, turn_high, y_bit), join(b, turn_batch, x_bit)
    a, b = join(a, turn_batch, x_bit), join(b, turn_high, y_bit)
    full = jnp.concatenate([a, b], axis=0)
    other = turn_low(full)
    return jnp.where(core, other, full).astype(F32), jnp.where(core, full, other).astype(F32)


def reduce_attn(own, partner):
    batch = lax.axis_index("batch")
    wide = lax.axis_index("wide")
    size = lax.axis_size("wide")
    own = own + turn_high(partner.astype(BF)).astype(F32)
    rows, width = own.shape
    mine = halve(own, turn_batch, batch)
    blocks = mine.reshape(size, -1, width)
    if size <= DIRECT:
        pick = lambda s: lax.dynamic_index_in_dim(blocks, (wide - s) % size, 0, keepdims=False)
        arrived = [shift(pick(s).astype(BF), -s) for s in range(1, size)]
        total = pick(0)
        for piece in arrived:
            total = total + piece.astype(F32)
        total = total.astype(BF)
        full = jnp.zeros(blocks.shape, BF)
        for s in range(size):
            piece = shift(total, s) if s else total
            full = lax.dynamic_update_index_in_dim(full, piece, (wide - s) % size, 0)
    else:
        total = lax.psum_scatter(blocks.astype(BF), "wide", scatter_dimension=0, tiled=False)
        full = lax.all_gather(total, "wide", axis=0, tiled=False)
    return join(full.reshape(rows // 2, width), turn_batch, batch).astype(F32)


def sum_all(x):
    x = x + turn_low(x)
    x = x + turn_high(x)
    x = x + turn_batch(x)
    size = lax.axis_size("wide")
    if size > DIRECT:
        return lax.psum(x, "wide")
    total = x
    for s in range(1, size):
        total = total + shift(x, s)
    return total


def general(tokens, patches, w_qkv, w_att, w_in, w_mlp, gains, cotangent):
    rows_all, slots, width = tokens.shape
    wide = lax.axis_size("wide")
    place = lax.axis_index("head")
    wide_place = lax.axis_index("wide")
    levels = w_qkv.shape[0]
    group = w_att.shape[1]
    n = rows_all * slots // 4
    rows = rows_all // 2

    def assemble(own, other, count):
        if rows == 1:
            return jnp.concatenate([own, other], axis=0)[None]
        half = rows // 2
        def turn(v):
            v = v.reshape(count, half, slots, *v.shape[1:])
            return jnp.moveaxis(v, 1, 0).reshape(half, count * slots, *v.shape[3:])
        return jnp.concatenate([turn(own), turn(other)], axis=0)

    def take_apart(v, count):
        if rows == 1:
            return v[0, : count * n], v[0, count * n :]
        half = rows // 2
        def turn(u):
            u = u.reshape(half, count, slots, *u.shape[2:])
            return jnp.moveaxis(u, 1, 0).reshape(count * n, *u.shape[3:])
        return turn(v[:half]), turn(v[half:])

    ends = jnp.cumsum(patches, axis=1)
    slot_index = jnp.arange(slots * wide, dtype=jnp.int32)
    image = jnp.sum((slot_index[None, :, None] >= ends[:, None, :]).astype(jnp.int32), axis=2)
    image = jnp.where(slot_index[None, :] < ends[:, -1:], image, -1)
    image = image.reshape(rows_all, wide, slots).transpose(1, 0, 2).reshape(wide, 4, n)
    order = (wide_place - jnp.arange(wide)) % wide
    image = image[order]
    own_image = lax.dynamic_index_in_dim(image, place, 1, keepdims=False)
    other_image = lax.dynamic_index_in_dim(image, place ^ 1, 1, keepdims=False)
    key_image = assemble(own_image.reshape(-1), other_image.reshape(-1), wide)
    query_image = assemble(own_image[0], other_image[0], 1)
    key_id = key_image[:, None, :]
    query_id = jnp.where(query_image >= 0, query_image, -2)[:, :, None]

    own = lax.dynamic_index_in_dim(tokens.reshape(4, n, width), place, 0, keepdims=False)
    cot = lax.dynamic_index_in_dim(cotangent.reshape(4, n, width), place, 0, keepdims=False)
    cot_other = lax.dynamic_index_in_dim(cotangent.reshape(4, n, width), place ^ 1, 0, keepdims=False)

    project = lambda act, w: jnp.einsum("rse,ce->rsc", act, w, preferred_element_type=F32).astype(BF)
    pull_back = lambda d, w: jnp.einsum("rkc,ce->rke", d, w, preferred_element_type=F32)
    weigh = lambda d, act: jnp.einsum("rqc,rqe->ce", d, act, preferred_element_type=F32)

    qkv_ws = [swap(w_qkv[l], 2) for l in range(levels)]
    att_ws = [swap(w_att[l], 2) for l in range(levels)]

    def weights(l, qkv_part, att_part):
        return jnp.concatenate([w_qkv[l], qkv_part], axis=1), jnp.concatenate([w_att[l], att_part], axis=0)

    def branch_of(attended, att_w):
        att_own, att_other = take_apart(
            jnp.einsum("rqc,ce->rqe", attended, att_w, preferred_element_type=F32), 1
        )
        return att_own + turn_low(att_other.astype(BF)).astype(F32)

    def act_terms(dq, dk, dv, qkv_w):
        d_act_kv = pull_back(dk, qkv_w[1]) + pull_back(dv, qkv_w[2])
        kv_own, kv_other = take_apart(d_act_kv, wide)
        q_own, q_other = take_apart(pull_back(dq, qkv_w[0]), 1)
        kv_other = kv_other.at[:n].add(q_other).astype(BF)
        return kv_own.at[:n].add(q_own) + turn_low(kv_other).astype(F32)

    def ff_back(pre, ff_grad, l):
        d_hidden = right_dot(ff_grad, w_mlp[l])
        unused, pull = jax.vjp(jax.nn.gelu, pre)
        return pull(d_hidden)[0].astype(BF)

    stream = own.astype(F32)
    saved = []
    for l in range(levels - 1):
        xhat, rstd = norm_parts(stream)
        act = (xhat * gains[l]).astype(BF)
        ff_act = gather_wide(act)
        other_act = turn_low(ff_act)
        pre = right_dot(ff_act, w_in[l])
        hidden = jax.nn.gelu(pre).astype(BF)
        parts = plain_dot(hidden, w_mlp[l])
        parts, ff_act, other_act = tie(parts, ff_act, other_act)
        branch = scatter_wide(parts)
        qkv_w, att_w = weights(l, qkv_ws[l], att_ws[l])
        key_act = assemble(ff_act, other_act, wide)
        query_act = assemble(act, other_act[:n], 1)
        q, k, v = project(query_act, qkv_w[0]), project(key_act, qkv_w[1]), project(key_act, qkv_w[2])
        attended, stats = attend(q, k, v, query_id, key_id)
        branch = branch + branch_of(attended, att_w)
        branch, qkv_ws[l + 1], att_ws[l + 1] = tie(branch, qkv_ws[l + 1], att_ws[l + 1])
        saved.append((xhat, rstd, ff_act, key_act, query_act, qkv_w, att_w, pre, hidden, q, k, v, attended, stats))
        stream = stream + branch

    l = levels - 1
    xhat, rstd = norm_parts(stream)
    act = (xhat * gains[l]).astype(BF)
    qkv_w, att_w = weights(l, qkv_ws[l], att_ws[l])
    query_grad = assemble(cot, cot_other, 1)
    d_attended = project(query_grad, att_w)
    ff_act = gather_wide(act)
    ff_act, cot, d_attended = tie(ff_act, cot, d_attended)
    ff_grad = gather_wide(cot)
    other_act = turn_low(ff_act)
    pre = right_dot(ff_act, w_in[l])
    hidden = jax.nn.gelu(pre).astype(BF)
    key_act = assemble(ff_act, other_act, wide)
    query_act = assemble(act, other_act[:n], 1)
    q, k, v = project(query_act, qkv_w[0]), project(key_act, qkv_w[1]), project(key_act, qkv_w[2])
    attended, dq, dk, dv = attend_back(q, k, v, d_attended, query_id, key_id)
    terms = act_terms(dq, dk, dv, qkv_w)
    d_pre = ff_back(pre, ff_grad, l)
    parts = terms + plain_dot(d_pre, w_in[l])
    parts, hidden, d_pre, dq, dk, dv, attended = tie(parts, hidden, d_pre, dq, dk, dv, attended)
    d_act = scatter_wide(parts)
    pieces = [weigh(dq, query_act), weigh(dk, key_act), weigh(dv, key_act), weigh(attended, query_grad)]
    last_attn = jnp.concatenate([t[:group] for t in pieces]) + turn_high(
        jnp.concatenate([t[group:] for t in pieces]).astype(BF)
    ).astype(F32)
    last_ff = jnp.concatenate([trans_dot(d_pre, ff_act), trans_dot(hidden, ff_grad)]).astype(BF)
    last_branch = branch_of(attended, att_w)
    last_parts = plain_dot(hidden, w_mlp[l])
    d_act, last_parts, last_attn, last_ff = tie(d_act, last_parts, last_attn, last_ff)
    gain_last = jnp.sum(d_act * xhat, axis=0)
    grad = cot.astype(F32) + norm_back(d_act, xhat, rstd, gains[l])
    last_attn = lax.psum(last_attn.astype(BF), ("batch", "wide"))
    last_ff = lax.psum(last_ff, ("batch", "head"))

    assert levels == 2
    l = 0
    xhat, rstd, ff_act, key_act, query_act, qkv_w, att_w, pre, hidden, q, k, v, attended, stats = saved[0]
    low = grad.astype(BF)
    other_low = turn_low(low)
    ff_grad = gather_wide(low)
    query_grad = assemble(low, other_low, 1)
    d_attended = project(query_grad, att_w)
    dq, dk, dv = attend_back(q, k, v, d_attended, query_id, key_id, stats)
    terms = act_terms(dq, dk, dv, qkv_w)
    piece_o, piece_v = weigh(attended, query_grad), weigh(dv, key_act)
    piece_q, piece_k = weigh(dq, query_act), weigh(dk, key_act)
    first_ov = reduce_attn(
        jnp.concatenate([piece_o[:group], piece_v[:group]]), jnp.concatenate([piece_o[group:], piece_v[group:]])
    )
    first_qk = reduce_attn(
        jnp.concatenate([piece_q[:group], piece_k[:group]]), jnp.concatenate([piece_q[group:], piece_k[group:]])
    )
    d_pre = ff_back(pre, ff_grad, l)
    parts = terms + plain_dot(d_pre, w_in[l])
    parts, hidden, d_pre = tie(parts, hidden, d_pre)
    d_act = scatter_wide(parts)
    first_in, first_mlp = reduce_ff(trans_dot(d_pre, ff_act), trans_dot(hidden, ff_grad))
    d_act, last_parts = tie(d_act, last_parts)
    gain_first = jnp.sum(d_act * xhat, axis=0)
    grad = grad + norm_back(d_act, xhat, rstd, gains[l])
    delta = gather_head((grad - cot.astype(F32)).astype(BF))
    d_tokens = cotangent.astype(F32) + delta.reshape(tokens.shape).astype(F32)
    d_gains = sum_all(jnp.stack([gain_first, gain_last]))
    stream = stream + last_branch + scatter_wide(last_parts)
    delta = gather_head((stream - own.astype(F32)).astype(BF))
    out = tokens.astype(F32) + delta.reshape(tokens.shape).astype(F32)
    last_attn = last_attn.astype(F32).reshape(4, group, width)
    last_in, last_mlp = last_ff[: last_ff.shape[0] // 2].astype(F32), last_ff[last_ff.shape[0] // 2 :].astype(F32)
    d_qkv = jnp.stack([jnp.stack([first_qk[:group], first_qk[group:], first_ov[group:]]), last_attn[:3]])
    return (
        out,
        d_tokens,
        d_qkv,
        jnp.stack([first_ov[:group], last_attn[3]]),
        jnp.stack([first_in, last_in]),
        jnp.stack([first_mlp, last_mlp]),
        d_gains,
    )


COST = 2 * 10**10
BACK_COST = COST
FF_COST = 10**8
NORM_COST = COST
LIMIT = 28
SMALL = 16
MIDDLE = 24
CORE, X_BIT, Y_BIT, WIDE, PLACE = range(5)


def full_spec(x):
    return pl.BlockSpec(x.shape, lambda i, *_, nd=x.ndim: (0,) * nd)


def layer_spec(x, l):
    return pl.BlockSpec((1, *x.shape[1:]), lambda i, *_, nd=x.ndim: (l,) + (0,) * (nd - 1))


def call(kernel, grid, ins, outs, scratch=(), prefetch=(), limit=SMALL, cost=COST, earlier=()):
    first = len(prefetch) + len(ins)
    ins = [*ins, *[(x, pl.BlockSpec(memory_space=pl.ANY)) for x in earlier]]
    return pl.pallas_call(
        kernel,
        grid_spec=pltpu.PrefetchScalarGridSpec(
            num_scalar_prefetch=len(prefetch),
            grid=(grid,),
            in_specs=[spec for _, spec in ins],
            out_specs=[spec for _, _, spec in outs],
            scratch_shapes=list(scratch),
        ),
        out_shape=[jax.ShapeDtypeStruct(shape, kind) for shape, kind, _ in outs],
        input_output_aliases={first + i: i for i in range(len(earlier))},
        cost_estimate=pl.CostEstimate(flops=cost, bytes_accessed=0, transcendentals=0),
        compiler_params=pltpu.CompilerParams(vmem_limit_bytes=limit * 2**20),
    )(*prefetch, *[x for x, _ in ins])


def far(x):
    return pltpu.with_memory_space_constraint(x, pltpu.HBM)


def whole_out(shape, kind):
    return (shape, kind, pl.BlockSpec(shape, lambda i, *_, nd=len(shape): (0,) * nd))


def total_of(refs):
    total = refs[0][...].astype(F32)
    for ref in refs[1:]:
        total = total + ref[...].astype(F32)
    return total


def start_norm_kernel(place_ref, tok_ref, gain_ref, act_ref):
    xhat, unused = norm_parts(tok_ref[...].astype(F32))
    act_ref[...] = (xhat * gain_ref[0]).astype(BF)


def start_norm(place, tokens, gains):
    n, width = tokens.shape
    return call(
        start_norm_kernel,
        1,
        [(tokens, full_spec(tokens)), (gains, layer_spec(gains, 0))],
        [whole_out((n, width), BF)],
        prefetch=(place,),
    )[0]


def norm_kernel(place_ref, tok_ref, gain_ref, *refs):
    stream_ref, act_ref = refs[-2:]
    stream = tok_ref[...].astype(F32) + total_of(refs[:-2])
    xhat, unused = norm_parts(stream)
    stream_ref[...] = stream
    act_ref[...] = (xhat * gain_ref[0]).astype(BF)


def norm(place, tokens, gains, l, terms):
    n, width = tokens.shape
    return call(
        norm_kernel,
        1,
        [(tokens, full_spec(tokens)), (gains, layer_spec(gains, l))]
        + [(t, full_spec(t)) for t in terms],
        [whole_out((n, width), F32), whole_out((n, width), BF)],
        prefetch=(place,),
        cost=FF_COST,
    )


def norm_back_kernel(first, place_ref, cot_ref, gain_ref, stream_ref, *refs):
    *refs, delta_ref, low_ref, gain_out = refs
    if not first:
        earlier, *refs = refs
    d_act = total_of(refs)
    xhat, rstd = norm_parts(stream_ref[...].astype(F32))
    gain_out[...] = jnp.sum(d_act * xhat, axis=0, keepdims=True)
    delta = norm_back(d_act, xhat, rstd, gain_ref[0])
    if not first:
        delta = delta + earlier[...]
        low_ref[...] = delta.astype(BF)
    else:
        low_ref[...] = (cot_ref[...].astype(F32) + delta).astype(BF)
    delta_ref[...] = delta


def norm_back_call(place, cotangent, gains, l, stream, terms, earlier=None):
    n, width = cotangent.shape
    first = earlier is None
    return call(
        functools.partial(norm_back_kernel, first),
        1,
        [(cotangent, full_spec(cotangent)), (gains, layer_spec(gains, l)), (stream, full_spec(stream))]
        + ([] if first else [(earlier, full_spec(earlier))])
        + [(t, full_spec(t)) for t in terms],
        [whole_out((n, width), F32), whole_out((n, width), BF), whole_out((1, width), F32)],
        prefetch=(place,),
        cost=NORM_COST,
    )


GELU_A = 0.7978845608028654
GELU_B = 0.044715


def gelu_both(x):
    square = x * x
    t = jnp.tanh(GELU_A * (x + GELU_B * (square * x)))
    value = 0.5 * x * (1.0 + t)
    slope = 0.5 * (1.0 + t) + 0.5 * x * (1.0 - t * t) * (GELU_A * (1.0 + 3.0 * GELU_B * square))
    return value, slope


def chunks_of(total):
    step = 256 if total % 256 == 0 else total
    return [slice(i, i + step) for i in range(0, total, step)]


def write_parts(total, n, part_refs):
    for s, ref in enumerate(part_refs):
        ref[...] = total[s * n : (s + 1) * n].astype(ref.dtype)


def ff_kernel(count, spot_ref, *refs):
    x_refs, (in_ref, mlp_ref, slope_ref, hidden_ref, all_ref), part_refs = refs[:count], refs[count : count + 5], refs[count + 5 :]
    n = x_refs[0].shape[0]
    x = jnp.concatenate([r[...] for r in x_refs], axis=0)
    all_ref[...] = x
    total = None
    for cut in chunks_of(in_ref.shape[1]):
        value, slope = gelu_both(right_dot(x, in_ref[0, cut, :]))
        low = value.astype(BF)
        slope_ref[:, cut] = slope
        hidden_ref[:, cut] = low
        term = plain_dot(low, mlp_ref[0, cut, :])
        total = term if total is None else total + term
    if len(part_refs) == 1:
        for s in range(count):
            part_refs[0][lax.rem(spot_ref[WIDE] - s + count, count)] = total[s * n : (s + 1) * n].astype(BF)
    else:
        write_parts(total, n, part_refs)


def part_outs(count, n, width):
    return [whole_out((n, width), F32 if s == 0 else BF) for s in range(count)]


def ff(spot, xs, w_in, w_mlp, l, blocks=False):
    count, (n, width) = len(xs), xs[0].shape
    w_in, w_mlp = w_in[l], w_mlp[l]
    hidden = w_in.shape[1]
    slope, low, x_all, *parts = call(
        functools.partial(ff_kernel, count),
        1,
        [(x, full_spec(x)) for x in (*xs, w_in, w_mlp)],
        [whole_out((count * n, hidden), F32), whole_out((count * n, hidden), BF), whole_out((count * n, width), BF)]
        + ([whole_out((count, n, width), BF)] if blocks else part_outs(count, n, width)),
        prefetch=(spot,),
        cost=FF_COST,
    )
    return slope, low, x_all, parts[0] if blocks else parts


def ff_slope_kernel(count, *refs):
    g_refs, (mlp_ref, slope_ref, d_pre_ref, all_ref) = refs[:count], refs[count:]
    g = jnp.concatenate([r[...] for r in g_refs], axis=0)
    all_ref[...] = g
    for cut in chunks_of(mlp_ref.shape[1]):
        d_pre_ref[:, cut] = (slope_ref[:, cut] * right_dot(g, mlp_ref[0, cut, :])).astype(BF)


def ff_slope(gs, w_mlp, l, slope):
    count, (n, width) = len(gs), gs[0].shape
    return call(
        functools.partial(ff_slope_kernel, count),
        1,
        [(g, full_spec(g)) for g in (*gs, w_mlp[l], slope)],
        [whole_out(slope.shape, BF), whole_out((count * n, width), BF)],
    )


def ff_back_kernel(n, d_pre_ref, in_ref, own_ref, got_ref, *part_refs):
    total = own_ref[...] + got_ref[...].astype(F32) + plain_dot(d_pre_ref[...], in_ref[0])
    write_parts(total, n, part_refs)


def ff_back(count, d_pre, w_in, l, own, got):
    n, width = d_pre.shape[0] // count, w_in[l].shape[2]
    return call(
        functools.partial(ff_back_kernel, n),
        1,
        [(x, full_spec(x)) for x in (d_pre, w_in[l], own, got)],
        part_outs(count, n, width),
    )


def ff_weights_kernel(outer, spot_ref, x_ref, g_ref, d_pre_ref, hidden_ref, keep_ref, send_ref):
    core = spot_ref[CORE] == 1
    d_in = trans_dot(d_pre_ref[...], x_ref[...])
    d_mlp = trans_dot(hidden_ref[...], g_ref[...])
    half = d_in.shape[0] // 2
    keep, send = jnp.where(core, d_mlp, d_in), jnp.where(core, d_in, d_mlp).astype(BF)
    for j in range(2):
        at = j ^ spot_ref[Y_BIT if outer == X_BIT else X_BIT]
        keep_ref[0, at] = keep[j * half : (j + 1) * half]
        send_ref[0, at] = send[j * half : (j + 1) * half]


def ff_weights(spot, xs, gs, d_pre, hidden, outer):
    width = xs.shape[1]
    tokens, size = d_pre.shape
    cut = pl.BlockSpec((tokens, size // 2), lambda i, p: (0, i))
    shape = (2, 2, size // 4, width)
    out = pl.BlockSpec((1, *shape[1:]), lambda i, p: (i ^ p[outer], 0, 0, 0))
    return call(
        functools.partial(ff_weights_kernel, outer),
        2,
        [(far(x), full_spec(x)) for x in (xs, gs)] + [(far(d_pre), cut), (far(hidden), cut)],
        [(shape, F32, out), (shape, BF, out)],
        prefetch=(spot,),
        cost=COST // 4,
    )


def ff_finish_kernel(spot_ref, mine_ref, got_ref, *refs):
    in_ref, mlp_ref = refs[-2:]
    core = spot_ref[CORE] == 1
    mine, got = mine_ref[0].astype(F32), got_ref[0].astype(F32)
    in_ref[0] = jnp.where(core, got, mine)
    mlp_ref[0] = jnp.where(core, mine, got)


def ff_finish(spot, l, mine, got, outer, earlier=()):
    unused, rows, width = mine.shape
    inner = Y_BIT if outer == X_BIT else X_BIT
    spec = pl.BlockSpec((1, rows, width), lambda i, p: (i ^ (2 * p[outer] + p[inner]), 0, 0))
    out = ((2, 4 * rows, width), F32, pl.BlockSpec((1, rows, width), lambda i, p: (l, i, 0)))
    return call(
        ff_finish_kernel, 4, [(mine, spec), (got, spec)], [out, out], prefetch=(spot,), earlier=earlier, cost=COST // 100
    )


def attn_kernel(mode, count, *refs):
    refs = list(refs)
    take = lambda k: [refs.pop(0) for _ in range(k)]
    if mode != "back":
        act_refs = take(2)
    if mode != "fwd":
        g_refs = take(2)
    w_own, a_own, p_qk, p_vo, qid_ref, kid_ref = take(6)
    if mode == "back":
        q_ref, k_ref, v_ref, stat_ref = take(4)
    step = pl.program_id(0)
    scale = HEAD_DIM ** (-0.5)
    n = qid_ref.shape[0] // 2
    half = count * n
    if mode == "fwd":
        q_out, k_out, v_out, o_out, stat_out, b_own, b_other, act_all, branch = refs
    elif mode == "both":
        q_out, k_out, v_out, o_out, t_own, t_other, b_own, b_other, act_all, branch, terms = refs
    else:
        q_out, k_out, v_out, t_own, t_other, terms = refs
    if mode != "back":

        @pl.when(step == 0)
        def _():
            act_all[:half, :] = act_refs[0][...]
            act_all[half:, :] = act_refs[1][...]

    w_kv = jnp.concatenate([w_own[0, 1], p_qk[1], w_own[0, 2], p_vo[0]], axis=0)
    w_q = jnp.concatenate([w_own[0, 0], p_qk[0]], axis=0)
    w_o = jnp.concatenate([a_own[0], p_vo[1]], axis=0)
    if mode != "back":
        kv = right_dot(act_all[...], w_kv).astype(BF)
        k, v = kv[:, :PAIR], kv[:, PAIR:]
        q_in = jnp.concatenate([act_refs[0][:n, :], act_refs[1][:n, :]], axis=0)
        q = right_dot(q_in, w_q).astype(BF)
    else:
        q, k, v = q_ref[...], k_ref[...], v_ref[...]
    if mode == "fwd":
        q_out[...], k_out[...], v_out[...] = q, k, v
    q = q * jnp.asarray(scale, BF)
    allowed = qid_ref[...] == kid_ref[...]
    if mode != "fwd":
        g = right_dot(jnp.concatenate([r[...] for r in g_refs], axis=0), w_o).astype(BF)
    lane = lax.broadcasted_iota(jnp.int32, (2 * n, PAIR), 1)
    stats = jnp.zeros((2 * n, PAIR), F32)
    outs, dqs, dks, dvs = [], [], [], []
    for j in range(2):
        cut = slice(j * HEAD_DIM, (j + 1) * HEAD_DIM)
        qj, kj, vj = q[:, cut], k[:, cut], v[:, cut]
        if mode == "back":
            top, inverse = stat_ref[0, :, 2 * j : 2 * j + 1], stat_ref[0, :, 2 * j + 1 : 2 * j + 2]
            probs = jnp.exp(jnp.where(allowed, right_dot(qj, kj), NEGATIVE) - top) * inverse
        else:
            probs, top, inverse = head_softmax(qj, kj, allowed)
            stats = jnp.where(lane == 2 * j, top, jnp.where(lane == 2 * j + 1, inverse, stats))
        low = probs.astype(BF)
        if mode != "back":
            outs.append(plain_dot(low, vj))
        if mode != "fwd":
            gj = g[:, cut]
            dp = right_dot(gj, vj)
            ds = (probs * (dp - jnp.sum(probs * dp, axis=-1, keepdims=True))).astype(BF)
            dqs.append(plain_dot(ds, kj) * scale)
            dks.append(trans_dot(ds, qj))
            dvs.append(trans_dot(low, gj))
    last = step == pl.num_programs(0) - 1
    if mode != "back":
        attended = jnp.concatenate(outs, axis=1).astype(BF)
        o_out[...] = attended
        term = plain_dot(attended, w_o)

        @pl.when(step == 0)
        def _():
            branch[...] = term

        @pl.when(step > 0)
        def _():
            branch[...] += term

        @pl.when(last)
        def _():
            b_own[...] = branch[:n, :]
            b_other[...] = branch[n:, :].astype(BF)

    if mode == "fwd":
        stat_out[0] = stats
    else:
        dq = jnp.concatenate(dqs, axis=1).astype(BF)
        dkv = jnp.concatenate(dks + dvs, axis=1).astype(BF)
        q_out[...], k_out[...], v_out[...] = dq, dkv[:, :PAIR], dkv[:, PAIR:]
        term_kv = plain_dot(dkv, w_kv)
        term_q = plain_dot(dq, w_q)

        @pl.when(step == 0)
        def _():
            terms[...] = term_kv

        @pl.when(step > 0)
        def _():
            terms[...] += term_kv

        terms[:n, :] += term_q[:n]
        terms[half : half + n, :] += term_q[n:]

        @pl.when(last)
        def _():
            t_own[...] = terms[:half, :]
            t_other[...] = terms[half:, :].astype(BF)


def attn(mode, count, l, w_qkv, w_att, part, qid, kid, acts=(), grads=(), kept=()):
    group, width = part.shape[1:]
    n = qid.shape[0] // 2
    tq, tk = 2 * n, 2 * count * n
    steps = group // HEAD_DIM
    pair_q = pl.BlockSpec((tq, PAIR), lambda i: (0, i))
    pair_k = pl.BlockSpec((tk, PAIR), lambda i: (0, i))
    stat = pl.BlockSpec((1, tq, PAIR), lambda i: (i, 0, 0))
    ins = [(x, full_spec(x)) for x in (*acts, *grads)] + [
        (far(w_qkv), pl.BlockSpec((1, 3, HEAD_DIM, width), lambda i: (l, 0, i, 0))),
        (far(w_att), pl.BlockSpec((1, HEAD_DIM, width), lambda i: (l, i, 0))),
        *[(far(part), pl.BlockSpec((2, HEAD_DIM, width), lambda i, h=h: (h, i, 0))) for h in range(2)],
        (qid, full_spec(qid)),
        (kid, full_spec(kid)),
    ]
    if mode == "back":
        q, k, v, stats = kept
        ins += [(far(q), pair_q), (far(k), pair_k), (far(v), pair_k), (far(stats), stat)]
    q_shape, k_shape = (tq, 2 * group), (tk, 2 * group)
    outs = [(q_shape, BF, pair_q), (k_shape, BF, pair_k), (k_shape, BF, pair_k)]
    scratch = []
    if mode != "back":
        outs += [(q_shape, BF, pair_q)]
        scratch += [pltpu.VMEM((tk, width), BF), pltpu.VMEM((tq, width), F32)]
    if mode == "fwd":
        outs += [((steps, tq, PAIR), F32, stat)]
    else:
        outs += [whole_out((tk // 2, width), F32), whole_out((tk // 2, width), BF)]
        scratch += [pltpu.VMEM((tk, width), F32)]
    if mode != "back":
        outs += [whole_out((n, width), F32), whole_out((n, width), BF)]
    cost = BACK_COST if mode == "back" else COST
    return call(functools.partial(attn_kernel, mode, count), steps, ins, outs, scratch, limit=LIMIT, cost=cost)


def attn_weights_kernel(spot_ref, own_act, other_act, g_own, g_other, dq_ref, dk_ref, dv_ref, o_ref, own_ref, part_ref, act_all):
    n = g_own.shape[0]
    half = act_all.shape[0] // 2
    step = pl.program_id(0)

    @pl.when(step == 0)
    def _():
        act_all[:half, :] = own_act[...]
        act_all[half:, :] = other_act[...]

    q_in = jnp.concatenate([own_act[:n, :], other_act[:n, :]], axis=0)
    g_in = jnp.concatenate([g_own[...], g_other[...]], axis=0)
    kv = trans_dot(jnp.concatenate([dk_ref[...], dv_ref[...]], axis=1), act_all[...])
    pairs = (trans_dot(dq_ref[...], q_in), kv[:PAIR], kv[PAIR:], trans_dot(o_ref[...], g_in))
    rows = own_ref.shape[2]
    for i in range(2 * rows // HEAD_DIM):

        @pl.when(step == i)
        def _():
            for t, pair in enumerate(pairs):
                back = lax.rem(spot_ref[WIDE] - t + 4, 4)
                low = i * HEAD_DIM
                while low < (i + 1) * HEAD_DIM:
                    high = min((i + 1) * HEAD_DIM, (low // rows + 1) * rows)
                    at = (low // rows) ^ spot_ref[X_BIT]
                    dest = slice(low % rows, low % rows + high - low)
                    source = slice(low - i * HEAD_DIM, high - i * HEAD_DIM)
                    own_ref[at, back, dest, :] = pair[:HEAD_DIM][source]
                    part_ref[at, back, dest, :] = pair[HEAD_DIM:][source].astype(BF)
                    low = high


def attn_weights(spot, acts, grads, dq, dk, dv, attended):
    n, width = grads[0].shape
    tq, tk, group = 2 * n, 2 * acts[0].shape[0], dq.shape[1] // 2
    pair_q = pl.BlockSpec((tq, PAIR), lambda i, p: (0, i))
    pair_k = pl.BlockSpec((tk, PAIR), lambda i, p: (0, i))
    shape = (2, 4, group // 2, width)
    return call(
        attn_weights_kernel,
        group // HEAD_DIM,
        [(x, full_spec(x)) for x in (*acts, *grads)] + [(dq, pair_q), (dk, pair_k), (dv, pair_k), (attended, pair_q)],
        [whole_out(shape, F32), whole_out(shape, BF)],
        [pltpu.VMEM((tk, width), BF)],
        (spot,),
        limit=MIDDLE,
        cost=COST // 4,
    )


def attn_finish_kernel(spot_ref, mine_ref, got_ref, *refs):
    qkv_ref, att_ref = refs[-2:]
    matrix = pl.program_id(0)
    second = spot_ref[X_BIT] == 1
    mine, got = mine_ref[0].astype(F32), got_ref[0].astype(F32)
    whole = jnp.concatenate([jnp.where(second, got, mine), jnp.where(second, mine, got)], axis=0)

    @pl.when(matrix < 3)
    def _():
        qkv_ref[0, 0] = whole

    @pl.when(matrix == 3)
    def _():
        att_ref[0] = whole


def attn_finish(spot, l, mine, got, earlier=()):
    unused, rows, width = mine.shape
    spec = pl.BlockSpec((1, rows, width), lambda i, p: (lax.rem(p[WIDE] - i + 4, 4), 0, 0))
    return call(
        attn_finish_kernel,
        4,
        [(mine, spec), (got, spec)],
        [
            ((2, 3, 2 * rows, width), F32, pl.BlockSpec((1, 1, 2 * rows, width), lambda i, p: (l, jnp.minimum(i, 2), 0, 0))),
            ((2, 2 * rows, width), F32, pl.BlockSpec((1, 2 * rows, width), lambda i, p: (l, 0, 0))),
        ],
        prefetch=(spot,),
        earlier=earlier,
        cost=COST // 100,
    )


def gather_list(x):
    return [x] + [shift(x, s) for s in range(1, lax.axis_size("wide"))]


def return_list(parts):
    return [parts[0]] + [shift(p, -s) for s, p in enumerate(parts) if s]


def reduce_ff_rest(keep, got):
    x_bit, y_bit = lax.axis_index("batch"), lax.axis_index("head") >> 1
    core = (lax.axis_index("head") & 1) == 1
    mine = keep + got.astype(F32)
    cut = mine.shape[0] // 2
    a, b = mine[:cut], mine[cut:]
    a, b = halve(a, turn_batch, x_bit), halve(b, turn_high, y_bit)
    a, b = halve(a, turn_high, y_bit), halve(b, turn_batch, x_bit)
    a, b = join(a, turn_high, y_bit), join(b, turn_batch, x_bit)
    a, b = join(a, turn_batch, x_bit), join(b, turn_high, y_bit)
    full = jnp.concatenate([a, b], axis=0)
    other = turn_low(full)
    return jnp.where(core, other, full), jnp.where(core, full, other)


def together(*pairs):
    sent = tie(*[x for x, _ in pairs])
    return tie(*[f(x) for x, (_, f) in zip(sent, pairs)])


def half_of(x, bit):
    halves = x.reshape(2, x.shape[0] // 2, x.shape[1])
    return (
        lax.dynamic_index_in_dim(halves, bit, 0, keepdims=False),
        lax.dynamic_index_in_dim(halves, 1 - bit, 0, keepdims=False).astype(BF),
    )


def shifts(sign):
    return [functools.partial(shift, step=sign * s) for s in range(1, lax.axis_size("wide"))]


def blocks_of(x):
    wide, size = lax.axis_index("wide"), lax.axis_size("wide")
    blocks = x.reshape(size, -1, x.shape[1])
    own, *others = [lax.dynamic_index_in_dim(blocks, (wide - s) % size, 0, keepdims=False) for s in range(size)]
    return own, [o.astype(BF) for o in others]


def laid(pieces):
    wide, size = lax.axis_index("wide"), lax.axis_size("wide")
    full = jnp.zeros((size, *pieces[0].shape), pieces[0].dtype)
    for s, piece in enumerate(pieces):
        full = lax.dynamic_update_index_in_dim(full, piece, (wide - s) % size, 0)
    return full.reshape(-1, pieces[0].shape[1])


def ordered(mine, other, bit):
    return jnp.where(bit == 0, mine, other), jnp.where(bit == 0, other, mine)


def sum_of(first, pieces):
    total = first.astype(F32)
    for piece in pieces:
        total = total + piece.astype(F32)
    return total


def fast(tokens, patches, w_qkv, w_att, w_in, w_mlp, gains, cotangent):
    rows_all, slots, width = tokens.shape
    shape = tokens.shape
    wide = lax.axis_size("wide")
    head_place, wide_place = lax.axis_index("head"), lax.axis_index("wide")
    x_bit, y_bit, core = lax.axis_index("batch"), head_place >> 1, head_place & 1
    spot = jnp.stack([core, x_bit, y_bit, wide_place, head_place]).astype(jnp.int32)
    group = w_att.shape[1]
    n = rows_all * slots // 4
    tokens, cotangent = tokens.reshape(4, n, width), cotangent.reshape(4, n, width)
    gains = gains[:, None, :]
    w_in, w_mlp = [w_in[l : l + 1] for l in range(2)], [w_mlp[l : l + 1] for l in range(2)]

    own_ws = [jnp.concatenate([w_qkv[l], w_att[l][None]]) for l in range(2)]
    tok = lax.dynamic_index_in_dim(tokens, head_place, 0, keepdims=False)
    act = start_norm(spot, tok, gains)
    xs = gather_list(act)
    part0 = turn_high(own_ws[0])

    ends = jnp.cumsum(patches, axis=1)
    slot_index = jnp.arange(slots * wide, dtype=jnp.int32)
    image = jnp.sum((slot_index[None, :, None] >= ends[:, None, :]).astype(jnp.int32), axis=2)
    image = jnp.where(slot_index[None, :] < ends[:, -1:], image, -1)
    image = image.reshape(rows_all, wide, slots).transpose(1, 0, 2).reshape(wide, 4, n)
    order = (wide_place - jnp.arange(wide)) % wide
    image = image[order]
    own_image = lax.dynamic_index_in_dim(image, head_place, 1, keepdims=False)
    other_image = lax.dynamic_index_in_dim(image, head_place ^ 1, 1, keepdims=False)
    kid = jnp.concatenate([own_image.reshape(-1), other_image.reshape(-1)])[None, :]
    qid = jnp.concatenate([own_image[0], other_image[0]])
    qid = jnp.where(qid >= 0, qid, -2)[:, None]
    cot = lax.dynamic_index_in_dim(cotangent, head_place, 0, keepdims=False)
    cot_other = lax.dynamic_index_in_dim(cotangent, head_place ^ 1, 0, keepdims=False)

    xs[1], kid, qid, own_ws[1], cot, cot_other = tie(xs[1], kid, qid, own_ws[1], cot, cot_other)

    slope0, hidden0, own0, parts = ff(spot, xs, w_in, w_mlp, 0)
    terms = return_list(parts)
    acts0 = (own0, turn_low(own0))
    part0, next_w = tie(part0, own_ws[1])
    part1 = turn_high(next_w)
    q, k, v, attended0, stats, b_own, b_other = attn("fwd", wide, 0, w_qkv, w_att, part0, qid, kid, acts=acts0)
    b_got = turn_low(b_other)
    stream1, act = norm(spot, tok, gains, 1, [*terms, b_own, b_got])

    xs1 = gather_list(act)
    slope1, hidden1, own1, out_parts = ff(spot, xs1, w_in, w_mlp, 1)
    other1 = turn_low(own1)
    cot_tied, unused = tie(cot, own1)
    gs1 = gather_list(cot_tied)
    dq1, dk1, dv1, attended1, t_own, t_other, b_own1, b_other1 = attn(
        "both", wide, 1, w_qkv, w_att, part1, qid, kid, acts=(own1, other1), grads=(cot, cot_other)
    )
    t_got = turn_low(t_other)
    d_pre1, g_all1 = ff_slope(gs1, w_mlp, 1, slope1)
    parts = list(ff_back(wide, d_pre1, w_in, 1, t_own, t_got))
    parts[1], dq1, hidden1, b_other1 = tie(parts[1], dq1, hidden1, b_other1)
    back1 = return_list(parts)
    own_w1, part_w1 = attn_weights(spot, (own1, other1), (cot, cot_other), dq1, dk1, dv1, attended1)
    keep_f1, send_f1 = ff_weights(spot, own1, g_all1, d_pre1, hidden1, X_BIT)
    b_got1 = turn_low(b_other1)
    back1[1], b_got1, send_f1, keep_f1, own_w1, part_w1 = tie(back1[1], b_got1, send_f1, keep_f1, own_w1, part_w1)
    got_f1 = turn_low(send_f1)
    got_w1 = turn_high(part_w1)
    delta1, low, gain1 = norm_back_call(spot, cot, gains, 1, stream1, back1)

    low_other = turn_low(low)
    gs = gather_list(low)
    dq, dk, dv, t_own, t_other = attn(
        "back", wide, 0, w_qkv, w_att, part0, qid, kid, grads=(low, low_other), kept=(q, k, v, stats)
    )
    t_got = turn_low(t_other)
    own_w0, part_w0 = attn_weights(spot, acts0, (low, low_other), dq, dk, dv, attended0)
    got_f1, part_w0, own_w0 = tie(got_f1, part_w0, own_w0)
    got_x1 = turn_batch((keep_f1[1] + got_f1[1].astype(F32)).astype(BF))
    got_w0 = turn_high(part_w0)
    gs[1], own_w0, part_w0 = tie(gs[1], own_w0, part_w0)
    d_pre0, g_all0 = ff_slope(gs, w_mlp, 0, slope0)
    parts = list(ff_back(wide, d_pre0, w_in, 0, t_own, t_got))
    parts[1], hidden0 = tie(parts[1], hidden0)
    back0 = return_list(parts)
    keep_f0, send_f0 = ff_weights(spot, own0, g_all0, d_pre0, hidden0, Y_BIT)
    got_w1, got_x1, keep_f0 = tie(got_w1, got_x1, keep_f0)
    sum_w1 = own_w1 + got_w1.astype(F32)
    got_w1 = turn_batch(sum_w1[1].astype(BF))
    back0[1], keep_f0, send_f0 = tie(back0[1], keep_f0, send_f0)
    half_w1 = sum_w1[0] + got_w1.astype(F32)
    half_f1 = sum_of(keep_f1[0], [got_f1[0], got_x1])
    delta0, low0, gain0 = norm_back_call(spot, cot, gains, 0, tok, back0, delta1)

    low0, *sent = tie(low0, *out_parts[1:])
    last = [f(p) for p, f in zip(sent, shifts(-1))]

    gain = jnp.concatenate([gain0, gain1, jnp.zeros((6, width), F32)])

    def with_gain(x, gain):
        high = gain.astype(BF)
        return jnp.concatenate([x.reshape(-1, width).astype(BF), high, (gain - high.astype(F32)).astype(BF)])

    def gain_of(got):
        return got[-16:-8].astype(F32) + got[-8:].astype(F32)

    got_f0 = turn_low(send_f0)
    got_w0, half_w1, half_f1, got_f0, *last = tie(got_w0, half_w1, half_f1, got_f0, *last)
    delta_out = (stream1 - tok.astype(F32) + sum_of(b_own1, [b_got1, out_parts[0], *last])).astype(BF)
    ends = lax.all_gather(jnp.concatenate([delta_out, low0], axis=1), "head", axis=0, tiled=False)
    sum_w0 = own_w0 + got_w0.astype(F32)
    got_w0, got_f1, *got_b1 = together(
        (sum_w0[1].astype(BF), turn_batch),
        (half_f1[1].astype(BF), turn_high),
        *[(half_w1[s + 1].astype(BF), f) for s, f in enumerate(shifts(-1))],
    )
    block_w1 = sum_of(half_w1[0], got_b1).astype(BF)
    half_w0 = sum_w0[0] + got_w0.astype(F32)
    block_f1 = (half_f1[0] + got_f1.astype(F32)).astype(BF)
    sum_f0 = keep_f0 + got_f0.astype(F32)
    rows_f = sum_f0.shape[2]
    got_f0, got_f1, *got_b0 = together(
        (with_gain(sum_f0[1], gain), turn_high),
        (block_f1, turn_batch),
        *[(half_w0[s + 1].astype(BF), f) for s, f in enumerate(shifts(-1))],
    )
    gain = gain + gain_of(got_f0)
    block_w0 = sum_of(half_w0[0], got_b0)
    half_f0 = sum_f0[0] + got_f0[: 2 * rows_f].reshape(2, rows_f, width).astype(F32)
    pair_f1 = jnp.stack([block_f1, got_f1])
    got_f0, got_f1, *got_b1 = together(
        (with_gain(half_f0[1], gain), turn_batch), (pair_f1, turn_high), *[(block_w1, f) for f in shifts(1)]
    )
    gain = gain + gain_of(got_f0)
    block_f0 = (half_f0[0] + got_f0[:rows_f].astype(F32)).astype(BF)
    full_f1 = jnp.stack([pair_f1, got_f1], axis=1).reshape(4, rows_f, width)
    mine_w1 = jnp.stack([block_w1, *got_b1])
    block_w0 = with_gain(block_w0, gain)
    got_f0, got_w1, *got_b0 = together(
        (block_f0, turn_batch), (mine_w1, turn_batch), *[(block_w0, f) for f in shifts(1)]
    )
    gain = sum_of(gain, [gain_of(g) for g in got_b0])
    pair_f0 = jnp.stack([block_f0, got_f0])
    rows_w = half_w0.shape[1]
    mine_w0 = jnp.stack([g[:rows_w] for g in (block_w0, *got_b0)])
    mine_w0, ends = tie(mine_w0, ends)
    mine_w0, pair_f0, full_f1 = tie(mine_w0, pair_f0, full_f1)
    got_w0, got_f0, got_f1 = turn_batch(mine_w0), turn_high(pair_f0), turn_low(full_f1)
    late = ff_finish(spot, 1, full_f1, got_f1, X_BIT)
    late_attn = attn_finish(spot, 1, mine_w1, got_w1)
    out = tokens.astype(F32) + ends[:, :, :width].astype(F32)
    d_tokens = cotangent.astype(F32) + ends[:, :, width:].astype(F32)
    d_gains = (gain + turn_low(gain))[:2]
    got_w0, got_f0, late, late_attn, out, d_tokens, d_gains = tie(got_w0, got_f0, late, late_attn, out, d_tokens, d_gains)
    full_f0 = jnp.concatenate([pair_f0, got_f0])
    got_f0 = turn_low(full_f0)
    d_in, d_mlp = ff_finish(spot, 0, full_f0, got_f0, Y_BIT, late)
    d_qkv, d_att = attn_finish(spot, 0, mine_w0, got_w0, late_attn)
    return (out.reshape(shape), d_tokens.reshape(shape), d_qkv, d_att, d_in, d_mlp, d_gains)


def solution(mesh):
    def local(*arrays):
        tokens, w_qkv = arrays[0], arrays[2]
        small = tokens.shape[0] == 2 and lax.axis_size("wide") == 4 and w_qkv.shape[0] == 2
        return (fast if small else general)(*arrays)

    return jax.shard_map(
        local,
        mesh=mesh,
        in_specs=(
            P("batch", "wide", None),
            P("batch", None),
            P(None, None, "head", None),
            P(None, "head", None),
            P(None, "wide", None),
            P(None, "wide", None),
            P(),
            P("batch", "wide", None),
        ),
        out_specs=(
            P("batch", "wide", None),
            P("batch", "wide", None),
            P(None, None, "head", None),
            P(None, "head", None),
            P(None, "wide", None),
            P(None, "wide", None),
            P(),
        ),
        check_vma=False,
    )
```
